128 devices in a mesh: seq: 16 (over y_hi, x, core), tp: 8 (over z, y_lo).
Axes of the slice: x: 4, y: 4 (y_hi: 2, y_lo: 2; y = y_hi * 2 + y_lo), z: 4, core: 2. Of those that a mesh axis runs over, the one named last changes fastest.
Arguments:
- teacher_queries: bfloat16 [2048, 8192], P('seq', 'tp'), may hold values from -110 to 110
- teacher_kv: bfloat16 [2, 12288, 1024], P(None, 'seq', 'tp'), may hold values from -4 to 4
- student_queries: bfloat16 [2048, 4096], P('seq', 'tp'), may hold values from -110 to 110
- student_kv: bfloat16 [2, 12288, 1024], P(None, 'seq', 'tp'), may hold values from -4 to 4
- doc_start: int32 [1], replicated, may hold values from 0 to 5119
- teacher_resid: bfloat16 [2048, 8192], P('tp', 'seq'), may hold values from -0.75 to 0.75
- teacher_out_proj: bfloat16 [8192, 8192], P('tp', 'seq'), may hold values from -0.0625 to 0.0625
- teacher_gain: float32 [8192], P('seq'), may hold values from 0.1 to 1.9
- student_resid: bfloat16 [2048, 4096], P('tp', 'seq'), may hold values from -0.75 to 0.75
- student_out_proj: bfloat16 [4096, 4096], P('tp', 'seq'), may hold values from -0.09375 to 0.09375
- student_gain: float32 [4096], P('seq'), may hold values from 0.1 to 1.9
- match_proj: bfloat16 [4096, 8192], P(None, 'seq'), may hold values from -0.09375 to 0.09375
Outputs:
- match_grad: float32 [4096, 8192], P('tp', 'seq')
The draws below stay inside these ranges and needn't reach their ends.
All inputs are finite; a program needn't handle non-finite values.
Results may differ from the reference program's by a relative error of at most 0.0055.
Values may be sent and summed in bfloat16 or wider, within the bound.
A program may use at most 192 MiB of HBM per device.

```python
import math
import jax
import jax.numpy as jnp
from jax import lax

D_T = 8192
H_T = 64
D_S = 4096
H_S = 32
KV_HEADS = 8
HEAD = 128
SLAB = 2048
KEYS = 12288
CACHE = 10240


def raw_keys(key, salt):
    return jax.random.truncated_normal(jax.random.fold_in(key, salt), -4.0, 4.0, (KEYS, KV_HEADS * HEAD), jnp.float32)


def draw_teacher_queries(key, part):
    key = jax.random.fold_in(key, 1)
    drawn = jax.random.truncated_normal(key, -4.0, 4.0, (SLAB, H_T * HEAD), jnp.float32)
    return drawn.astype(jnp.bfloat16)


def draw_teacher_kv(key, part):
    keys = raw_keys(key, 101)
    key = jax.random.fold_in(key, 2)
    values = jax.random.truncated_normal(key, -4.0, 4.0, (KEYS, KV_HEADS * HEAD), jnp.float32)
    return jnp.stack([keys, values]).astype(jnp.bfloat16)


def draw_student_queries(key, part):
    key = jax.random.fold_in(key, 3)
    drawn = jax.random.truncated_normal(key, -4.0, 4.0, (SLAB, H_S * HEAD), jnp.float32)
    return drawn.astype(jnp.bfloat16)


def draw_student_kv(key, part):
    keys = raw_keys(key, 202)
    key = jax.random.fold_in(key, 4)
    values = jax.random.truncated_normal(key, -4.0, 4.0, (KEYS, KV_HEADS * HEAD), jnp.float32)
    return jnp.stack([keys, values]).astype(jnp.bfloat16)


def steps_of(rng, extent, split, least, high):
    def one(axis_at, shards_of):
        steps = jax.random.uniform(jax.random.fold_in(jax.random.fold_in(rng, 6), axis_at), (shards_of,), jnp.float32, least / len(split), high / len(split))
        return jnp.repeat(jnp.exp(steps), extent[axis_at] // shards_of).reshape((-1,) + (1,) * (len(extent) - axis_at - 1))

    loudness = one(*split[0])
    for cut in split[1:]:
        loudness = loudness * one(*cut)
    return loudness


def noise(key, dims, width, most, split=(), held_as=jnp.bfloat16):
    drawn = width * jax.random.normal(key, dims, jnp.float32)
    if split:
        drawn = drawn * steps_of(key, dims, split, -0.22, 0.18)
    return jnp.clip(drawn, -most, most).astype(held_as)


def setup_inputs(seed: int = 0) -> dict:
    arg_keys = jax.random.split(jax.random.key(seed), 13)
    teacher_queries = draw_teacher_queries(jax.random.fold_in(arg_keys[12], 71), 0)
    teacher_kv = draw_teacher_kv(jax.random.fold_in(arg_keys[12], 71), 0)
    student_queries = draw_student_queries(jax.random.fold_in(arg_keys[12], 71), 0)
    student_kv = draw_student_kv(jax.random.fold_in(arg_keys[12], 71), 0)
    doc_start = jax.random.randint(arg_keys[4], (1,), 0, CACHE // 2).astype(jnp.int32)
    teacher_resid = noise(arg_keys[5], (SLAB, D_T), 0.05, 0.75, ((0, 8), (1, 16)))
    teacher_out_proj = noise(arg_keys[6], (H_T * HEAD, D_T), (H_T * HEAD) ** -0.5, 0.0625, ((0, 8), (1, 16)))
    teacher_gain = jnp.clip(1.0 + 0.18 * jax.random.normal(arg_keys[7], (D_T,), jnp.float32), 0.1, 1.9)
    student_resid = noise(arg_keys[8], (SLAB, D_S), 0.05, 0.75, ((0, 8), (1, 16)))
    student_out_proj = noise(arg_keys[9], (H_S * HEAD, D_S), (H_S * HEAD) ** -0.5, 0.09375, ((0, 8), (1, 16)))
    student_gain = jnp.clip(1.0 + 0.18 * jax.random.normal(arg_keys[10], (D_S,), jnp.float32), 0.1, 1.9)
    match_proj = noise(arg_keys[11], (D_S, D_T), D_S ** -0.5, 0.09375, ((1, 16),))
    return {"teacher_queries": teacher_queries, "teacher_kv": teacher_kv, "student_queries": student_queries, "student_kv": student_kv, "doc_start": doc_start, "teacher_resid": teacher_resid, "teacher_out_proj": teacher_out_proj, "teacher_gain": teacher_gain, "student_resid": student_resid, "student_out_proj": student_out_proj, "student_gain": student_gain, "match_proj": match_proj}


def attend(queries, keys_values, doc_start, heads):
    group = heads // KV_HEADS
    query_heads = queries.reshape(SLAB, heads, HEAD).transpose(1, 0, 2)
    key_heads = keys_values[0].reshape(KEYS, KV_HEADS, HEAD).transpose(1, 0, 2)
    value_heads = keys_values[1].reshape(KEYS, KV_HEADS, HEAD).transpose(1, 0, 2)
    query_index = CACHE + jnp.arange(SLAB, dtype=jnp.int32)
    key_index = jnp.arange(KEYS, dtype=jnp.int32)
    visible = (key_index[None, :] <= query_index[:, None]) & (key_index[None, :] >= doc_start[0])

    def one_head(head_index):
        kv_index = head_index // group
        scores = jnp.dot(query_heads[head_index], key_heads[kv_index].T, preferred_element_type=jnp.float32) * (1.0 / math.sqrt(HEAD))
        scores = jnp.where(visible, scores, -1e+30)
        largest = lax.optimization_barrier(jnp.max(scores, axis=1, keepdims=True))
        weights = jnp.where(visible, jnp.exp(scores - largest), 0.0)
        totals = lax.optimization_barrier(jnp.sum(weights, axis=1, keepdims=True))
        context = jnp.dot(weights.astype(jnp.bfloat16), value_heads[kv_index], preferred_element_type=jnp.float32) / totals
        return context.astype(jnp.bfloat16)
    outputs = lax.map(one_head, jnp.arange(heads, dtype=jnp.int32))
    return outputs.transpose(1, 0, 2).reshape(SLAB, heads * HEAD)

def reference(teacher_queries, teacher_kv, student_queries, student_kv, doc_start, teacher_resid, teacher_out_proj, teacher_gain, student_resid, student_out_proj, student_gain, match_proj):
    teacher_context = attend(teacher_queries, teacher_kv, doc_start, H_T)
    student_context = attend(student_queries, student_kv, doc_start, H_S)
    teacher_hidden = teacher_resid.astype(jnp.float32) + jnp.dot(teacher_context, teacher_out_proj, preferred_element_type=jnp.float32)
    student_hidden = student_resid.astype(jnp.float32) + jnp.dot(student_context, student_out_proj, preferred_element_type=jnp.float32)
    teacher_scale = jnp.sqrt(lax.optimization_barrier(jnp.sum(teacher_hidden * teacher_hidden, axis=1, keepdims=True)) / D_T + 1e-05)
    target = teacher_hidden / teacher_scale * teacher_gain
    student_scale = jnp.sqrt(lax.optimization_barrier(jnp.sum(student_hidden * student_hidden, axis=1, keepdims=True)) / D_S + 1e-05)
    normed = (student_hidden / student_scale * student_gain).astype(jnp.bfloat16)
    diff = jnp.dot(normed, match_proj, preferred_element_type=jnp.float32) - target
    delta = diff / math.sqrt(SLAB)
    return jnp.dot(normed.astype(jnp.float32).T, delta, precision=lax.Precision.HIGHEST, preferred_element_type=jnp.float32)
```

```python
import math

import jax
import jax.numpy as jnp
from jax import lax
from jax.experimental import pallas as pl
from jax.experimental.pallas import tpu as pltpu
from jax.sharding import PartitionSpec as P

D_T = 8192
D_S = 4096
HEAD = 128
SLAB = 2048
CACHE = 10240
KEYS_CHIP = 1536
HIDDEN = -1e30
LOG2E = math.log2(math.e)
SCALE = LOG2E / math.sqrt(HEAD)
MESH = pl.DeviceIdType.MESH
BF = jnp.bfloat16
F32 = jnp.float32


class Wire:
    def __init__(self, send, recv):
        self.send, self.recv, self.made = send, recv, []

    def copy(self, src, dst, dev):
        i = len(self.made)
        made = pltpu.make_async_remote_copy(
            src_ref=src, dst_ref=dst, send_sem=self.send.at[i], recv_sem=self.recv.at[i],
            device_id=dev, device_id_type=MESH,
        )
        self.made.append(made)
        return made

    def close(self):
        for made in self.made:
            made.wait_send()


class Gather:
    def __init__(self, wire, block, right, left, across=None, core=None, planes=None):
        self.planes = planes or (1 if across is None else 2)
        self.core = core is not None
        self.cross = wire.copy(block(0, 0, None), block(0, 0, None), across) if across is not None else None
        self.right, self.left, self.on_right, self.on_left, self.pass_on = [], [], [], [], []
        for plane in range(self.planes):
            own = block(plane, 0, None)
            self.right.append(wire.copy(own, own, right))
            self.left.append(wire.copy(own, own, left))
            first, second = block(plane, 3, 0), block(plane, 1, 1)
            self.on_right.append(wire.copy(first, first, right))
            self.on_left.append(wire.copy(second, second, left))
            if self.core:
                refs = [own, block(plane, 3, None), block(plane, 1, None), block(plane, 2, 0), block(plane, 2, 1)]
                self.pass_on.append([wire.copy(ref, ref, core) for ref in refs])

    def root(self, plane):
        if plane == 1 and self.cross is not None:
            self.cross.wait_recv()
        self.right[plane].start()
        self.left[plane].start()
        if plane == 0 and self.cross is not None:
            self.cross.start()
        if self.core:
            self.pass_on[plane][0].start()

    def mid(self, plane):
        self.right[plane].wait_recv()
        self.on_right[plane].start()
        if self.core:
            self.pass_on[plane][1].start()
        self.left[plane].wait_recv()
        self.on_left[plane].start()
        if self.core:
            self.pass_on[plane][2].start()

    def far(self, plane):
        self.on_right[plane].wait_recv()
        if self.core:
            self.pass_on[plane][3].start()
        self.on_left[plane].wait_recv()
        if self.core:
            self.pass_on[plane][4].start()

    def have_own(self, plane):
        self.pass_on[plane][0].wait_recv()

    def have_left(self, plane):
        self.pass_on[plane][1].wait_recv()

    def have_right(self, plane):
        self.pass_on[plane][2].wait_recv()

    def have_near(self, plane):
        self.have_left(plane)
        self.have_right(plane)

    def have_far(self, plane):
        self.pass_on[plane][3].wait_recv()
        self.pass_on[plane][4].wait_recv()


def dot(a, b, dims=((1,), (0,)), precision=None):
    return lax.dot_general(a, b, (dims, ((), ())), precision=precision, preferred_element_type=F32)


def scratch_plan():
    V = pltpu.VMEM
    D = pltpu.SemaphoreType.DMA
    return dict(
        kv=V((2, 4, 2, 2, 768, 128), BF),
        kx=V((2, 4, 2, 768, 256), BF),
        vt=V((2, 4, 2, 144, 768), BF),
        qa=V((3, 2, 512, 256), BF),
        tq_in=V((128, 1024), BF),
        sq_in=V((128, 512), BF),
        m=V((3, 2, 8, 512), F32),
        acc=V((3, 2, 144, 512), F32),
        o_out=V((3, 2, 128, 512), BF),
        o_in=V((3, 2, 128, 512), BF),
        l_out=V((3, 2, 8, 512), F32),
        l_in=V((3, 2, 8, 512), F32),
        tctx=V((8, 2, 128, 1024), BF),
        sctx=V((8, 2, 128, 512), BF),
        tw=V((1024, 512), BF),
        sw=V((512, 256), BF),
        mp=V((8, 512, 512), BF),
        ty_out=V((2, 128, 512), BF),
        ty_in=V((2, 128, 512), BF),
        sy_out=V((256, 256), BF),
        sy_in=V((256, 256), BF),
        tpart=V((2, 4, 2, 128, 512), F32),
        spart=V((4, 2, 256, 256), F32),
        tr_out=V((2, 2, 128, 512), BF),
        tr_in=V((2, 2, 2, 64, 512), BF),
        sr_out=V((2, 256, 256), BF),
        sr_in=V((2, 2, 128, 256), BF),
        tz_out=V((2, 2, 2, 128, 512), BF),
        tz_in=V((2, 2, 2, 128, 512), BF),
        sz_out=V((2, 2, 256, 256), BF),
        sz_in=V((2, 2, 256, 256), BF),
        thid=V((2, 128, 512), F32),
        shid=V((256, 256), F32),
        tsq=V((2, 16, 8, 128), F32),
        ssq=V((16, 8, 256), F32),
        nb=V((16, 256, 256), BF),
        ng=V((8, 2, 256, 256), BF),
        dl=V((2, 8, 128, 512), BF),
        diff=V((2, 128, 512), F32),
        wsend=D((200,)),
        wrecv=D((200,)),
        loc=D((8,)),
    )


def kernel(doc, tq, tkv_h, sq, skv_h, tres, tw_h, tg, sres, sw_h, sg, mp_h, out, *scratch):
    b = dict(zip(scratch_plan(), scratch))
    s = lax.axis_index("seq")
    p = lax.axis_index("tp")
    yh, x, c = s // 8, (s // 2) % 4, s % 2
    z, yl = p // 2, p % 2
    k_own = yh * 4 + x

    def seq_dev(plane, off, other):
        return ((((yh + plane) % 2) * 4 + (x + off) % 4) * 2 + (c + other) % 2, p)

    def tp_dev(plane, off):
        return (s, ((z + off) % 4) * 2 + (yl + plane) % 2)

    right, left, across, core = seq_dev(0, 1, 0), seq_dev(0, 3, 0), seq_dev(1, 0, 0), seq_dev(0, 0, 1)

    loads = [
        pltpu.make_async_copy(skv_h, b["kv"].at[0, x, c], b["loc"].at[0]),
        pltpu.make_async_copy(tkv_h, b["kv"].at[1, x, c], b["loc"].at[1]),
        pltpu.make_async_copy(sw_h, b["sw"], b["loc"].at[2]),
        pltpu.make_async_copy(tw_h, b["tw"], b["loc"].at[3]),
        pltpu.make_async_copy(mp_h, b["mp"], b["loc"].at[4]),
    ]
    for load in loads:
        load.start()

    barrier = pltpu.get_barrier_semaphore()
    for off in range(1, 16):
        pl.semaphore_signal(barrier, inc=1, device_id=((s + off) % 16, p), device_id_type=MESH)
    for off in range(1, 8):
        pl.semaphore_signal(barrier, inc=1, device_id=(s, (p + off) % 8), device_id_type=MESH)
    pl.semaphore_wait(barrier, 22)

    wire = Wire(b["wsend"], b["wrecv"])
    give_sq = wire.copy(sq, b["sq_in"], across)
    give_tq = wire.copy(tq, b["tq_in"], across)

    def kv_block(model):
        def block(plane, off, part):
            at = (x + off) % 4
            if part is None:
                return b["kv"].at[model, at, c]
            return b["kv"].at[model, at, c, part]

        return block

    def s_block(plane, off, part):
        at = ((yh + plane) % 2) * 4 + (x + off) % 4
        if part is None:
            return b["sctx"].at[at, c]
        return b["sctx"].at[at, c, pl.ds(part * 64, 64)]

    def t_block(half):
        def block(plane, off, part):
            at = ((yh + plane) % 2) * 4 + (x + off) % 4
            if part is None:
                return b["tctx"].at[at, c, pl.ds(half * 64, 64)]
            return b["tctx"].at[at, c, pl.ds(half * 64 + part * 32, 32)]

        return block

    def nb_block(plane, off, part):
        at = (((yh + plane) % 2) * 4 + (x + off) % 4) * 2 + c
        if part is None:
            return b["nb"].at[at]
        return b["nb"].at[at, pl.ds(part * 128, 128)]

    def dl_block(half):
        def block(plane, off, part):
            at = ((z + off) % 4) * 2 + (yl + plane) % 2
            if part is None:
                return b["dl"].at[half, at]
            return b["dl"].at[half, at, pl.ds(part * 64, 64)]

        return block

    g_skv = Gather(wire, kv_block(0), right, left, None, core)
    g_tkv = Gather(wire, kv_block(1), right, left, None, core)
    g_s = Gather(wire, s_block, right, left, None, core, 2)
    g_t = [Gather(wire, t_block(half), right, left, None, core, 2) for half in range(2)]
    g_n = Gather(wire, nb_block, right, left, across, core)
    g_d = [Gather(wire, dl_block(half), tp_dev(0, 1), tp_dev(0, 3), tp_dev(1, 0), None) for half in range(2)]
    give_o = [[wire.copy(b["o_out"].at[i, 1 - g], b["o_in"].at[i, g], across) for g in range(2)] for i in range(3)]
    give_l = [[wire.copy(b["l_out"].at[i, 1 - g], b["l_in"].at[i, g], across) for g in range(2)] for i in range(3)]
    s_sq = [wire.copy(b["ssq"].at[s], b["ssq"].at[s], ((s + off) % 16, p)) for off in range(1, 16)]
    t_sq = [
        [wire.copy(b["tsq"].at[half, s], b["tsq"].at[half, s], ((s + off) % 16, p)) for off in range(1, 16)]
        for half in range(2)
    ]
    n_tp = [
        wire.copy(b["nb"].at[((p + off) % 8) * 2 + c], b["ng"].at[p, c], (s, (p + off) % 8)) for off in range(1, 8)
    ]
    n_core = [
        wire.copy(b["ng"].at[(p + 8 - off) % 8, c], b["ng"].at[(p + 8 - off) % 8, c], core) for off in range(1, 8)
    ]

    qa, m, acc = b["qa"], b["m"], b["acc"]
    heads, tokens = (4, 8, 8), (128, 64, 64)

    def fill_queries(one, src, group):
        first = 64 * (one // 2)
        for h in range(heads[one]):
            rows = slice(h * tokens[one], (h + 1) * tokens[one])
            qa[one, group, rows, 0:128] = src[first : first + tokens[one], h * 128 : (h + 1) * 128]

    def prepare(model, passes):
        rows = lax.broadcasted_iota(jnp.int32, (128, 128), 0)
        lanes = lax.broadcasted_iota(jnp.int32, (128, 128), 1)
        for one in passes:
            eye = jnp.where(rows % tokens[one] + 64 * (one // 2) == lanes, 1.0, 0.0).astype(BF)
            for g in range(2):
                for i in range(4):
                    qa[one, g, i * 128 : (i + 1) * 128, 128:256] = eye
            m[one] = jnp.full((2, 8, 512), HIDDEN, F32)
            acc[one] = jnp.zeros((2, 144, 512), F32)

        def extra(i, carry):
            b["kx"][model, i, :, :, 128:256] = jnp.zeros((2, 768, 128), BF)
            b["vt"][model, i, :, 128:144, :] = jnp.ones((2, 16, 768), BF)
            return carry

        lax.fori_loop(0, 4, extra, 0)

    first_key = doc[0]

    def attention(hooks):
        def step(n, carry):
            for at_step, hook in hooks.items():
                pl.when(n == at_step)(hook)
            one, i, half, g = n // 16, (n % 16) // 4, (n % 4) // 2, n % 2
            model = (one + 1) // 2
            at = (x + 3 * i + 3 * (i // 2) + 2 * (i // 3)) % 4
            from_core = (c + half) % 2
            base = (yh * 4 + at) * KEYS_CHIP + from_core * 768

            @pl.when((g == 0) & (one <= 1))
            def _():
                b["vt"][model, at, from_core, 0:128, :] = b["kv"][model, at, from_core, 1].T
                b["kx"][model, at, from_core, :, 0:128] = b["kv"][model, at, from_core, 0]

            @pl.when((yh == 0) & (g == 0) & (one <= 1))
            def _():
                key = lax.broadcasted_iota(jnp.int32, (768, 128), 0)
                b["kx"][model, at, from_core, :, 128:256] = jnp.where(key >= first_key - base, 0.0, HIDDEN).astype(BF)

            @pl.when((yh == 1) & (at >= 2))
            def _():
                first_row = CACHE + ((((yh + g) % 2) * 4 + x) * 2 + c) * 128
                key = lax.broadcasted_iota(jnp.int32, (768, 128), 0)
                row = lax.broadcasted_iota(jnp.int32, (768, 128), 1)
                b["kx"][model, at, from_core, :, 128:256] = jnp.where(key - row <= first_row - base, 0.0, HIDDEN).astype(BF)

            scores = dot(b["kx"][model, at, from_core], qa[one, g], ((1,), (1,)))
            old = m[one, g]
            new = jnp.maximum(old, jnp.broadcast_to(jnp.max(scores, axis=0, keepdims=True), (8, 512)))
            weights = jnp.exp2((scores.reshape(96, 8, 512) - new[None]) * SCALE).reshape(768, 512).astype(BF)
            shrink = jnp.exp2((old - new) * SCALE)
            fresh = dot(b["vt"][model, at, from_core], weights)
            m[one, g] = new
            acc[one, g] = (acc[one, g].reshape(18, 8, 512) * shrink[None]).reshape(144, 512) + fresh
            return carry

        lax.fori_loop(0, 48, step, 0)

    def part_of(one, g):
        total = acc[one, g, 128:136, :]
        mean = (acc[one, g, 0:128, :].reshape(16, 8, 512) * (1.0 / total)[None]).reshape(128, 512)
        return mean, m[one, g] * SCALE + jnp.log(total) * LOG2E

    def partner_part(one):
        for g in (1, 0):
            mean, logs = part_of(one, g)
            b["o_out"][one, g] = mean.astype(BF)
            b["l_out"][one, g] = logs
            give_o[one][1 - g].start()
            give_l[one][1 - g].start()

    def combine(one, g, ctx):
        give_o[one][g].wait_recv()
        give_l[one][g].wait_recv()
        mine, log_mine = part_of(one, g)
        share = 1.0 / (1.0 + jnp.exp2(log_mine - b["l_in"][one, g]))
        other = b["o_in"][one, g].astype(F32)
        both = mine + ((other - mine).reshape(16, 8, 512) * share[None]).reshape(128, 512)
        both = both.T.astype(BF)
        count, first = tokens[one], 64 * (one // 2)
        for h in range(heads[one]):
            held = both[h * count : (h + 1) * count, :]
            ctx[((yh + g) % 2) * 4 + x, c, first : first + count, h * 128 : (h + 1) * 128] = held

    class Reduce:
        def __init__(self, ctx, w, name, half):
            self.ctx, self.w, self.half = ctx, w, half

            def of(key):
                return b[name + key] if half is None else b[name + key].at[half]

            self.y_out, self.y_in, self.part, self.hid = of("y_out"), of("y_in"), of("part"), of("hid")
            self.r_out, self.r_in, self.z_out, self.z_in = of("r_out"), of("r_in"), of("z_out"), of("z_in")
            self.rows = self.part.shape[2] // 2
            near = (tp_dev(0, 3), tp_dev(0, 1))
            self.relay = [
                wire.copy(self.r_out.at[:, pl.ds(i * self.rows, self.rows)], self.r_in.at[i], near[i]) for i in range(2)
            ]
            self.along = [wire.copy(self.z_out.at[i], self.z_in.at[i], near[i]) for i in range(2)]
            self.beside = wire.copy(self.y_out, self.y_in, tp_dev(1, 0))

        def multiply(self, first, last, waits):
            def pair(j, carry):
                for at, wait in waits.items():
                    pl.when(j == at)(wait)
                zd = ((yh + j // 2) % 2) * 2 + (x // 2 + j % 2) % 2

                both = pl.ds(zd * 2, 2)
                if self.half is None:
                    held = self.ctx[both]
                else:
                    held = self.ctx[both, :, self.half * 64 : self.half * 64 + 64]
                done = dot(held.reshape(-1, held.shape[3]), self.w[...])
                self.part[zd] = done.reshape(2, -1, done.shape[1])

                @pl.when(zd == (z + 2) % 4)
                def _():
                    self.r_out[...] = self.part[zd].astype(BF)
                    self.relay[0].start()
                    self.relay[1].start()

                return carry

            lax.fori_loop(first, last, pair, 0)

        def send_on(self):
            for i, zd in enumerate(((z + 3) % 4, (z + 1) % 4)):
                mid = slice(i * self.rows, (i + 1) * self.rows)
                rest = slice((1 - i) * self.rows, (2 - i) * self.rows)
                self.z_out[i, :, rest, :] = self.part[zd, :, rest, :].astype(BF)
                self.relay[i].wait_recv()
                self.z_out[i, :, mid, :] = (self.part[zd, :, mid, :] + self.r_in[i].astype(F32)).astype(BF)
                self.along[i].start()

        def settle(self):
            self.along[0].wait_recv()
            self.along[1].wait_recv()

            def block(u):
                return self.part[z, u] + self.z_in[0, u].astype(F32) + self.z_in[1, u].astype(F32)

            self.y_out[...] = block(1 - yl).astype(BF)
            self.beside.start()
            self.hid[...] = block(yl)

        def finish(self, resid):
            if self.half is None:
                own = resid[...]
            else:
                first = self.half * 64
                own = jnp.concatenate([resid[first : first + 64, :], resid[first + 128 : first + 192, :]], axis=0)
            total = self.hid[...] + own.astype(F32)
            self.beside.wait_recv()
            self.hid[...] = total + self.y_in[...].astype(F32)

    def send_squares(hid, sq, copies):
        value = hid[...]
        ones = jnp.ones((8, value.shape[1]), F32)
        sq[s] = dot(ones, value * value, ((1,), (1,)), lax.Precision.HIGHEST)
        for made in copies:
            made.start()

    def inverse_scale(sq, copies, width):
        for made in copies:
            made.wait_recv()
        total = sq[0]
        for i in range(1, 16):
            total = total + sq[i]
        first = jnp.where(lax.broadcasted_iota(jnp.int32, (8, 128), 0) == 0, 1.0, 0.0)
        column = dot(total, first, ((0,), (0,)), lax.Precision.HIGHEST)
        return 1.0 / jnp.sqrt(column * (1.0 / width) + 1e-05)

    r_s = Reduce(b["sctx"], b["sw"], "s", None)
    r_t = [Reduce(b["tctx"], b["tw"], "t", half) for half in range(2)]

    def ready(gather, plane):
        gather.have_own(plane)
        gather.have_near(plane)
        gather.have_far(plane)

    give_sq.start()
    loads[0].wait()
    g_skv.root(0)
    give_tq.start()
    fill_queries(0, sq, 0)
    prepare(0, (0,))

    def s_partner():
        give_sq.wait_recv()
        fill_queries(0, b["sq_in"], 1)

    def s_near():
        prepare(1, (1, 2))
        fill_queries(1, tq, 0)
        fill_queries(2, tq, 0)
        loads[1].wait()
        g_skv.mid(0)
        g_tkv.root(0)

    def t_start():
        partner_part(0)
        give_tq.wait_recv()
        fill_queries(1, b["tq_in"], 1)
        fill_queries(2, b["tq_in"], 1)

    def t_near():
        g_tkv.mid(0)
        g_tkv.have_own(0)

    def context(one, g, ctx, gather):
        combine(one, g, ctx)
        gather.root(g)

    def s_sums():
        for load in loads[2:]:
            load.wait()
        r_s.multiply(0, 4, {0: lambda: ready(g_s, 0), 2: lambda: ready(g_s, 1)})

    def s_squares():
        r_s.finish(sres)
        send_squares(b["shid"], b["ssq"], s_sq)

    def s_normed():
        inverse = inverse_scale(b["ssq"], s_sq, D_S)
        inverse = jnp.concatenate([inverse, inverse], axis=1)
        normed = (b["shid"][...] * inverse * sg[...]).astype(BF)
        for at, first in enumerate((0, 128, 64, 192)):
            b["nb"][s, at * 64 : (at + 1) * 64, :] = normed[first : first + 64, :]
        g_n.root(0)

    def t1_sums():
        r_t[0].multiply(0, 4, {0: lambda: ready(g_t[0], 0), 2: lambda: ready(g_t[0], 1)})

    def s_last_spread():
        g_s.mid(1)
        g_s.far(0)

    def s_squares_t1():
        s_squares()
        g_t[0].mid(0)

    def t1_spread():
        g_t[0].mid(1)
        g_t[0].far(0)

    def last():
        g_n.mid(0)
        t1_sums()

    attention(
        {
            1: s_partner,
            2: lambda: g_skv.have_own(0),
            4: s_near,
            6: lambda: g_skv.have_left(0),
            10: lambda: g_skv.have_right(0),
            12: lambda: g_skv.far(0),
            14: lambda: g_skv.have_far(0),
            16: t_start,
            18: t_near,
            21: lambda: context(0, 0, b["sctx"], g_s),
            22: lambda: g_tkv.have_left(0),
            25: lambda: context(0, 1, b["sctx"], g_s),
            26: lambda: g_tkv.have_right(0),
            27: lambda: g_s.mid(0),
            28: lambda: g_tkv.far(0),
            29: s_last_spread,
            30: lambda: g_tkv.have_far(0),
            31: lambda: g_s.far(1),
            32: lambda: partner_part(1),
            33: s_sums,
            35: r_s.send_on,
            37: lambda: context(1, 0, b["tctx"], g_t[0]),
            39: r_s.settle,
            41: lambda: context(1, 1, b["tctx"], g_t[0]),
            42: s_squares_t1,
            44: s_normed,
            45: t1_spread,
            46: lambda: g_t[0].far(1),
            47: last,
        }
    )
    partner_part(2)
    g_n.root(1)
    r_t[0].send_on()
    g_n.far(0)
    g_n.mid(1)
    context(2, 0, b["tctx"], g_t[1])
    g_n.far(1)
    r_t[0].settle()
    for made in n_tp:
        made.start()
    ready(g_n, 0)
    ready(g_n, 1)
    b["diff"][...] = jnp.zeros((2, 128, 512), F32)

    def match(k, carry):
        lhs = jnp.concatenate([b["nb"][2 * k], b["nb"][2 * k + 1]], axis=1)
        b["diff"][...] += dot(lhs, b["mp"][k]).reshape(2, 128, 512)
        return carry

    lax.fori_loop(0, 8, match, 0)

    def delta(half):
        inverse = inverse_scale(b["tsq"].at[half], t_sq[half], D_T)
        inverse = jnp.concatenate([inverse, inverse, inverse, inverse], axis=1)
        target = b["thid"][half] * inverse * tg[...]
        b["dl"][half, p] = ((b["diff"][half] - target) * (1.0 / math.sqrt(SLAB))).astype(BF)
        g_d[half].root(0)

    def gradient(half, plane, offs):
        def one(i, carry):
            q = ((z + offs[0] + i * offs[1]) % 4) * 2 + (yl + plane) % 2
            for at in range(2):
                rows = slice(at * 256, (at + 1) * 256)
                lhs = b["ng"][q, at, half * 128 : (half + 1) * 128, :]
                out[rows, :] += dot(lhs, b["dl"][half, q], ((0,), (0,)))
            return carry

        lax.fori_loop(0, offs[2], one, 0)

    own, near, far = (0, 1, 1), (1, 2, 2), (2, 1, 1)
    context(2, 1, b["tctx"], g_t[1])
    g_t[1].mid(0)
    g_t[1].far(0)
    r_t[0].finish(tres)
    send_squares(b["thid"].at[0], b["tsq"].at[0], t_sq[0])
    r_t[1].multiply(0, 2, {0: lambda: ready(g_t[1], 0)})
    g_t[1].mid(1)
    g_t[1].far(1)
    delta(0)
    r_t[1].multiply(2, 4, {2: lambda: ready(g_t[1], 1)})
    for made, onward in zip(n_tp, n_core):
        made.wait_recv()
        onward.start()
    b["ng"][p, 0] = b["nb"][2 * p]
    b["ng"][p, 1] = b["nb"][2 * p + 1]
    out[...] = jnp.zeros((512, 512), F32)
    r_t[1].send_on()
    g_d[0].mid(0)
    g_d[0].root(1)
    for made in n_core:
        made.wait_recv()
    gradient(0, 0, own)
    gradient(0, 0, near)
    r_t[1].settle()
    g_d[0].far(0)
    g_d[0].mid(1)
    r_t[1].finish(tres)
    send_squares(b["thid"].at[1], b["tsq"].at[1], t_sq[1])
    gradient(0, 0, far)
    gradient(0, 1, own)
    delta(1)
    gradient(0, 1, near)
    g_d[0].far(1)
    gradient(0, 1, far)
    gradient(1, 0, own)
    g_d[1].mid(0)
    g_d[1].root(1)
    gradient(1, 0, near)
    gradient(1, 1, own)
    g_d[1].far(0)
    g_d[1].mid(1)
    gradient(1, 0, far)
    gradient(1, 1, near)
    g_d[1].far(1)
    gradient(1, 1, far)
    wire.close()


def per_device(tq, tkv, sq, skv, doc, tres, tw, tg, sres, sw, sg, mp):
    V = pl.BlockSpec(memory_space=pltpu.VMEM)
    A = pl.BlockSpec(memory_space=pl.ANY)
    S = pl.BlockSpec(memory_space=pltpu.SMEM)
    return pl.pallas_call(
        kernel,
        out_shape=jax.ShapeDtypeStruct((512, 512), F32),
        in_specs=[S, V, A, V, A, V, A, V, V, A, V, A],
        out_specs=V,
        scratch_shapes=list(scratch_plan().values()),
        compiler_params=pltpu.CompilerParams(
            collective_id=0, has_side_effects=True, vmem_limit_bytes=63 * 1024 * 1024
        ),
    )(
        doc, tq, tkv, sq, skv, tres, tw, tg.reshape(1, -1), sres, sw, sg.reshape(1, -1), mp.reshape(8, 512, 512)
    )


def solution(mesh):
    in_specs = (
        P("seq", "tp"),
        P(None, "seq", "tp"),
        P("seq", "tp"),
        P(None, "seq", "tp"),
        P(),
        P("tp", "seq"),
        P("tp", "seq"),
        P("seq"),
        P("tp", "seq"),
        P("tp", "seq"),
        P("seq"),
        P(None, "seq"),
    )
    out_specs = P("tp", "seq")
    return jax.shard_map(per_device, mesh=mesh, in_specs=in_specs, out_specs=out_specs, check_vma=False)
```

```python
import math

import jax
import jax.numpy as jnp
from jax import lax
from jax.experimental import pallas as pl
from jax.experimental.pallas import tpu as pltpu
from jax.sharding import PartitionSpec as P

D_T = 8192
D_S = 4096
HEAD = 128
SLAB = 2048
CACHE = 10240
KEYS_CHIP = 1536
HIDDEN = -1e30
LOG2E = math.log2(math.e)
SCALE = LOG2E / math.sqrt(HEAD)
MESH = pl.DeviceIdType.MESH
BF = jnp.bfloat16
F32 = jnp.float32


class Wire:
    def __init__(self, send, recv):
        self.send, self.recv, self.made, self.left = send, recv, [], set()

    def copy(self, src, dst, dev):
        i = len(self.made)
        made = pltpu.make_async_remote_copy(
            src_ref=src, dst_ref=dst, send_sem=self.send.at[i], recv_sem=self.recv.at[i],
            device_id=dev, device_id_type=MESH,
        )
        self.made.append(made)
        return made

    def close(self, first=0, last=None):
        for i in range(first, len(self.made) if last is None else last):
            if i not in self.left:
                self.left.add(i)
                self.made[i].wait_send()


class Gather:
    def __init__(self, wire, block, right, left, across=None, core=None, planes=None):
        self.planes = planes or (1 if across is None else 2)
        self.core = core is not None
        self.cross = wire.copy(block(0, 0, None), block(0, 0, None), across) if across is not None else None
        self.right, self.left, self.on_right, self.on_left, self.pass_on = [], [], [], [], []
        for plane in range(self.planes):
            own = block(plane, 0, None)
            self.right.append(wire.copy(own, own, right))
            self.left.append(wire.copy(own, own, left))
            first, second = block(plane, 3, 0), block(plane, 1, 1)
            self.on_right.append(wire.copy(first, first, right))
            self.on_left.append(wire.copy(second, second, left))
            if self.core:
                refs = [own, block(plane, 3, None), block(plane, 1, None), block(plane, 2, 0), block(plane, 2, 1)]
                self.pass_on.append([wire.copy(ref, ref, core) for ref in refs])

    def root(self, plane, start_cross=True):
        if plane == 1 and self.cross is not None:
            self.cross.wait_recv()
        self.right[plane].start()
        self.left[plane].start()
        if plane == 0 and self.cross is not None and start_cross:
            self.cross.start()
        if self.core:
            self.pass_on[plane][0].start()

    def mid(self, plane):
        self.right[plane].wait_recv()
        self.on_right[plane].start()
        if self.core:
            self.pass_on[plane][1].start()
        self.left[plane].wait_recv()
        self.on_left[plane].start()
        if self.core:
            self.pass_on[plane][2].start()

    def far(self, plane):
        self.on_right[plane].wait_recv()
        if self.core:
            self.pass_on[plane][3].start()
        self.on_left[plane].wait_recv()
        if self.core:
            self.pass_on[plane][4].start()

    def have_own(self, plane):
        self.pass_on[plane][0].wait_recv()

    def have_left(self, plane):
        self.pass_on[plane][1].wait_recv()

    def have_right(self, plane):
        self.pass_on[plane][2].wait_recv()

    def have_near(self, plane):
        self.have_left(plane)
        self.have_right(plane)

    def have_far(self, plane):
        self.pass_on[plane][3].wait_recv()
        self.pass_on[plane][4].wait_recv()


def dot(a, b, dims=((1,), (0,)), precision=None):
    return lax.dot_general(a, b, (dims, ((), ())), precision=precision, preferred_element_type=F32)


def scratch_plan():
    V = pltpu.VMEM
    D = pltpu.SemaphoreType.DMA
    return dict(
        kv=V((12, 2, 2, 768, 128), BF),
        kx=V((12, 2, 768, 256), BF),
        vt=V((12, 2, 144, 768), BF),
        score0=V((768, 512), F32),
        score1=V((768, 512), F32),
        top0=V((8, 512), F32),
        top1=V((8, 512), F32),
        qa=V((3, 2, 512, 256), BF),
        sq_in=V((128, 512), BF),
        m=V((3, 2, 8, 512), F32),
        acc=V((3, 2, 144, 512), F32),
        o_out=V((2, 128, 512), BF),
        o_in=V((2, 128, 512), BF),
        l_out=V((2, 8, 512), F32),
        l_in=V((2, 8, 512), F32),
        tctx=V((8, 2, 128, 1024), BF),
        sctx=V((8, 2, 128, 512), BF),
        tw=V((1024, 512), BF),
        sw=V((512, 256), BF),
        ty_out=V((2, 128, 512), BF),
        ty_in=V((2, 128, 512), BF),
        sy_out=V((256, 256), BF),
        sy_in=V((256, 256), BF),
        tpart=V((4, 2, 128, 512), F32),
        spart=V((4, 2, 256, 256), F32),
        tr_out=V((2, 2, 128, 512), BF),
        tr_in=V((2, 2, 2, 64, 512), BF),
        sr_out=V((2, 256, 256), BF),
        sr_in=V((2, 2, 128, 256), BF),
        tz_out=V((2, 2, 2, 128, 512), BF),
        tz_in=V((2, 2, 2, 128, 512), BF),
        sz_out=V((2, 2, 256, 256), BF),
        sz_in=V((2, 2, 256, 256), BF),
        thid=V((2, 128, 512), F32),
        shid=V((256, 256), F32),
        tsq=V((2, 16, 8, 128), F32),
        ssq=V((16, 8, 256), F32),
        nb=V((16, 256, 256), BF),
        ng=V((8, 2, 256, 256), BF),
        dl=V((2, 8, 128, 512), BF),
        diff=V((2, 128, 512), F32),
        wsend=D((200,)),
        wrecv=D((200,)),
        loc=D((8,)),
    )


def kernel(doc, tq, tkv_h, sq, skv_h, tres, tw_h, tg, sres, sw_h, sg, mp_h, out, *scratch):
    b = dict(zip(scratch_plan(), scratch))
    s = lax.axis_index("seq")
    p = lax.axis_index("tp")
    yh, x, c = s // 8, (s // 2) % 4, s % 2
    z, yl = p // 2, p % 2
    k_own = yh * 4 + x

    def seq_dev(plane, off, other):
        return ((((yh + plane) % 2) * 4 + (x + off) % 4) * 2 + (c + other) % 2, p)

    def tp_dev(plane, off):
        return (s, ((z + off) % 4) * 2 + (yl + plane) % 2)

    right, left, across, core = seq_dev(0, 1, 0), seq_dev(0, 3, 0), seq_dev(1, 0, 0), seq_dev(0, 0, 1)

    loads = [
        pltpu.make_async_copy(skv_h, b["kv"].at[x, c], b["loc"].at[0]),
        pltpu.make_async_copy(tkv_h, b["kv"].at[4 + k_own, c], b["loc"].at[1]),
        pltpu.make_async_copy(sw_h, b["sw"], b["loc"].at[2]),
        pltpu.make_async_copy(tw_h, b["tw"], b["loc"].at[3]),
    ]
    for load in loads:
        load.start()
    map_loads = [
        pltpu.make_async_copy(
            mp_h.at[:, :, pl.ds(u * 256, 256)], b["kx"].at[pl.ds(0, 8), u, pl.ds(0, 512)], b["loc"].at[4 + u]
        )
        for u in range(2)
    ]

    barrier = pltpu.get_barrier_semaphore()
    for off in range(1, 16):
        pl.semaphore_signal(barrier, inc=1, device_id=((s + off) % 16, p), device_id_type=MESH)
    for off in range(1, 8):
        pl.semaphore_signal(barrier, inc=1, device_id=(s, (p + off) % 8), device_id_type=MESH)

    wire = Wire(b["wsend"], b["wrecv"])
    give_sq = wire.copy(sq, b["sq_in"], across)

    def kv_block(model):
        def block(plane, off, part):
            at = (x + off) % 4 + model * (4 + ((yh + plane) % 2) * 4)
            if part is None:
                return b["kv"].at[at, c]
            return b["kv"].at[at, c, part]

        return block

    def s_block(plane, off, part):
        at = ((yh + plane) % 2) * 4 + (x + off) % 4
        if part is None:
            return b["sctx"].at[at, c]
        return b["sctx"].at[at, c, pl.ds(part * 64, 64)]

    def t_block(half):
        def block(plane, off, part):
            at = ((yh + plane) % 2) * 4 + (x + off) % 4
            if part is None:
                return b["tctx"].at[at, c, pl.ds(half * 64, 64)]
            return b["tctx"].at[at, c, pl.ds(half * 64 + part * 32, 32)]

        return block

    def nb_block(plane, off, part):
        at = (((yh + plane) % 2) * 4 + (x + off) % 4) * 2 + c
        if part is None:
            return b["nb"].at[at]
        return b["nb"].at[at, pl.ds(part * 128, 128)]

    def dl_block(half):
        def block(plane, off, part):
            at = ((z + off) % 4) * 2 + (yl + plane) % 2
            if part is None:
                return b["dl"].at[half, at]
            return b["dl"].at[half, at, pl.ds(part * 64, 64)]

        return block

    g_skv = Gather(wire, kv_block(0), right, left, None, core)
    g_tkv = Gather(wire, kv_block(1), right, left, across, core)
    keys_sent = len(wire.made)
    g_s = Gather(wire, s_block, right, left, None, core, 2)
    g_t = [Gather(wire, t_block(half), right, left, across, core) for half in range(2)]
    contexts_sent = len(wire.made)
    g_n = Gather(wire, nb_block, right, left, across, core)
    g_d = [Gather(wire, dl_block(half), tp_dev(0, 1), tp_dev(0, 3), tp_dev(1, 0), None) for half in range(2)]
    give_o = [wire.copy(b["o_out"].at[1 - g], b["o_in"].at[g], across) for g in range(2)]
    give_l = [wire.copy(b["l_out"].at[1 - g], b["l_in"].at[g], across) for g in range(2)]
    s_sq = [wire.copy(b["ssq"].at[s], b["ssq"].at[s], ((s + off) % 16, p)) for off in range(1, 16)]
    t_sq = [
        [wire.copy(b["tsq"].at[half, s], b["tsq"].at[half, s], ((s + off) % 16, p)) for off in range(1, 16)]
        for half in range(2)
    ]
    n_tp = [
        wire.copy(b["nb"].at[((p + off) % 8) * 2 + c], b["ng"].at[p, c], (s, (p + off) % 8)) for off in range(1, 8)
    ]
    n_core = [
        wire.copy(b["ng"].at[(p + 8 - off) % 8, c], b["ng"].at[(p + 8 - off) % 8, c], core) for off in range(1, 8)
    ]

    qa, m, acc = b["qa"], b["m"], b["acc"]
    heads, tokens = (4, 8, 8), (128, 64, 64)

    def fill_queries(one, src, group):
        first = 64 * (one // 2)
        for h in range(heads[one]):
            rows = slice(h * tokens[one], (h + 1) * tokens[one])
            qa[one, group, rows, 0:128] = src[first : first + tokens[one], h * 128 : (h + 1) * 128]

    def prepare(first, last, passes):
        rows = lax.broadcasted_iota(jnp.int32, (128, 128), 0)
        lanes = lax.broadcasted_iota(jnp.int32, (128, 128), 1)
        for one in passes:
            eye = jnp.where(rows % tokens[one] + 64 * (one // 2) == lanes, 1.0, 0.0).astype(BF)
            for g in range(2 if one == 0 else 1):
                for i in range(4):
                    qa[one, g, i * 128 : (i + 1) * 128, 128:256] = eye
            m[one] = jnp.full((2, 8, 512), HIDDEN, F32)
            acc[one] = jnp.zeros((2, 144, 512), F32)

        def extra(i, carry):
            b["kx"][i, :, :, 128:256] = jnp.zeros((2, 768, 128), BF)
            b["vt"][i, :, 128:144, :] = jnp.ones((2, 16, 768), BF)
            return carry

        lax.fori_loop(first, last, extra, 0)

    first_key = doc[0]

    def tile_at(n, u):
        third = n // 8
        t = (third + 1) // 2
        other = third // 2
        one = t * (1 + (1 - other) * ((n % 8) // 4) + other * (n % 2))
        i = (1 - t + other) * ((n % 8) // 2) + (t - other) * (n % 4)
        plane = (yh + other) % 2
        at = (x + 3 * i + 3 * (i // 2) + 2 * (i // 3)) % 4
        from_core = (c + (1 - t) * (n % 2) + t * u) % 2
        return one, (1 - t) * u, t * (4 + plane * 4) + at, plane, at, from_core

    def build(n, u):
        one, g, block, plane, at, from_core = tile_at(n, u)
        base = (plane * 4 + at) * KEYS_CHIP + from_core * 768

        @pl.when((one <= 1) if u == 0 else (one == 1))
        def _():
            b["vt"][block, from_core, 0:128, :] = b["kv"][block, from_core, 1].T
            b["kx"][block, from_core, :, 0:128] = b["kv"][block, from_core, 0]

            @pl.when(plane == 0)
            def _():
                key = lax.broadcasted_iota(jnp.int32, (768, 128), 0)
                b["kx"][block, from_core, :, 128:256] = jnp.where(key >= first_key - base, 0.0, HIDDEN).astype(BF)

        @pl.when((one <= 1) & (plane == 1) & (at >= 2))
        def _():
            ahead = CACHE + ((((yh + g) % 2) * 4 + x) * 2 + c) * 128 - base
            key = lax.broadcasted_iota(jnp.int32, (768, 128), 0)
            row = lax.broadcasted_iota(jnp.int32, (768, 128), 1)
            b["kx"][block, from_core, :, 128:256] = jnp.where(key - row <= ahead, 0.0, HIDDEN).astype(BF)

    scores, tops = (b["score0"], b["score1"]), (b["top0"], b["top1"])

    def overlapped(n, u, weigh_n, weigh=True):
        one, g, block, _, _, from_core = tile_at(n, u)
        queries = qa[one, g]
        top = jnp.full((8, 512), HIDDEN, F32)
        if weigh:
            w_one, w_g, w_block, _, _, w_core = tile_at(weigh_n, 1 - u)
            old = m[w_one, w_g]
            peak = jnp.max(tops[1 - u][...], axis=0, keepdims=True)
            new = jnp.maximum(old, jnp.broadcast_to(peak, (8, 512)))
            total = (acc[w_one, w_g].reshape(18, 8, 512) * jnp.exp2((old - new) * SCALE)[None]).reshape(144, 512)
        for j in range(3):
            keys = slice(j * 256, (j + 1) * 256)
            fresh = dot(b["kx"][block, from_core, keys, :], queries, ((1,), (1,)))
            scores[u][keys, :] = fresh
            top = jnp.maximum(top, jnp.max(fresh.reshape(32, 8, 512), axis=0))
            if weigh:
                held = scores[1 - u][keys, :].reshape(32, 8, 512)
                weights = jnp.exp2((held - new[None]) * SCALE).reshape(256, 512).astype(BF)
                total = total + dot(b["vt"][w_block, w_core, :, keys], weights)
        tops[u][...] = top
        if weigh:
            m[w_one, w_g] = new
            acc[w_one, w_g] = total

    def attention(hooks):
        build(0, 0)
        overlapped(0, 0, 0, weigh=False)

        def step(n, carry):
            for at_step, hook in hooks.items():
                pl.when(n == at_step)(hook)
            build(n, 1)
            overlapped(n, 1, n)
            after = (n + 1) % 24
            build(after, 0)
            overlapped(after, 0, n)
            return carry

        lax.fori_loop(0, 24, step, 0)

    def part_of(one, g):
        total = acc[one, g, 128:136, :]
        mean = (acc[one, g, 0:128, :].reshape(16, 8, 512) * (1.0 / total)[None]).reshape(128, 512)
        return mean, m[one, g] * SCALE + jnp.log(total) * LOG2E

    def partner_part():
        for g in (1, 0):
            mean, logs = part_of(0, g)
            b["o_out"][g] = mean.astype(BF)
            b["l_out"][g] = logs
            give_o[1 - g].start()
            give_l[1 - g].start()

    def keep_context(one, plane, both, ctx):
        both = both.T.astype(BF)
        count, first = tokens[one], 64 * (one // 2)
        for h in range(heads[one]):
            held = both[h * count : (h + 1) * count, :]
            ctx[plane * 4 + x, c, first : first + count, h * 128 : (h + 1) * 128] = held

    def s_context(g):
        give_o[g].wait_recv()
        give_l[g].wait_recv()
        mine, log_mine = part_of(0, g)
        share = 1.0 / (1.0 + jnp.exp2(log_mine - b["l_in"][g]))
        other = b["o_in"][g].astype(F32)
        both = mine + ((other - mine).reshape(16, 8, 512) * share[None]).reshape(128, 512)
        keep_context(0, (yh + g) % 2, both, b["sctx"])
        g_s.root(g)

    def t_context(half):
        keep_context(1 + half, yh, part_of(1 + half, 0)[0], b["tctx"])
        g_t[half].root(0)

    class Reduce:
        def __init__(self, ctx, w, name, half):
            self.ctx, self.w, self.half = ctx, w, half

            def of(key):
                return b[name + key] if half is None else b[name + key].at[half]

            self.y_out, self.y_in, self.part, self.hid = of("y_out"), of("y_in"), b[name + "part"], of("hid")
            self.r_out, self.r_in, self.z_out, self.z_in = of("r_out"), of("r_in"), of("z_out"), of("z_in")
            self.rows = self.part.shape[2] // 2
            near = (tp_dev(0, 3), tp_dev(0, 1))
            self.relay = [
                wire.copy(self.r_out.at[:, pl.ds(i * self.rows, self.rows)], self.r_in.at[i], near[i]) for i in range(2)
            ]
            self.along = [wire.copy(self.z_out.at[i], self.z_in.at[i], near[i]) for i in range(2)]
            self.beside = wire.copy(self.y_out, self.y_in, tp_dev(1, 0))

        def multiply(self, first, last, waits):
            def pair(j, carry):
                for at, wait in waits.items():
                    pl.when(j == at)(wait)
                zd = ((yh + j // 2) % 2) * 2 + (x // 2 + j % 2) % 2

                both = pl.ds(zd * 2, 2)
                if self.half is None:
                    held = self.ctx[both]
                else:
                    held = self.ctx[both, :, self.half * 64 : self.half * 64 + 64]
                done = dot(held.reshape(-1, held.shape[3]), self.w[...])
                self.part[zd] = done.reshape(2, -1, done.shape[1])

                @pl.when(zd == (z + 2) % 4)
                def _():
                    self.r_out[...] = self.part[zd].astype(BF)
                    self.relay[0].start()
                    self.relay[1].start()

                return carry

            lax.fori_loop(first, last, pair, 0)

        def send_on(self):
            for i, zd in enumerate(((z + 3) % 4, (z + 1) % 4)):
                mid = slice(i * self.rows, (i + 1) * self.rows)
                rest = slice((1 - i) * self.rows, (2 - i) * self.rows)
                self.z_out[i, :, rest, :] = self.part[zd, :, rest, :].astype(BF)
                self.relay[i].wait_recv()
                self.z_out[i, :, mid, :] = (self.part[zd, :, mid, :] + self.r_in[i].astype(F32)).astype(BF)
                self.along[i].start()

        def settle(self):
            self.along[0].wait_recv()
            self.along[1].wait_recv()

            def block(u):
                return self.part[z, u] + self.z_in[0, u].astype(F32) + self.z_in[1, u].astype(F32)

            self.y_out[...] = block(1 - yl).astype(BF)
            self.beside.start()
            self.hid[...] = block(yl)

        def finish(self, resid):
            if self.half is None:
                own = resid[...]
            else:
                first = self.half * 64
                own = jnp.concatenate([resid[first : first + 64, :], resid[first + 128 : first + 192, :]], axis=0)
            total = self.hid[...] + own.astype(F32)
            self.beside.wait_recv()
            self.hid[...] = total + self.y_in[...].astype(F32)

    def send_squares(hid, sq, copies):
        value = hid[...]
        ones = jnp.ones((8, value.shape[1]), F32)
        sq[s] = dot(ones, value * value, ((1,), (1,)), lax.Precision.HIGHEST)
        for made in copies:
            made.start()

    def inverse_scale(sq, copies, width):
        for made in copies:
            made.wait_recv()
        total = sq[0]
        for i in range(1, 16):
            total = total + sq[i]
        first = jnp.where(lax.broadcasted_iota(jnp.int32, (8, 128), 0) == 0, 1.0, 0.0)
        column = dot(total, first, ((0,), (0,)), lax.Precision.HIGHEST)
        return 1.0 / jnp.sqrt(column * (1.0 / width) + 1e-05)

    r_s = Reduce(b["sctx"], b["sw"], "s", None)
    r_t = [Reduce(b["tctx"], b["tw"], "t", half) for half in range(2)]

    def ready(gather, plane):
        gather.have_own(plane)
        gather.have_near(plane)
        gather.have_far(plane)

    fill_queries(0, sq, 0)
    prepare(0, 4, (0,))
    loads[0].wait()
    loads[1].wait()
    pl.semaphore_wait(barrier, 22)
    g_skv.root(0)
    give_sq.start()
    g_tkv.cross.start()

    def s_partner():
        g_skv.have_own(0)
        give_sq.wait_recv()
        fill_queries(0, b["sq_in"], 1)

    def s_near():
        prepare(4, 12, (1, 2))
        fill_queries(1, tq, 0)
        fill_queries(2, tq, 0)
        g_skv.mid(0)
        g_tkv.root(0, False)

    def t_start():
        partner_part()
        g_tkv.have_own(0)
        g_tkv.mid(0)
        g_tkv.root(1)

    def s_sums():
        for load in loads[2:]:
            load.wait()
        r_s.multiply(0, 4, {0: lambda: ready(g_s, 0), 2: lambda: ready(g_s, 1)})

    def s_squares():
        r_s.finish(sres)
        send_squares(b["shid"], b["ssq"], s_sq)

    def s_normed():
        inverse = inverse_scale(b["ssq"], s_sq, D_S)
        inverse = jnp.concatenate([inverse, inverse], axis=1)
        normed = (b["shid"][...] * inverse * sg[...]).astype(BF)
        for at, first in enumerate((0, 128, 64, 192)):
            b["nb"][s, at * 64 : (at + 1) * 64, :] = normed[first : first + 64, :]
        g_n.root(0)

    def t1_sums():
        r_t[0].multiply(0, 4, {0: lambda: ready(g_t[0], 0), 2: lambda: ready(g_t[0], 1)})

    def both(*hooks):
        def run():
            for hook in hooks:
                hook()

        return run

    attention(
        {
            0: s_partner,
            1: s_near,
            2: lambda: g_skv.have_left(0),
            4: lambda: g_skv.have_right(0),
            5: lambda: g_skv.far(0),
            6: lambda: g_skv.have_far(0),
            8: t_start,
            9: lambda: g_tkv.have_left(0),
            10: both(lambda: g_tkv.have_right(0), lambda: g_tkv.far(0)),
            11: lambda: g_tkv.have_far(0),
            12: lambda: s_context(0),
            16: both(lambda: g_tkv.have_own(1), lambda: s_context(1)),
            17: lambda: g_tkv.mid(1),
            18: both(lambda: g_tkv.have_left(1), lambda: g_s.mid(0)),
            20: both(lambda: g_tkv.have_right(1), lambda: g_s.mid(1), lambda: g_s.far(0)),
            21: lambda: g_tkv.far(1),
            22: both(lambda: g_tkv.have_far(1), lambda: g_s.far(1)),
            23: lambda: t_context(0),
        }
    )
    for load in map_loads:
        load.start()
    t_context(1)
    s_sums()
    g_t[0].mid(0)
    g_t[0].root(1)
    r_s.send_on()
    g_t[1].mid(0)
    g_t[1].root(1)
    g_t[0].far(0)
    g_t[0].mid(1)
    r_s.settle()
    wire.close(0, keys_sent)
    g_t[0].far(1)
    t1_sums()
    s_squares()
    g_t[1].far(0)
    g_t[1].mid(1)
    r_t[0].send_on()
    s_normed()
    g_t[1].far(1)
    r_t[0].settle()
    g_n.mid(0)
    g_n.root(1)
    r_t[1].multiply(0, 4, {0: lambda: ready(g_t[1], 0), 2: lambda: ready(g_t[1], 1)})
    r_t[0].finish(tres)
    send_squares(b["thid"].at[0], b["tsq"].at[0], t_sq[0])
    g_n.far(0)
    g_n.mid(1)
    r_t[1].send_on()
    wire.close(keys_sent, contexts_sent)
    g_n.far(1)
    for made in n_tp:
        made.start()
    ready(g_n, 0)
    ready(g_n, 1)
    b["diff"][...] = jnp.zeros((2, 128, 512), F32)
    for load in map_loads:
        load.wait()

    def match(k, carry):
        lhs = jnp.concatenate([b["nb"][2 * k], b["nb"][2 * k + 1]], axis=1)
        for u in range(2):
            b["diff"][:, :, u * 256 : (u + 1) * 256] += dot(lhs, b["kx"][k, u, 0:512, :]).reshape(2, 128, 256)
        return carry

    lax.fori_loop(0, 8, match, 0)

    def delta(half):
        inverse = inverse_scale(b["tsq"].at[half], t_sq[half], D_T)
        inverse = jnp.concatenate([inverse, inverse, inverse, inverse], axis=1)
        target = b["thid"][half] * inverse * tg[...]
        b["dl"][half, p] = ((b["diff"][half] - target) * (1.0 / math.sqrt(SLAB))).astype(BF)
        g_d[half].root(0)

    def gradient(half, plane, offs):
        def one(i, carry):
            q = ((z + offs[0] + i * offs[1]) % 4) * 2 + (yl + plane) % 2
            for at in range(2):
                rows = slice(at * 256, (at + 1) * 256)
                lhs = b["ng"][q, at, half * 128 : (half + 1) * 128, :]
                out[rows, :] += dot(lhs, b["dl"][half, q], ((0,), (0,)))
            return carry

        lax.fori_loop(0, offs[2], one, 0)

    own, near, far = (0, 1, 1), (1, 2, 2), (2, 1, 1)
    r_t[1].settle()
    delta(0)
    r_t[1].finish(tres)
    send_squares(b["thid"].at[1], b["tsq"].at[1], t_sq[1])
    b["ng"][p, 0] = b["nb"][2 * p]
    b["ng"][p, 1] = b["nb"][2 * p + 1]
    out[...] = jnp.zeros((512, 512), F32)
    g_d[0].mid(0)
    g_d[0].root(1)
    delta(1)
    for made, onward in zip(n_tp, n_core):
        made.wait_recv()
        onward.start()
    g_d[0].far(0)
    g_d[0].mid(1)
    for made in n_core:
        made.wait_recv()
    gradient(0, 0, own)
    gradient(0, 0, near)
    gradient(0, 0, far)
    gradient(0, 1, own)
    g_d[1].mid(0)
    g_d[1].root(1)
    gradient(0, 1, near)
    g_d[0].far(1)
    gradient(0, 1, far)
    gradient(1, 0, own)
    gradient(1, 0, near)
    gradient(1, 1, own)
    g_d[1].far(0)
    g_d[1].mid(1)
    gradient(1, 0, far)
    gradient(1, 1, near)
    g_d[1].far(1)
    gradient(1, 1, far)
    wire.close()


def per_device(tq, tkv, sq, skv, doc, tres, tw, tg, sres, sw, sg, mp):
    V = pl.BlockSpec(memory_space=pltpu.VMEM)
    A = pl.BlockSpec(memory_space=pl.ANY)
    S = pl.BlockSpec(memory_space=pltpu.SMEM)
    return pl.pallas_call(
        kernel,
        out_shape=jax.ShapeDtypeStruct((512, 512), F32),
        in_specs=[S, V, A, V, A, V, A, V, V, A, V, A],
        out_specs=V,
        scratch_shapes=list(scratch_plan().values()),
        compiler_params=pltpu.CompilerParams(
            collective_id=0, has_side_effects=True, vmem_limit_bytes=63 * 1024 * 1024
        ),
    )(
        doc, tq, tkv, sq, skv, tres, tw, tg.reshape(1, -1), sres, sw, sg.reshape(1, -1), mp.reshape(8, 512, 512)
    )


def solution(mesh):
    in_specs = (
        P("seq", "tp"),
        P(None, "seq", "tp"),
        P("seq", "tp"),
        P(None, "seq", "tp"),
        P(),
        P("tp", "seq"),
        P("tp", "seq"),
        P("seq"),
        P("tp", "seq"),
        P("tp", "seq"),
        P("seq"),
        P(None, "seq"),
    )
    out_specs = P("tp", "seq")
    return jax.shard_map(per_device, mesh=mesh, in_specs=in_specs, out_specs=out_specs, check_vma=False)
```

```python
import math

import jax
import jax.numpy as jnp
from jax import lax
from jax.experimental import pallas as pl
from jax.experimental.pallas import tpu as pltpu
from jax.sharding import PartitionSpec as P

D_T = 8192
D_S = 4096
HEAD = 128
SLAB = 2048
CACHE = 10240
KEYS_CHIP = 1536
HIDDEN = -1e30
LOG2E = math.log2(math.e)
SCALE = LOG2E / math.sqrt(HEAD)
MESH = pl.DeviceIdType.MESH
BF = jnp.bfloat16
F32 = jnp.float32


class Wire:
    def __init__(self, send, recv):
        self.send, self.recv, self.made, self.left = send, recv, [], set()

    def copy(self, src, dst, dev):
        i = len(self.made)
        made = pltpu.make_async_remote_copy(
            src_ref=src, dst_ref=dst, send_sem=self.send.at[i], recv_sem=self.recv.at[i],
            device_id=dev, device_id_type=MESH,
        )
        self.made.append(made)
        return made

    def close(self, first=0, last=None):
        for i in range(first, len(self.made) if last is None else last):
            if i not in self.left:
                self.left.add(i)
                self.made[i].wait_send()


class Gather:
    def __init__(self, wire, block, right, left, across=None, core=None, planes=None):
        self.planes = planes or (1 if across is None else 2)
        self.core = core is not None
        self.cross = wire.copy(block(0, 0, None), block(0, 0, None), across) if across is not None else None
        self.right, self.left, self.on_right, self.on_left, self.pass_on = [], [], [], [], []
        for plane in range(self.planes):
            own = block(plane, 0, None)
            self.right.append(wire.copy(own, own, right))
            self.left.append(wire.copy(own, own, left))
            first, second = block(plane, 3, 0), block(plane, 1, 1)
            self.on_right.append(wire.copy(first, first, right))
            self.on_left.append(wire.copy(second, second, left))
            if self.core:
                refs = [own, block(plane, 3, None), block(plane, 1, None), block(plane, 2, 0), block(plane, 2, 1)]
                self.pass_on.append([wire.copy(ref, ref, core) for ref in refs])

    def root(self, plane, start_cross=True):
        if plane == 1 and self.cross is not None:
            self.cross.wait_recv()
        self.right[plane].start()
        self.left[plane].start()
        if plane == 0 and self.cross is not None and start_cross:
            self.cross.start()
        if self.core:
            self.pass_on[plane][0].start()

    def mid(self, plane):
        self.right[plane].wait_recv()
        self.on_right[plane].start()
        if self.core:
            self.pass_on[plane][1].start()
        self.left[plane].wait_recv()
        self.on_left[plane].start()
        if self.core:
            self.pass_on[plane][2].start()

    def far(self, plane):
        self.on_right[plane].wait_recv()
        if self.core:
            self.pass_on[plane][3].start()
        self.on_left[plane].wait_recv()
        if self.core:
            self.pass_on[plane][4].start()

    def have_own(self, plane):
        self.pass_on[plane][0].wait_recv()

    def have_left(self, plane):
        self.pass_on[plane][1].wait_recv()

    def have_right(self, plane):
        self.pass_on[plane][2].wait_recv()

    def have_near(self, plane):
        self.have_left(plane)
        self.have_right(plane)

    def have_far(self, plane):
        self.pass_on[plane][3].wait_recv()
        self.pass_on[plane][4].wait_recv()


def dot(a, b, dims=((1,), (0,)), precision=None):
    return lax.dot_general(a, b, (dims, ((), ())), precision=precision, preferred_element_type=F32)


def scratch_plan():
    V = pltpu.VMEM
    D = pltpu.SemaphoreType.DMA
    return dict(
        kv=V((12, 2, 2, 768, 128), BF),
        kx=V((12, 2, 768, 256), BF),
        vt=V((12, 2, 144, 768), BF),
        score0=V((768, 512), F32),
        score1=V((768, 512), F32),
        top0=V((8, 512), F32),
        top1=V((8, 512), F32),
        qa=V((3, 2, 512, 256), BF),
        sq_in=V((128, 512), BF),
        m=V((3, 2, 8, 512), F32),
        acc=V((3, 2, 144, 512), F32),
        o_out=V((2, 128, 512), BF),
        o_in=V((2, 128, 512), BF),
        l_out=V((2, 8, 512), F32),
        l_in=V((2, 8, 512), F32),
        tctx=V((8, 2, 128, 1024), BF),
        sctx=V((8, 2, 128, 512), BF),
        tw=V((1024, 512), BF),
        sw=V((512, 256), BF),
        ty_out=V((2, 128, 512), BF),
        ty_in=V((2, 128, 512), BF),
        sy_out=V((256, 256), BF),
        sy_in=V((256, 256), BF),
        tpart=V((4, 2, 128, 512), F32),
        spart=V((4, 2, 256, 256), F32),
        tr_out=V((2, 2, 128, 512), BF),
        tr_in=V((2, 2, 2, 64, 512), BF),
        sr_out=V((2, 256, 256), BF),
        sr_in=V((2, 2, 128, 256), BF),
        tz_out=V((2, 2, 2, 128, 512), BF),
        tz_in=V((2, 2, 2, 128, 512), BF),
        sz_out=V((2, 2, 256, 256), BF),
        sz_in=V((2, 2, 256, 256), BF),
        thid=V((2, 128, 512), F32),
        shid=V((256, 256), F32),
        tsq=V((2, 16, 8, 128), F32),
        ssq=V((16, 8, 256), F32),
        nb=V((16, 256, 256), BF),
        ng=V((8, 2, 256, 256), BF),
        dl=V((2, 8, 128, 512), BF),
        diff=V((2, 128, 512), F32),
        wsend=D((208,)),
        wrecv=D((208,)),
        loc=D((8,)),
    )


def kernel(doc, tq, tkv_h, sq, skv_h, tres, tw_h, tg, sres, sw_h, sg, mp_h, out, *scratch):
    b = dict(zip(scratch_plan(), scratch))
    s = lax.axis_index("seq")
    p = lax.axis_index("tp")
    yh, x, c = s // 8, (s // 2) % 4, s % 2
    z, yl = p // 2, p % 2
    k_own = yh * 4 + x

    def seq_dev(plane, off, other):
        return ((((yh + plane) % 2) * 4 + (x + off) % 4) * 2 + (c + other) % 2, p)

    def tp_dev(plane, off):
        return (s, ((z + off) % 4) * 2 + (yl + plane) % 2)

    right, left, across, core = seq_dev(0, 1, 0), seq_dev(0, 3, 0), seq_dev(1, 0, 0), seq_dev(0, 0, 1)

    loads = [
        pltpu.make_async_copy(skv_h, b["kv"].at[x, c], b["loc"].at[0]),
        pltpu.make_async_copy(tkv_h, b["kv"].at[4 + k_own, c], b["loc"].at[1]),
        pltpu.make_async_copy(sw_h, b["sw"], b["loc"].at[2]),
        pltpu.make_async_copy(tw_h, b["tw"], b["loc"].at[3]),
    ]
    for load in loads:
        load.start()
    map_loads = [
        pltpu.make_async_copy(
            mp_h.at[:, :, pl.ds(u * 256, 256)], b["kx"].at[pl.ds(0, 8), u, pl.ds(0, 512)], b["loc"].at[4 + u]
        )
        for u in range(2)
    ]

    barrier = pltpu.get_barrier_semaphore()
    for off in range(1, 16):
        pl.semaphore_signal(barrier, inc=1, device_id=((s + off) % 16, p), device_id_type=MESH)
    for off in range(1, 8):
        pl.semaphore_signal(barrier, inc=1, device_id=(s, (p + off) % 8), device_id_type=MESH)

    wire = Wire(b["wsend"], b["wrecv"])
    give_sq = wire.copy(sq, b["sq_in"], across)

    def kv_block(model):
        def block(plane, off, part):
            at = (x + off) % 4 + model * (4 + ((yh + plane) % 2) * 4)
            if part is None:
                return b["kv"].at[at, c]
            return b["kv"].at[at, c, part]

        return block

    def s_block(plane, off, part):
        at = ((yh + plane) % 2) * 4 + (x + off) % 4
        if part is None:
            return b["sctx"].at[at, c]
        return b["sctx"].at[at, c, pl.ds(part * 64, 64)]

    def t_block(half):
        def block(plane, off, part):
            at = ((yh + plane) % 2) * 4 + (x + off) % 4
            if part is None:
                return b["tctx"].at[at, c, pl.ds(half * 64, 64)]
            return b["tctx"].at[at, c, pl.ds(half * 64 + part * 32, 32)]

        return block

    def nb_block(plane, off, part):
        at = (((yh + plane) % 2) * 4 + (x + off) % 4) * 2 + c
        if part is None:
            return b["nb"].at[at]
        return b["nb"].at[at, pl.ds(part * 128, 128)]

    def dl_block(half):
        def block(plane, off, part):
            at = ((z + off) % 4) * 2 + (yl + plane) % 2
            if part is None:
                return b["dl"].at[half, at]
            return b["dl"].at[half, at, pl.ds(part * 64, 64)]

        return block

    g_skv = Gather(wire, kv_block(0), right, left, None, core)
    g_tkv = Gather(wire, kv_block(1), right, left, across, core)
    keys_sent = len(wire.made)
    g_s = Gather(wire, s_block, right, left, None, core, 2)
    g_t = [Gather(wire, t_block(half), right, left, across, core) for half in range(2)]
    contexts_sent = len(wire.made)
    g_n = Gather(wire, nb_block, right, left, across, core)
    g_d = [Gather(wire, dl_block(half), tp_dev(0, 1), tp_dev(0, 3), tp_dev(1, 0), None) for half in range(2)]
    give_o = [wire.copy(b["o_out"].at[1 - g], b["o_in"].at[g], across) for g in range(2)]
    give_l = [wire.copy(b["l_out"].at[1 - g], b["l_in"].at[g], across) for g in range(2)]
    s_sq = [wire.copy(b["ssq"].at[s], b["ssq"].at[s], ((s + off) % 16, p)) for off in range(1, 16)]
    t_sq = [
        [wire.copy(b["tsq"].at[half, s], b["tsq"].at[half, s], ((s + off) % 16, p)) for off in range(1, 16)]
        for half in range(2)
    ]
    half_rows = pl.ds((x % 2) * 128, 128)
    beside_x = seq_dev(0, 1 + 2 * (x % 2), 0)
    n_tp = [
        wire.copy(
            b["nb"].at[((p + off) % 8) * 2 + c, half_rows], b["ng"].at[p, c, half_rows], (s, (p + off) % 8)
        )
        for off in range(1, 8)
    ]
    n_x = [
        wire.copy(
            b["ng"].at[(p + 8 - off) % 8, c, half_rows], b["ng"].at[(p + 8 - off) % 8, c, half_rows], beside_x
        )
        for off in range(1, 8)
    ]
    n_core = [
        wire.copy(b["ng"].at[(p + 8 - off) % 8, c], b["ng"].at[(p + 8 - off) % 8, c], core) for off in range(1, 8)
    ]

    qa, m, acc = b["qa"], b["m"], b["acc"]
    heads, tokens = (4, 8, 8), (128, 64, 64)

    def fill_queries(one, src, group):
        first = 64 * (one // 2)
        for h in range(heads[one]):
            rows = slice(h * tokens[one], (h + 1) * tokens[one])
            qa[one, group, rows, 0:128] = src[first : first + tokens[one], h * 128 : (h + 1) * 128]

    def prepare(first, last, passes):
        rows = lax.broadcasted_iota(jnp.int32, (128, 128), 0)
        lanes = lax.broadcasted_iota(jnp.int32, (128, 128), 1)
        for one in passes:
            eye = jnp.where(rows % tokens[one] + 64 * (one // 2) == lanes, 1.0, 0.0).astype(BF)
            for g in range(2 if one == 0 else 1):
                for i in range(4):
                    qa[one, g, i * 128 : (i + 1) * 128, 128:256] = eye
            m[one] = jnp.full((2, 8, 512), HIDDEN, F32)
            acc[one] = jnp.zeros((2, 144, 512), F32)

        def extra(i, carry):
            b["kx"][i, :, :, 128:256] = jnp.zeros((2, 768, 128), BF)
            b["vt"][i, :, 128:144, :] = jnp.ones((2, 16, 768), BF)
            return carry

        lax.fori_loop(first, last, extra, 0)

    first_key = doc[0]

    def tile_at(n, u):
        third = n // 8
        t = (third + 1) // 2
        other = third // 2
        one = t * (1 + (1 - other) * ((n % 8) // 4) + other * (n % 2))
        i = (1 - t + other) * ((n % 8) // 2) + (t - other) * (n % 4)
        plane = (yh + other) % 2
        at = (x + 3 * i + 3 * (i // 2) + 2 * (i // 3)) % 4
        from_core = (c + (1 - t) * (n % 2) + t * u) % 2
        return one, (1 - t) * u, t * (4 + plane * 4) + at, plane, at, from_core

    def build(n, u):
        one, g, block, plane, at, from_core = tile_at(n, u)
        base = (plane * 4 + at) * KEYS_CHIP + from_core * 768

        @pl.when((one <= 1) if u == 0 else (one == 1))
        def _():
            b["vt"][block, from_core, 0:128, :] = b["kv"][block, from_core, 1].T
            b["kx"][block, from_core, :, 0:128] = b["kv"][block, from_core, 0]

            @pl.when(plane == 0)
            def _():
                key = lax.broadcasted_iota(jnp.int32, (768, 128), 0)
                b["kx"][block, from_core, :, 128:256] = jnp.where(key >= first_key - base, 0.0, HIDDEN).astype(BF)

        @pl.when((one <= 1) & (plane == 1) & (at >= 2))
        def _():
            ahead = CACHE + ((((yh + g) % 2) * 4 + x) * 2 + c) * 128 - base
            key = lax.broadcasted_iota(jnp.int32, (768, 128), 0)
            row = lax.broadcasted_iota(jnp.int32, (768, 128), 1)
            b["kx"][block, from_core, :, 128:256] = jnp.where(key - row <= ahead, 0.0, HIDDEN).astype(BF)

    scores, tops = (b["score0"], b["score1"]), (b["top0"], b["top1"])

    def overlapped(n, u, weigh_n, weigh=True):
        one, g, block, _, _, from_core = tile_at(n, u)
        queries = qa[one, g]
        top = jnp.full((8, 512), HIDDEN, F32)
        if weigh:
            w_one, w_g, w_block, _, _, w_core = tile_at(weigh_n, 1 - u)
            old = m[w_one, w_g]
            peak = jnp.max(tops[1 - u][...], axis=0, keepdims=True)
            new = jnp.maximum(old, jnp.broadcast_to(peak, (8, 512)))
            total = (acc[w_one, w_g].reshape(18, 8, 512) * jnp.exp2((old - new) * SCALE)[None]).reshape(144, 512)
        for j in range(3):
            keys = slice(j * 256, (j + 1) * 256)
            fresh = dot(b["kx"][block, from_core, keys, :], queries, ((1,), (1,)))
            scores[u][keys, :] = fresh
            top = jnp.maximum(top, jnp.max(fresh.reshape(32, 8, 512), axis=0))
            if weigh:
                held = scores[1 - u][keys, :].reshape(32, 8, 512)
                weights = jnp.exp2((held - new[None]) * SCALE).reshape(256, 512).astype(BF)
                total = total + dot(b["vt"][w_block, w_core, :, keys], weights)
        tops[u][...] = top
        if weigh:
            m[w_one, w_g] = new
            acc[w_one, w_g] = total

    def attention(hooks):
        build(0, 0)
        overlapped(0, 0, 0, weigh=False)

        def step(n, carry):
            for at_step, hook in hooks.items():
                pl.when(n == at_step)(hook)
            build(n, 1)
            overlapped(n, 1, n)
            after = (n + 1) % 24
            build(after, 0)
            overlapped(after, 0, n)
            return carry

        lax.fori_loop(0, 24, step, 0)

    def part_of(one, g):
        total = acc[one, g, 128:136, :]
        mean = (acc[one, g, 0:128, :].reshape(16, 8, 512) * (1.0 / total)[None]).reshape(128, 512)
        return mean, m[one, g] * SCALE + jnp.log(total) * LOG2E

    def partner_part():
        for g in (1, 0):
            mean, logs = part_of(0, g)
            b["o_out"][g] = mean.astype(BF)
            b["l_out"][g] = logs
            give_o[1 - g].start()
            give_l[1 - g].start()

    def keep_context(one, plane, both, ctx):
        both = both.T.astype(BF)
        count, first = tokens[one], 64 * (one // 2)
        for h in range(heads[one]):
            held = both[h * count : (h + 1) * count, :]
            ctx[plane * 4 + x, c, first : first + count, h * 128 : (h + 1) * 128] = held

    def s_context(g):
        give_o[g].wait_recv()
        give_l[g].wait_recv()
        mine, log_mine = part_of(0, g)
        share = 1.0 / (1.0 + jnp.exp2(log_mine - b["l_in"][g]))
        other = b["o_in"][g].astype(F32)
        both = mine + ((other - mine).reshape(16, 8, 512) * share[None]).reshape(128, 512)
        keep_context(0, (yh + g) % 2, both, b["sctx"])
        g_s.root(g)

    def t_context(half):
        keep_context(1 + half, yh, part_of(1 + half, 0)[0], b["tctx"])
        g_t[half].root(0)

    class Reduce:
        def __init__(self, ctx, w, name, half):
            self.ctx, self.w, self.half = ctx, w, half

            def of(key):
                return b[name + key] if half is None else b[name + key].at[half]

            self.y_out, self.y_in, self.part, self.hid = of("y_out"), of("y_in"), b[name + "part"], of("hid")
            self.r_out, self.r_in, self.z_out, self.z_in = of("r_out"), of("r_in"), of("z_out"), of("z_in")
            self.rows = self.part.shape[2] // 2
            near = (tp_dev(0, 3), tp_dev(0, 1))
            self.relay = [
                wire.copy(self.r_out.at[:, pl.ds(i * self.rows, self.rows)], self.r_in.at[i], near[i]) for i in range(2)
            ]
            self.along = [wire.copy(self.z_out.at[i], self.z_in.at[i], near[i]) for i in range(2)]
            self.beside = wire.copy(self.y_out, self.y_in, tp_dev(1, 0))

        def multiply(self, first, last, waits):
            def pair(j, carry):
                for at, wait in waits.items():
                    pl.when(j == at)(wait)
                zd = ((yh + j // 2) % 2) * 2 + (x // 2 + j % 2) % 2

                both = pl.ds(zd * 2, 2)
                if self.half is None:
                    held = self.ctx[both]
                else:
                    held = self.ctx[both, :, self.half * 64 : self.half * 64 + 64]
                done = dot(held.reshape(-1, held.shape[3]), self.w[...])
                self.part[zd] = done.reshape(2, -1, done.shape[1])

                @pl.when(zd == (z + 2) % 4)
                def _():
                    self.r_out[...] = self.part[zd].astype(BF)
                    self.relay[0].start()
                    self.relay[1].start()

                return carry

            lax.fori_loop(first, last, pair, 0)

        def send_on(self):
            for i, zd in enumerate(((z + 3) % 4, (z + 1) % 4)):
                mid = slice(i * self.rows, (i + 1) * self.rows)
                rest = slice((1 - i) * self.rows, (2 - i) * self.rows)
                self.z_out[i, :, rest, :] = self.part[zd, :, rest, :].astype(BF)
                self.relay[i].wait_recv()
                self.z_out[i, :, mid, :] = (self.part[zd, :, mid, :] + self.r_in[i].astype(F32)).astype(BF)
                self.along[i].start()

        def settle(self):
            self.along[0].wait_recv()
            self.along[1].wait_recv()

            def block(u):
                return self.part[z, u] + self.z_in[0, u].astype(F32) + self.z_in[1, u].astype(F32)

            self.y_out[...] = block(1 - yl).astype(BF)
            self.beside.start()
            self.hid[...] = block(yl)

        def finish(self, resid):
            if self.half is None:
                own = resid[...]
            else:
                first = self.half * 64
                own = jnp.concatenate([resid[first : first + 64, :], resid[first + 128 : first + 192, :]], axis=0)
            total = self.hid[...] + own.astype(F32)
            self.beside.wait_recv()
            self.hid[...] = total + self.y_in[...].astype(F32)

    def send_squares(hid, sq, copies):
        value = hid[...]
        ones = jnp.ones((8, value.shape[1]), F32)
        sq[s] = dot(ones, value * value, ((1,), (1,)), lax.Precision.HIGHEST)
        for made in copies:
            made.start()

    def inverse_scale(sq, copies, width):
        for made in copies:
            made.wait_recv()
        total = sq[0]
        for i in range(1, 16):
            total = total + sq[i]
        first = jnp.where(lax.broadcasted_iota(jnp.int32, (8, 128), 0) == 0, 1.0, 0.0)
        column = dot(total, first, ((0,), (0,)), lax.Precision.HIGHEST)
        return 1.0 / jnp.sqrt(column * (1.0 / width) + 1e-05)

    r_s = Reduce(b["sctx"], b["sw"], "s", None)
    r_t = [Reduce(b["tctx"], b["tw"], "t", half) for half in range(2)]

    def ready(gather, plane):
        gather.have_own(plane)
        gather.have_near(plane)
        gather.have_far(plane)

    fill_queries(0, sq, 0)
    prepare(0, 4, (0,))
    loads[0].wait()
    loads[1].wait()
    pl.semaphore_wait(barrier, 22)
    g_skv.root(0)
    give_sq.start()
    g_tkv.cross.start()

    def s_partner():
        g_skv.have_own(0)
        give_sq.wait_recv()
        fill_queries(0, b["sq_in"], 1)

    def s_near():
        prepare(4, 12, (1, 2))
        fill_queries(1, tq, 0)
        fill_queries(2, tq, 0)
        g_skv.mid(0)
        g_tkv.root(0, False)

    def t_start():
        partner_part()
        g_tkv.have_own(0)
        g_tkv.mid(0)
        g_tkv.root(1)

    def s_sums():
        for load in loads[2:]:
            load.wait()
        r_s.multiply(0, 4, {0: lambda: ready(g_s, 0), 2: lambda: ready(g_s, 1)})

    def s_squares():
        r_s.finish(sres)
        send_squares(b["shid"], b["ssq"], s_sq)

    def s_normed():
        inverse = inverse_scale(b["ssq"], s_sq, D_S)
        inverse = jnp.concatenate([inverse, inverse], axis=1)
        normed = (b["shid"][...] * inverse * sg[...]).astype(BF)
        for at, first in enumerate((0, 128, 64, 192)):
            b["nb"][s, at * 64 : (at + 1) * 64, :] = normed[first : first + 64, :]
        g_n.root(0)

    def t1_sums():
        r_t[0].multiply(0, 4, {0: lambda: ready(g_t[0], 0), 2: lambda: ready(g_t[0], 1)})

    def both(*hooks):
        def run():
            for hook in hooks:
                hook()

        return run

    attention(
        {
            0: s_partner,
            1: s_near,
            2: lambda: g_skv.have_left(0),
            4: lambda: g_skv.have_right(0),
            5: lambda: g_skv.far(0),
            6: lambda: g_skv.have_far(0),
            8: t_start,
            9: lambda: g_tkv.have_left(0),
            10: both(lambda: g_tkv.have_right(0), lambda: g_tkv.far(0)),
            11: lambda: g_tkv.have_far(0),
            12: lambda: s_context(0),
            16: both(lambda: g_tkv.have_own(1), lambda: s_context(1)),
            17: lambda: g_tkv.mid(1),
            18: both(lambda: g_tkv.have_left(1), lambda: g_s.mid(0)),
            20: both(lambda: g_tkv.have_right(1), lambda: g_s.mid(1), lambda: g_s.far(0)),
            21: lambda: g_tkv.far(1),
            22: both(lambda: g_tkv.have_far(1), lambda: g_s.far(1)),
            23: both(lambda: t_context(0), s_sums),
        }
    )
    for load in map_loads:
        load.start()
    t_context(1)
    r_s.send_on()
    g_t[0].mid(0)
    g_t[0].root(1)
    g_t[1].mid(0)
    g_t[1].root(1)
    g_t[0].far(0)
    g_t[0].mid(1)
    r_s.settle()
    wire.close(0, keys_sent)
    g_t[0].far(1)
    t1_sums()
    s_squares()
    g_t[1].far(0)
    g_t[1].mid(1)
    r_t[0].send_on()
    s_normed()
    g_t[1].far(1)
    r_t[0].settle()
    g_n.mid(0)
    g_n.root(1)
    r_t[1].multiply(0, 4, {0: lambda: ready(g_t[1], 0), 2: lambda: ready(g_t[1], 1)})
    r_t[0].finish(tres)
    send_squares(b["thid"].at[0], b["tsq"].at[0], t_sq[0])
    g_n.far(0)
    g_n.mid(1)
    r_t[1].send_on()
    wire.close(keys_sent, contexts_sent)
    g_n.far(1)
    for made in n_tp:
        made.start()
    ready(g_n, 0)
    ready(g_n, 1)
    b["diff"][...] = jnp.zeros((2, 128, 512), F32)
    for load in map_loads:
        load.wait()

    def match(k, carry):
        lhs = jnp.concatenate([b["nb"][2 * k], b["nb"][2 * k + 1]], axis=1)
        for u in range(2):
            b["diff"][:, :, u * 256 : (u + 1) * 256] += dot(lhs, b["kx"][k, u, 0:512, :]).reshape(2, 128, 256)
        return carry

    lax.fori_loop(0, 8, match, 0)

    def delta(half):
        inverse = inverse_scale(b["tsq"].at[half], t_sq[half], D_T)
        inverse = jnp.concatenate([inverse, inverse, inverse, inverse], axis=1)
        target = b["thid"][half] * inverse * tg[...]
        b["dl"][half, p] = ((b["diff"][half] - target) * (1.0 / math.sqrt(SLAB))).astype(BF)
        g_d[half].root(0)

    def gradient(half, plane, offs):
        def one(i, carry):
            q = ((z + offs[0] + i * offs[1]) % 4) * 2 + (yl + plane) % 2
            for at in range(2):
                rows = slice(at * 256, (at + 1) * 256)
                lhs = b["ng"][q, at, half * 128 : (half + 1) * 128, :]
                out[rows, :] += dot(lhs, b["dl"][half, q], ((0,), (0,)))
            return carry

        lax.fori_loop(0, offs[2], one, 0)

    own, near, far = (0, 1, 1), (1, 2, 2), (2, 1, 1)
    r_t[1].settle()
    delta(0)
    r_t[1].finish(tres)
    send_squares(b["thid"].at[1], b["tsq"].at[1], t_sq[1])
    b["ng"][p, 0] = b["nb"][2 * p]
    b["ng"][p, 1] = b["nb"][2 * p + 1]
    out[...] = jnp.zeros((512, 512), F32)
    g_d[0].mid(0)
    g_d[0].root(1)
    delta(1)
    for made, onward in zip(n_tp, n_x):
        made.wait_recv()
        onward.start()
    for made, onward in zip(n_x, n_core):
        made.wait_recv()
        onward.start()
    g_d[0].far(0)
    g_d[0].mid(1)
    for made in n_core:
        made.wait_recv()
    gradient(0, 0, own)
    gradient(0, 0, near)
    gradient(0, 0, far)
    gradient(0, 1, own)
    g_d[1].mid(0)
    g_d[1].root(1)
    gradient(0, 1, near)
    g_d[0].far(1)
    gradient(0, 1, far)
    gradient(1, 0, own)
    gradient(1, 0, near)
    gradient(1, 1, own)
    g_d[1].far(0)
    g_d[1].mid(1)
    gradient(1, 0, far)
    gradient(1, 1, near)
    g_d[1].far(1)
    gradient(1, 1, far)
    wire.close()


def per_device(tq, tkv, sq, skv, doc, tres, tw, tg, sres, sw, sg, mp):
    V = pl.BlockSpec(memory_space=pltpu.VMEM)
    A = pl.BlockSpec(memory_space=pl.ANY)
    S = pl.BlockSpec(memory_space=pltpu.SMEM)
    return pl.pallas_call(
        kernel,
        out_shape=jax.ShapeDtypeStruct((512, 512), F32),
        in_specs=[S, V, A, V, A, V, A, V, V, A, V, A],
        out_specs=V,
        scratch_shapes=list(scratch_plan().values()),
        compiler_params=pltpu.CompilerParams(
            collective_id=0, has_side_effects=True, vmem_limit_bytes=63 * 1024 * 1024
        ),
    )(
        doc, tq, tkv, sq, skv, tres, tw, tg.reshape(1, -1), sres, sw, sg.reshape(1, -1), mp.reshape(8, 512, 512)
    )


def solution(mesh):
    in_specs = (
        P("seq", "tp"),
        P(None, "seq", "tp"),
        P("seq", "tp"),
        P(None, "seq", "tp"),
        P(),
        P("tp", "seq"),
        P("tp", "seq"),
        P("seq"),
        P("tp", "seq"),
        P("tp", "seq"),
        P("seq"),
        P(None, "seq"),
    )
    out_specs = P("tp", "seq")
    return jax.shard_map(per_device, mesh=mesh, in_specs=in_specs, out_specs=out_specs, check_vma=False)
```

```python
import math

import jax
import jax.numpy as jnp
from jax import lax
from jax.experimental import pallas as pl
from jax.experimental.pallas import tpu as pltpu
from jax.sharding import PartitionSpec as P

D_T = 8192
D_S = 4096
HEAD = 128
SLAB = 2048
CACHE = 10240
KEYS_CHIP = 1536
HIDDEN = -1e30
LOG2E = math.log2(math.e)
SCALE = LOG2E / math.sqrt(HEAD)
MESH = pl.DeviceIdType.MESH
BF = jnp.bfloat16
F32 = jnp.float32


class Wire:
    def __init__(self, send, recv):
        self.send, self.recv, self.made, self.left = send, recv, [], set()

    def copy(self, src, dst, dev):
        i = len(self.made)
        made = pltpu.make_async_remote_copy(
            src_ref=src, dst_ref=dst, send_sem=self.send.at[i], recv_sem=self.recv.at[i],
            device_id=dev, device_id_type=MESH,
        )
        self.made.append(made)
        return made

    def close(self, first=0, last=None):
        for i in range(first, len(self.made) if last is None else last):
            if i not in self.left:
                self.left.add(i)
                self.made[i].wait_send()


class Gather:
    def __init__(self, wire, block, right, left, across=None, core=None, planes=None):
        self.planes = planes or (1 if across is None else 2)
        self.core = core is not None
        self.cross = wire.copy(block(0, 0, None), block(0, 0, None), across) if across is not None else None
        self.right, self.left, self.on_right, self.on_left, self.pass_on = [], [], [], [], []
        for plane in range(self.planes):
            own = block(plane, 0, None)
            self.right.append(wire.copy(own, own, right))
            self.left.append(wire.copy(own, own, left))
            first, second = block(plane, 3, 0), block(plane, 1, 1)
            self.on_right.append(wire.copy(first, first, right))
            self.on_left.append(wire.copy(second, second, left))
            if self.core:
                refs = [own, block(plane, 3, None), block(plane, 1, None), block(plane, 2, 0), block(plane, 2, 1)]
                self.pass_on.append([wire.copy(ref, ref, core) for ref in refs])

    def root(self, plane, start_cross=True):
        if plane == 1 and self.cross is not None:
            self.cross.wait_recv()
        self.right[plane].start()
        self.left[plane].start()
        if plane == 0 and self.cross is not None and start_cross:
            self.cross.start()
        if self.core:
            self.pass_on[plane][0].start()

    def mid(self, plane):
        self.right[plane].wait_recv()
        self.on_right[plane].start()
        if self.core:
            self.pass_on[plane][1].start()
        self.left[plane].wait_recv()
        self.on_left[plane].start()
        if self.core:
            self.pass_on[plane][2].start()

    def far(self, plane):
        self.on_right[plane].wait_recv()
        if self.core:
            self.pass_on[plane][3].start()
        self.on_left[plane].wait_recv()
        if self.core:
            self.pass_on[plane][4].start()

    def have_own(self, plane):
        self.pass_on[plane][0].wait_recv()

    def have_left(self, plane):
        self.pass_on[plane][1].wait_recv()

    def have_right(self, plane):
        self.pass_on[plane][2].wait_recv()

    def have_near(self, plane):
        self.have_left(plane)
        self.have_right(plane)

    def have_far(self, plane):
        self.pass_on[plane][3].wait_recv()
        self.pass_on[plane][4].wait_recv()


def dot(a, b, dims=((1,), (0,)), precision=None):
    return lax.dot_general(a, b, (dims, ((), ())), precision=precision, preferred_element_type=F32)


def scratch_plan():
    V = pltpu.VMEM
    D = pltpu.SemaphoreType.DMA
    return dict(
        kv=V((12, 2, 2, 768, 128), BF),
        kx=V((12, 2, 768, 256), BF),
        vt=V((12, 2, 144, 768), BF),
        score0=V((768, 512), F32),
        score1=V((768, 512), F32),
        top0=V((8, 512), F32),
        top1=V((8, 512), F32),
        qa=V((3, 2, 512, 256), BF),
        sq_in=V((128, 512), BF),
        m=V((3, 2, 8, 512), F32),
        acc=V((3, 2, 144, 512), F32),
        o_out=V((2, 128, 512), BF),
        o_in=V((2, 128, 512), BF),
        l_out=V((2, 8, 512), F32),
        l_in=V((2, 8, 512), F32),
        tctx=V((8, 2, 128, 1024), BF),
        sctx=V((8, 2, 128, 512), BF),
        tw=V((1024, 512), BF),
        sw=V((512, 256), BF),
        ty_out=V((2, 128, 512), BF),
        ty_in=V((2, 128, 512), BF),
        sy_out=V((256, 256), BF),
        sy_in=V((256, 256), BF),
        tpart=V((2, 4, 2, 128, 512), F32),
        spart=V((4, 2, 256, 256), F32),
        tr_out=V((2, 2, 128, 512), BF),
        tr_in=V((2, 2, 2, 64, 512), BF),
        sr_out=V((2, 256, 256), BF),
        sr_in=V((2, 2, 128, 256), BF),
        tz_out=V((2, 2, 2, 128, 512), BF),
        tz_in=V((2, 2, 2, 128, 512), BF),
        sz_out=V((2, 2, 256, 256), BF),
        sz_in=V((2, 2, 256, 256), BF),
        thid=V((2, 128, 512), F32),
        shid=V((256, 256), F32),
        tsq=V((2, 16, 8, 128), F32),
        ssq=V((16, 8, 256), F32),
        nb=V((16, 256, 256), BF),
        ng=V((8, 2, 256, 256), BF),
        dl=V((2, 8, 128, 512), BF),
        diff=V((2, 128, 512), F32),
        wsend=D((200,)),
        wrecv=D((200,)),
        loc=D((8,)),
    )


def kernel(doc, tq, tkv_h, sq, skv_h, tres, tw_h, tg, sres, sw_h, sg, mp_h, out, *scratch):
    b = dict(zip(scratch_plan(), scratch))
    s = lax.axis_index("seq")
    p = lax.axis_index("tp")
    yh, x, c = s // 8, (s // 2) % 4, s % 2
    z, yl = p // 2, p % 2
    k_own = yh * 4 + x

    def seq_dev(plane, off, other):
        return ((((yh + plane) % 2) * 4 + (x + off) % 4) * 2 + (c + other) % 2, p)

    def tp_dev(plane, off):
        return (s, ((z + off) % 4) * 2 + (yl + plane) % 2)

    right, left, across, core = seq_dev(0, 1, 0), seq_dev(0, 3, 0), seq_dev(1, 0, 0), seq_dev(0, 0, 1)

    loads = [
        pltpu.make_async_copy(skv_h, b["kv"].at[x, c], b["loc"].at[0]),
        pltpu.make_async_copy(tkv_h, b["kv"].at[4 + k_own, c], b["loc"].at[1]),
        pltpu.make_async_copy(sw_h, b["sw"], b["loc"].at[2]),
        pltpu.make_async_copy(tw_h, b["tw"], b["loc"].at[3]),
    ]
    for load in loads:
        load.start()
    map_loads = [
        pltpu.make_async_copy(
            mp_h.at[:, :, pl.ds(u * 256, 256)], b["kx"].at[pl.ds(0, 8), u, pl.ds(0, 512)], b["loc"].at[4 + u]
        )
        for u in range(2)
    ]

    barrier = pltpu.get_barrier_semaphore()
    for off in range(1, 16):
        pl.semaphore_signal(barrier, inc=1, device_id=((s + off) % 16, p), device_id_type=MESH)
    for off in range(1, 8):
        pl.semaphore_signal(barrier, inc=1, device_id=(s, (p + off) % 8), device_id_type=MESH)

    wire = Wire(b["wsend"], b["wrecv"])
    give_sq = wire.copy(sq, b["sq_in"], across)

    def kv_block(model):
        def block(plane, off, part):
            at = (x + off) % 4 + model * (4 + ((yh + plane) % 2) * 4)
            if part is None:
                return b["kv"].at[at, c]
            return b["kv"].at[at, c, part]

        return block

    def s_block(plane, off, part):
        at = ((yh + plane) % 2) * 4 + (x + off) % 4
        if part is None:
            return b["sctx"].at[at, c]
        return b["sctx"].at[at, c, pl.ds(part * 64, 64)]

    def t_block(half):
        def block(plane, off, part):
            at = ((yh + plane) % 2) * 4 + (x + off) % 4
            if part is None:
                return b["tctx"].at[at, c, pl.ds(half * 64, 64)]
            return b["tctx"].at[at, c, pl.ds(half * 64 + part * 32, 32)]

        return block

    def nb_block(plane, off, part):
        at = (((yh + plane) % 2) * 4 + (x + off) % 4) * 2 + c
        if part is None:
            return b["nb"].at[at]
        return b["nb"].at[at, pl.ds(part * 128, 128)]

    def dl_block(half):
        def block(plane, off, part):
            at = ((z + off) % 4) * 2 + (yl + plane) % 2
            if part is None:
                return b["dl"].at[half, at]
            return b["dl"].at[half, at, pl.ds(part * 64, 64)]

        return block

    g_skv = Gather(wire, kv_block(0), right, left, None, core)
    g_tkv = Gather(wire, kv_block(1), right, left, across, core)
    keys_sent = len(wire.made)
    g_s = Gather(wire, s_block, right, left, None, core, 2)
    g_t = [Gather(wire, t_block(half), right, left, across, core) for half in range(2)]
    contexts_sent = len(wire.made)
    g_n = Gather(wire, nb_block, right, left, across, core)
    g_d = [Gather(wire, dl_block(half), tp_dev(0, 1), tp_dev(0, 3), tp_dev(1, 0), None) for half in range(2)]
    give_o = [wire.copy(b["o_out"].at[1 - g], b["o_in"].at[g], across) for g in range(2)]
    give_l = [wire.copy(b["l_out"].at[1 - g], b["l_in"].at[g], across) for g in range(2)]
    s_sq = [wire.copy(b["ssq"].at[s], b["ssq"].at[s], ((s + off) % 16, p)) for off in range(1, 16)]
    t_sq = [
        [wire.copy(b["tsq"].at[half, s], b["tsq"].at[half, s], ((s + off) % 16, p)) for off in range(1, 16)]
        for half in range(2)
    ]
    n_tp = [
        wire.copy(b["nb"].at[((p + off) % 8) * 2 + c], b["ng"].at[p, c], (s, (p + off) % 8)) for off in range(1, 8)
    ]
    n_core = [
        wire.copy(b["ng"].at[(p + 8 - off) % 8, c], b["ng"].at[(p + 8 - off) % 8, c], core) for off in range(1, 8)
    ]

    qa, m, acc = b["qa"], b["m"], b["acc"]
    heads, tokens = (4, 8, 8), (128, 64, 64)

    def fill_queries(one, src, group):
        first = 64 * (one // 2)
        for h in range(heads[one]):
            rows = slice(h * tokens[one], (h + 1) * tokens[one])
            qa[one, group, rows, 0:128] = src[first : first + tokens[one], h * 128 : (h + 1) * 128]

    def prepare(first, last, passes):
        rows = lax.broadcasted_iota(jnp.int32, (128, 128), 0)
        lanes = lax.broadcasted_iota(jnp.int32, (128, 128), 1)
        for one in passes:
            eye = jnp.where(rows % tokens[one] + 64 * (one // 2) == lanes, 1.0, 0.0).astype(BF)
            for g in range(2 if one == 0 else 1):
                for i in range(4):
                    qa[one, g, i * 128 : (i + 1) * 128, 128:256] = eye
            m[one] = jnp.full((2, 8, 512), HIDDEN, F32)
            acc[one] = jnp.zeros((2, 144, 512), F32)

        def extra(i, carry):
            b["kx"][i, :, :, 128:256] = jnp.zeros((2, 768, 128), BF)
            b["vt"][i, :, 128:144, :] = jnp.ones((2, 16, 768), BF)
            return carry

        lax.fori_loop(first, last, extra, 0)

    first_key = doc[0]

    def tile_at(n, u):
        third = n // 8
        t = (third + 1) // 2
        other = third // 2
        one = t * (1 + (1 - other) * ((n % 8) // 4) + other * (n % 2))
        i = (1 - t + other) * ((n % 8) // 2) + (t - other) * (n % 4)
        plane = (yh + other) % 2
        at = (x + 3 * i + 3 * (i // 2) + 2 * (i // 3)) % 4
        from_core = (c + (1 - t) * (n % 2) + t * u) % 2
        return one, (1 - t) * u, t * (4 + plane * 4) + at, plane, at, from_core

    def build(n, u):
        one, g, block, plane, at, from_core = tile_at(n, u)
        base = (plane * 4 + at) * KEYS_CHIP + from_core * 768

        @pl.when((one <= 1) if u == 0 else (one == 1))
        def _():
            b["vt"][block, from_core, 0:128, :] = b["kv"][block, from_core, 1].T
            b["kx"][block, from_core, :, 0:128] = b["kv"][block, from_core, 0]

            @pl.when(plane == 0)
            def _():
                key = lax.broadcasted_iota(jnp.int32, (768, 128), 0)
                b["kx"][block, from_core, :, 128:256] = jnp.where(key >= first_key - base, 0.0, HIDDEN).astype(BF)

        @pl.when((one <= 1) & (plane == 1) & (at >= 2))
        def _():
            ahead = CACHE + ((((yh + g) % 2) * 4 + x) * 2 + c) * 128 - base
            key = lax.broadcasted_iota(jnp.int32, (768, 128), 0)
            row = lax.broadcasted_iota(jnp.int32, (768, 128), 1)
            b["kx"][block, from_core, :, 128:256] = jnp.where(key - row <= ahead, 0.0, HIDDEN).astype(BF)

    scores, tops = (b["score0"], b["score1"]), (b["top0"], b["top1"])

    def overlapped(n, u, weigh_n, weigh=True):
        one, g, block, _, _, from_core = tile_at(n, u)
        queries = qa[one, g]
        top = jnp.full((8, 512), HIDDEN, F32)
        if weigh:
            w_one, w_g, w_block, _, _, w_core = tile_at(weigh_n, 1 - u)
            old = m[w_one, w_g]
            peak = jnp.max(tops[1 - u][...], axis=0, keepdims=True)
            new = jnp.maximum(old, jnp.broadcast_to(peak, (8, 512)))
            total = (acc[w_one, w_g].reshape(18, 8, 512) * jnp.exp2((old - new) * SCALE)[None]).reshape(144, 512)
        for j in range(3):
            keys = slice(j * 256, (j + 1) * 256)
            fresh = dot(b["kx"][block, from_core, keys, :], queries, ((1,), (1,)))
            scores[u][keys, :] = fresh
            top = jnp.maximum(top, jnp.max(fresh.reshape(32, 8, 512), axis=0))
            if weigh:
                held = scores[1 - u][keys, :].reshape(32, 8, 512)
                weights = jnp.exp2((held - new[None]) * SCALE).reshape(256, 512).astype(BF)
                total = total + dot(b["vt"][w_block, w_core, :, keys], weights)
        tops[u][...] = top
        if weigh:
            m[w_one, w_g] = new
            acc[w_one, w_g] = total

    def attention(hooks):
        build(0, 0)
        overlapped(0, 0, 0, weigh=False)

        def step(n, carry):
            for at_step, hook in hooks.items():
                pl.when(n == at_step)(hook)
            build(n, 1)
            overlapped(n, 1, n)
            after = (n + 1) % 24
            build(after, 0)
            overlapped(after, 0, n)
            return carry

        lax.fori_loop(0, 24, step, 0)

    def part_of(one, g):
        total = acc[one, g, 128:136, :]
        mean = (acc[one, g, 0:128, :].reshape(16, 8, 512) * (1.0 / total)[None]).reshape(128, 512)
        return mean, m[one, g] * SCALE + jnp.log(total) * LOG2E

    def partner_part():
        for g in (1, 0):
            mean, logs = part_of(0, g)
            b["o_out"][g] = mean.astype(BF)
            b["l_out"][g] = logs
            give_o[1 - g].start()
            give_l[1 - g].start()

    def keep_context(one, plane, both, ctx):
        both = both.T.astype(BF)
        count, first = tokens[one], 64 * (one // 2)
        for h in range(heads[one]):
            held = both[h * count : (h + 1) * count, :]
            ctx[plane * 4 + x, c, first : first + count, h * 128 : (h + 1) * 128] = held

    def s_context(g):
        give_o[g].wait_recv()
        give_l[g].wait_recv()
        mine, log_mine = part_of(0, g)
        share = 1.0 / (1.0 + jnp.exp2(log_mine - b["l_in"][g]))
        other = b["o_in"][g].astype(F32)
        both = mine + ((other - mine).reshape(16, 8, 512) * share[None]).reshape(128, 512)
        keep_context(0, (yh + g) % 2, both, b["sctx"])
        g_s.root(g)

    def t_context(half):
        keep_context(1 + half, yh, part_of(1 + half, 0)[0], b["tctx"])
        g_t[half].root(0)

    class Reduce:
        def __init__(self, ctx, w, name, half):
            self.ctx, self.w, self.half = ctx, w, half

            def of(key):
                return b[name + key] if half is None else b[name + key].at[half]

            self.y_out, self.y_in, self.part, self.hid = of("y_out"), of("y_in"), of("part"), of("hid")
            self.r_out, self.r_in, self.z_out, self.z_in = of("r_out"), of("r_in"), of("z_out"), of("z_in")
            self.rows = self.part.shape[2] // 2
            near = (tp_dev(0, 3), tp_dev(0, 1))
            self.relay = [
                wire.copy(self.r_out.at[:, pl.ds(i * self.rows, self.rows)], self.r_in.at[i], near[i]) for i in range(2)
            ]
            self.along = [wire.copy(self.z_out.at[i], self.z_in.at[i], near[i]) for i in range(2)]
            self.beside = wire.copy(self.y_out, self.y_in, tp_dev(1, 0))

        def multiply(self, first, last, waits):
            def pair(j, carry):
                for at, wait in waits.items():
                    pl.when(j == at)(wait)
                zd = ((yh + j // 2) % 2) * 2 + (x // 2 + j % 2) % 2

                both = pl.ds(zd * 2, 2)
                if self.half is None:
                    held = self.ctx[both]
                else:
                    held = self.ctx[both, :, self.half * 64 : self.half * 64 + 64]
                done = dot(held.reshape(-1, held.shape[3]), self.w[...])
                self.part[zd] = done.reshape(2, -1, done.shape[1])

                @pl.when(zd == (z + 2) % 4)
                def _():
                    self.r_out[...] = self.part[zd].astype(BF)
                    self.relay[0].start()
                    self.relay[1].start()

                return carry

            lax.fori_loop(first, last, pair, 0)

        def send_on(self):
            for i, zd in enumerate(((z + 3) % 4, (z + 1) % 4)):
                mid = slice(i * self.rows, (i + 1) * self.rows)
                rest = slice((1 - i) * self.rows, (2 - i) * self.rows)
                self.z_out[i, :, rest, :] = self.part[zd, :, rest, :].astype(BF)
                self.relay[i].wait_recv()
                self.z_out[i, :, mid, :] = (self.part[zd, :, mid, :] + self.r_in[i].astype(F32)).astype(BF)
                self.along[i].start()

        def settle(self):
            self.along[0].wait_recv()
            self.along[1].wait_recv()

            def block(u):
                return self.part[z, u] + self.z_in[0, u].astype(F32) + self.z_in[1, u].astype(F32)

            self.y_out[...] = block(1 - yl).astype(BF)
            self.beside.start()
            self.hid[...] = block(yl)

        def finish(self, resid):
            if self.half is None:
                own = resid[...]
            else:
                first = self.half * 64
                own = jnp.concatenate([resid[first : first + 64, :], resid[first + 128 : first + 192, :]], axis=0)
            total = self.hid[...] + own.astype(F32)
            self.beside.wait_recv()
            self.hid[...] = total + self.y_in[...].astype(F32)

    def send_squares(hid, sq, copies):
        value = hid[...]
        ones = jnp.ones((8, value.shape[1]), F32)
        sq[s] = dot(ones, value * value, ((1,), (1,)), lax.Precision.HIGHEST)
        for made in copies:
            made.start()

    def inverse_scale(sq, copies, width):
        for made in copies:
            made.wait_recv()
        total = sq[0]
        for i in range(1, 16):
            total = total + sq[i]
        first = jnp.where(lax.broadcasted_iota(jnp.int32, (8, 128), 0) == 0, 1.0, 0.0)
        column = dot(total, first, ((0,), (0,)), lax.Precision.HIGHEST)
        return 1.0 / jnp.sqrt(column * (1.0 / width) + 1e-05)

    r_s = Reduce(b["sctx"], b["sw"], "s", None)
    r_t = [Reduce(b["tctx"], b["tw"], "t", half) for half in range(2)]

    def ready(gather, plane):
        gather.have_own(plane)
        gather.have_near(plane)
        gather.have_far(plane)

    fill_queries(0, sq, 0)
    prepare(0, 4, (0,))
    loads[0].wait()
    loads[1].wait()
    pl.semaphore_wait(barrier, 22)
    g_skv.root(0)
    give_sq.start()
    g_tkv.cross.start()

    def s_partner():
        g_skv.have_own(0)
        give_sq.wait_recv()
        fill_queries(0, b["sq_in"], 1)

    def s_near():
        prepare(4, 12, (1, 2))
        fill_queries(1, tq, 0)
        fill_queries(2, tq, 0)
        g_skv.mid(0)
        g_tkv.root(0, False)

    def t_start():
        partner_part()
        g_tkv.have_own(0)
        g_tkv.mid(0)
        g_tkv.root(1)

    def s_sums():
        for load in loads[2:]:
            load.wait()
        r_s.multiply(0, 4, {0: lambda: ready(g_s, 0), 2: lambda: ready(g_s, 1)})

    def s_squares():
        r_s.finish(sres)
        send_squares(b["shid"], b["ssq"], s_sq)

    def s_normed():
        inverse = inverse_scale(b["ssq"], s_sq, D_S)
        inverse = jnp.concatenate([inverse, inverse], axis=1)
        normed = (b["shid"][...] * inverse * sg[...]).astype(BF)
        for at, first in enumerate((0, 128, 64, 192)):
            b["nb"][s, at * 64 : (at + 1) * 64, :] = normed[first : first + 64, :]
        g_n.root(0)

    def t1_sums():
        r_t[0].multiply(0, 4, {0: lambda: ready(g_t[0], 0), 2: lambda: ready(g_t[0], 1)})

    def both(*hooks):
        def run():
            for hook in hooks:
                hook()

        return run

    attention(
        {
            0: s_partner,
            1: s_near,
            2: lambda: g_skv.have_left(0),
            4: lambda: g_skv.have_right(0),
            5: lambda: g_skv.far(0),
            6: lambda: g_skv.have_far(0),
            8: t_start,
            9: lambda: g_tkv.have_left(0),
            10: both(lambda: g_tkv.have_right(0), lambda: g_tkv.far(0)),
            11: lambda: g_tkv.have_far(0),
            12: lambda: s_context(0),
            15: lambda: s_context(1),
            16: lambda: g_tkv.have_own(1),
            17: both(lambda: g_tkv.mid(1), lambda: g_s.mid(0)),
            18: lambda: g_tkv.have_left(1),
            19: both(lambda: g_s.mid(1), lambda: g_s.far(0)),
            20: lambda: g_tkv.have_right(1),
            21: both(lambda: g_tkv.far(1), lambda: g_s.far(1)),
            22: both(lambda: g_tkv.have_far(1), s_sums),
            23: lambda: t_context(0),
        }
    )
    for load in map_loads:
        load.start()
    t_context(1)
    r_s.send_on()
    g_t[0].mid(0)
    g_t[0].root(1)
    g_t[1].mid(0)
    g_t[1].root(1)
    wire.close(0, keys_sent)
    g_t[0].far(0)
    g_t[0].mid(1)
    r_s.settle()
    g_t[0].far(1)
    t1_sums()
    g_t[1].far(0)
    g_t[1].mid(1)
    s_squares()
    g_t[1].far(1)
    r_t[0].send_on()
    r_t[1].multiply(0, 4, {0: lambda: ready(g_t[1], 0), 2: lambda: ready(g_t[1], 1)})
    s_normed()
    r_t[1].send_on()
    r_t[0].settle()
    g_n.mid(0)
    g_n.root(1)
    r_t[0].finish(tres)
    send_squares(b["thid"].at[0], b["tsq"].at[0], t_sq[0])
    g_n.far(0)
    g_n.mid(1)
    r_t[1].settle()
    g_n.far(1)
    for made in n_tp:
        made.start()
    r_t[1].finish(tres)
    send_squares(b["thid"].at[1], b["tsq"].at[1], t_sq[1])
    wire.close(keys_sent, contexts_sent)
    ready(g_n, 0)
    ready(g_n, 1)
    b["diff"][...] = jnp.zeros((2, 128, 512), F32)
    for load in map_loads:
        load.wait()

    def match(k, carry):
        lhs = jnp.concatenate([b["nb"][2 * k], b["nb"][2 * k + 1]], axis=1)
        for u in range(2):
            b["diff"][:, :, u * 256 : (u + 1) * 256] += dot(lhs, b["kx"][k, u, 0:512, :]).reshape(2, 128, 256)
        return carry

    lax.fori_loop(0, 8, match, 0)

    def delta(half):
        inverse = inverse_scale(b["tsq"].at[half], t_sq[half], D_T)
        inverse = jnp.concatenate([inverse, inverse, inverse, inverse], axis=1)
        target = b["thid"][half] * inverse * tg[...]
        b["dl"][half, p] = ((b["diff"][half] - target) * (1.0 / math.sqrt(SLAB))).astype(BF)
        g_d[half].root(0)

    def gradient(half, plane, offs):
        def one(i, carry):
            q = ((z + offs[0] + i * offs[1]) % 4) * 2 + (yl + plane) % 2
            for at in range(2):
                rows = slice(at * 256, (at + 1) * 256)
                lhs = b["ng"][q, at, half * 128 : (half + 1) * 128, :]
                out[rows, :] += dot(lhs, b["dl"][half, q], ((0,), (0,)))
            return carry

        lax.fori_loop(0, offs[2], one, 0)

    own, near, far = (0, 1, 1), (1, 2, 2), (2, 1, 1)
    delta(0)
    delta(1)
    b["ng"][p, 0] = b["nb"][2 * p]
    b["ng"][p, 1] = b["nb"][2 * p + 1]
    out[...] = jnp.zeros((512, 512), F32)
    g_d[0].mid(0)
    g_d[0].root(1)
    for made, onward in zip(n_tp, n_core):
        made.wait_recv()
        onward.start()
    g_d[0].far(0)
    g_d[0].mid(1)
    for made in n_core:
        made.wait_recv()
    gradient(0, 0, own)
    gradient(0, 0, near)
    gradient(0, 0, far)
    gradient(0, 1, own)
    g_d[1].mid(0)
    g_d[1].root(1)
    gradient(0, 1, near)
    g_d[0].far(1)
    gradient(0, 1, far)
    gradient(1, 0, own)
    gradient(1, 0, near)
    gradient(1, 1, own)
    g_d[1].far(0)
    g_d[1].mid(1)
    gradient(1, 0, far)
    gradient(1, 1, near)
    g_d[1].far(1)
    gradient(1, 1, far)
    wire.close()


def per_device(tq, tkv, sq, skv, doc, tres, tw, tg, sres, sw, sg, mp):
    V = pl.BlockSpec(memory_space=pltpu.VMEM)
    A = pl.BlockSpec(memory_space=pl.ANY)
    S = pl.BlockSpec(memory_space=pltpu.SMEM)
    return pl.pallas_call(
        kernel,
        out_shape=jax.ShapeDtypeStruct((512, 512), F32),
        in_specs=[S, V, A, V, A, V, A, V, V, A, V, A],
        out_specs=V,
        scratch_shapes=list(scratch_plan().values()),
        compiler_params=pltpu.CompilerParams(
            collective_id=0, has_side_effects=True, vmem_limit_bytes=63 * 1024 * 1024
        ),
    )(
        doc, tq, tkv, sq, skv, tres, tw, tg.reshape(1, -1), sres, sw, sg.reshape(1, -1), mp.reshape(8, 512, 512)
    )


def solution(mesh):
    in_specs = (
        P("seq", "tp"),
        P(None, "seq", "tp"),
        P("seq", "tp"),
        P(None, "seq", "tp"),
        P(),
        P("tp", "seq"),
        P("tp", "seq"),
        P("seq"),
        P("tp", "seq"),
        P("tp", "seq"),
        P("seq"),
        P(None, "seq"),
    )
    out_specs = P("tp", "seq")
    return jax.shard_map(per_device, mesh=mesh, in_specs=in_specs, out_specs=out_specs, check_vma=False)
```

```python
import math

import jax
import jax.numpy as jnp
from jax import lax
from jax.experimental import pallas as pl
from jax.experimental.pallas import tpu as pltpu
from jax.sharding import PartitionSpec as P

D_T = 8192
D_S = 4096
HEAD = 128
SLAB = 2048
CACHE = 10240
KEYS_CHIP = 1536
HIDDEN = -1e30
LOG2E = math.log2(math.e)
SCALE = LOG2E / math.sqrt(HEAD)
MESH = pl.DeviceIdType.MESH
BF = jnp.bfloat16
F32 = jnp.float32


class Wire:
    def __init__(self, send, recv):
        self.send, self.recv, self.made, self.left = send, recv, [], set()

    def copy(self, src, dst, dev):
        i = len(self.made)
        made = pltpu.make_async_remote_copy(
            src_ref=src, dst_ref=dst, send_sem=self.send.at[i], recv_sem=self.recv.at[i],
            device_id=dev, device_id_type=MESH,
        )
        self.made.append(made)
        return made

    def close(self, first=0, last=None):
        for i in range(first, len(self.made) if last is None else last):
            if i not in self.left:
                self.left.add(i)
                self.made[i].wait_send()


class Gather:
    def __init__(self, wire, block, right, left, across=None, core=None, planes=None):
        self.planes = planes or (1 if across is None else 2)
        self.core = core is not None
        self.cross = wire.copy(block(0, 0, None), block(0, 0, None), across) if across is not None else None
        self.right, self.left, self.on_right, self.on_left, self.pass_on = [], [], [], [], []
        for plane in range(self.planes):
            own = block(plane, 0, None)
            self.right.append(wire.copy(own, own, right))
            self.left.append(wire.copy(own, own, left))
            first, second = block(plane, 3, 0), block(plane, 1, 1)
            self.on_right.append(wire.copy(first, first, right))
            self.on_left.append(wire.copy(second, second, left))
            if self.core:
                refs = [own, block(plane, 3, None), block(plane, 1, None), block(plane, 2, 0), block(plane, 2, 1)]
                self.pass_on.append([wire.copy(ref, ref, core) for ref in refs])

    def root(self, plane, start_cross=True):
        if plane == 1 and self.cross is not None:
            self.cross.wait_recv()
        self.right[plane].start()
        self.left[plane].start()
        if plane == 0 and self.cross is not None and start_cross:
            self.cross.start()
        if self.core:
            self.pass_on[plane][0].start()

    def mid(self, plane):
        self.right[plane].wait_recv()
        self.on_right[plane].start()
        if self.core:
            self.pass_on[plane][1].start()
        self.left[plane].wait_recv()
        self.on_left[plane].start()
        if self.core:
            self.pass_on[plane][2].start()

    def far(self, plane):
        self.on_right[plane].wait_recv()
        if self.core:
            self.pass_on[plane][3].start()
        self.on_left[plane].wait_recv()
        if self.core:
            self.pass_on[plane][4].start()

    def have_own(self, plane):
        self.pass_on[plane][0].wait_recv()

    def have_left(self, plane):
        self.pass_on[plane][1].wait_recv()

    def have_right(self, plane):
        self.pass_on[plane][2].wait_recv()

    def have_near(self, plane):
        self.have_left(plane)
        self.have_right(plane)

    def have_far(self, plane):
        self.pass_on[plane][3].wait_recv()
        self.pass_on[plane][4].wait_recv()


def dot(a, b, dims=((1,), (0,)), precision=None):
    return lax.dot_general(a, b, (dims, ((), ())), precision=precision, preferred_element_type=F32)


def scratch_plan():
    V = pltpu.VMEM
    D = pltpu.SemaphoreType.DMA
    return dict(
        kv=V((12, 2, 2, 768, 128), BF),
        kx=V((12, 2, 768, 256), BF),
        vt=V((12, 2, 144, 768), BF),
        score0=V((768, 512), F32),
        score1=V((768, 512), F32),
        top0=V((8, 512), F32),
        top1=V((8, 512), F32),
        qa=V((3, 2, 256, 512), BF),
        sq_in=V((128, 512), BF),
        m=V((3, 2, 8, 512), F32),
        acc=V((3, 2, 144, 512), F32),
        o_out=V((2, 128, 512), BF),
        o_in=V((2, 128, 512), BF),
        l_out=V((2, 8, 512), F32),
        l_in=V((2, 8, 512), F32),
        tctx=V((8, 2, 128, 1024), BF),
        sctx=V((8, 2, 128, 512), BF),
        tw=V((1024, 512), BF),
        sw=V((512, 256), BF),
        ty_out=V((2, 128, 512), BF),
        ty_in=V((2, 128, 512), BF),
        sy_out=V((256, 256), BF),
        sy_in=V((256, 256), BF),
        tpart=V((2, 4, 2, 128, 512), F32),
        spart=V((4, 2, 256, 256), F32),
        tr_out=V((2, 2, 128, 512), BF),
        tr_in=V((2, 2, 2, 64, 512), BF),
        sr_out=V((2, 256, 256), BF),
        sr_in=V((2, 2, 128, 256), BF),
        tz_out=V((2, 2, 2, 128, 512), BF),
        tz_in=V((2, 2, 2, 128, 512), BF),
        sz_out=V((2, 2, 256, 256), BF),
        sz_in=V((2, 2, 256, 256), BF),
        thid=V((2, 128, 512), F32),
        shid=V((256, 256), F32),
        tsq=V((2, 16, 8, 128), F32),
        ssq=V((16, 8, 256), F32),
        nb=V((16, 256, 256), BF),
        ng=V((8, 2, 256, 256), BF),
        dl=V((2, 8, 128, 512), BF),
        diff=V((2, 128, 512), F32),
        wsend=D((200,)),
        wrecv=D((200,)),
        loc=D((8,)),
    )


def kernel(doc, tq, tkv_h, sq, skv_h, tres, tw_h, tg, sres, sw_h, sg, mp_h, out, *scratch):
    b = dict(zip(scratch_plan(), scratch))
    s = lax.axis_index("seq")
    p = lax.axis_index("tp")
    yh, x, c = s // 8, (s // 2) % 4, s % 2
    z, yl = p // 2, p % 2
    k_own = yh * 4 + x

    def seq_dev(plane, off, other):
        return ((((yh + plane) % 2) * 4 + (x + off) % 4) * 2 + (c + other) % 2, p)

    def tp_dev(plane, off):
        return (s, ((z + off) % 4) * 2 + (yl + plane) % 2)

    right, left, across, core = seq_dev(0, 1, 0), seq_dev(0, 3, 0), seq_dev(1, 0, 0), seq_dev(0, 0, 1)

    loads = [
        pltpu.make_async_copy(skv_h, b["kv"].at[x, c], b["loc"].at[0]),
        pltpu.make_async_copy(tkv_h, b["kv"].at[4 + k_own, c], b["loc"].at[1]),
        pltpu.make_async_copy(sw_h, b["sw"], b["loc"].at[2]),
        pltpu.make_async_copy(tw_h, b["tw"], b["loc"].at[3]),
    ]
    for load in loads:
        load.start()
    map_loads = [
        pltpu.make_async_copy(
            mp_h.at[:, :, pl.ds(u * 256, 256)], b["kx"].at[pl.ds(0, 8), u, pl.ds(0, 512)], b["loc"].at[4 + u]
        )
        for u in range(2)
    ]

    barrier = pltpu.get_barrier_semaphore()
    for off in range(1, 16):
        pl.semaphore_signal(barrier, inc=1, device_id=((s + off) % 16, p), device_id_type=MESH)
    for off in range(1, 8):
        pl.semaphore_signal(barrier, inc=1, device_id=(s, (p + off) % 8), device_id_type=MESH)

    wire = Wire(b["wsend"], b["wrecv"])
    give_sq = wire.copy(sq, b["sq_in"], across)

    def kv_block(model):
        def block(plane, off, part):
            at = (x + off) % 4 + model * (4 + ((yh + plane) % 2) * 4)
            if part is None:
                return b["kv"].at[at, c]
            return b["kv"].at[at, c, part]

        return block

    def s_block(plane, off, part):
        at = ((yh + plane) % 2) * 4 + (x + off) % 4
        if part is None:
            return b["sctx"].at[at, c]
        return b["sctx"].at[at, c, pl.ds(part * 64, 64)]

    def t_block(half):
        def block(plane, off, part):
            at = ((yh + plane) % 2) * 4 + (x + off) % 4
            if part is None:
                return b["tctx"].at[at, c, pl.ds(half * 64, 64)]
            return b["tctx"].at[at, c, pl.ds(half * 64 + part * 32, 32)]

        return block

    def nb_block(plane, off, part):
        at = (((yh + plane) % 2) * 4 + (x + off) % 4) * 2 + c
        if part is None:
            return b["nb"].at[at]
        return b["nb"].at[at, pl.ds(part * 128, 128)]

    def dl_block(half):
        def block(plane, off, part):
            at = ((z + off) % 4) * 2 + (yl + plane) % 2
            if part is None:
                return b["dl"].at[half, at]
            return b["dl"].at[half, at, pl.ds(part * 64, 64)]

        return block

    g_skv = Gather(wire, kv_block(0), right, left, None, core)
    g_tkv = Gather(wire, kv_block(1), right, left, across, core)
    keys_sent = len(wire.made)
    g_s = Gather(wire, s_block, right, left, None, core, 2)
    g_t = [Gather(wire, t_block(half), right, left, across, core) for half in range(2)]
    contexts_sent = len(wire.made)
    g_n = Gather(wire, nb_block, right, left, across, core)
    g_d = [Gather(wire, dl_block(half), tp_dev(0, 1), tp_dev(0, 3), tp_dev(1, 0), None) for half in range(2)]
    give_o = [wire.copy(b["o_out"].at[1 - g], b["o_in"].at[g], across) for g in range(2)]
    give_l = [wire.copy(b["l_out"].at[1 - g], b["l_in"].at[g], across) for g in range(2)]
    s_sq = [wire.copy(b["ssq"].at[s], b["ssq"].at[s], ((s + off) % 16, p)) for off in range(1, 16)]
    t_sq = [
        [wire.copy(b["tsq"].at[half, s], b["tsq"].at[half, s], ((s + off) % 16, p)) for off in range(1, 16)]
        for half in range(2)
    ]
    n_tp = [
        wire.copy(b["nb"].at[((p + off) % 8) * 2 + c], b["ng"].at[p, c], (s, (p + off) % 8)) for off in range(1, 8)
    ]
    n_core = [
        wire.copy(b["ng"].at[(p + 8 - off) % 8, c], b["ng"].at[(p + 8 - off) % 8, c], core) for off in range(1, 8)
    ]

    qa, m, acc = b["qa"], b["m"], b["acc"]
    heads, tokens = (4, 8, 8), (128, 64, 64)

    def fill_queries(one, src, group):
        first = 64 * (one // 2)
        for i in range(4):
            if one == 0:
                held = src[:, i * 128 : (i + 1) * 128]
            else:
                pair = [src[first : first + 64, h * 128 : (h + 1) * 128] for h in (2 * i, 2 * i + 1)]
                held = jnp.concatenate(pair, axis=0)
            qa[one, group, 0:128, i * 128 : (i + 1) * 128] = held.T

    def prepare(first, last, passes):
        rows = lax.broadcasted_iota(jnp.int32, (128, 128), 0)
        lanes = lax.broadcasted_iota(jnp.int32, (128, 128), 1)
        for one in passes:
            eye = jnp.where(lanes % tokens[one] + 64 * (one // 2) == rows, 1.0, 0.0).astype(BF)
            for g in range(2 if one == 0 else 1):
                for i in range(4):
                    qa[one, g, 128:256, i * 128 : (i + 1) * 128] = eye
            m[one] = jnp.full((2, 8, 512), HIDDEN, F32)
            acc[one] = jnp.zeros((2, 144, 512), F32)

        def extra(i, carry):
            b["kx"][i, :, :, 128:256] = jnp.zeros((2, 768, 128), BF)
            b["vt"][i, :, 128:144, :] = jnp.ones((2, 16, 768), BF)
            return carry

        lax.fori_loop(first, last, extra, 0)

    first_key = doc[0]

    def tile_at(n, u):
        third = n // 8
        t = (third + 1) // 2
        other = third // 2
        one = t * (1 + (1 - other) * ((n % 8) // 4) + other * (n % 2))
        i = (1 - t + other) * ((n % 8) // 2) + (t - other) * (n % 4)
        plane = (yh + other) % 2
        at = (x + 3 * i + 3 * (i // 2) + 2 * (i // 3)) % 4
        from_core = (c + (1 - t) * (n % 2) + t * u) % 2
        return one, (1 - t) * u, t * (4 + plane * 4) + at, plane, at, from_core

    def build(n, u):
        one, g, block, plane, at, from_core = tile_at(n, u)
        base = (plane * 4 + at) * KEYS_CHIP + from_core * 768

        @pl.when((one <= 1) if u == 0 else (one == 1))
        def _():
            b["vt"][block, from_core, 0:128, :] = b["kv"][block, from_core, 1].T
            b["kx"][block, from_core, :, 0:128] = b["kv"][block, from_core, 0]

            @pl.when(plane == 0)
            def _():
                key = lax.broadcasted_iota(jnp.int32, (768, 128), 0)
                b["kx"][block, from_core, :, 128:256] = jnp.where(key >= first_key - base, 0.0, HIDDEN).astype(BF)

        @pl.when((one <= 1) & (plane == 1) & (at >= 2))
        def _():
            ahead = CACHE + ((((yh + g) % 2) * 4 + x) * 2 + c) * 128 - base
            key = lax.broadcasted_iota(jnp.int32, (768, 128), 0)
            row = lax.broadcasted_iota(jnp.int32, (768, 128), 1)
            b["kx"][block, from_core, :, 128:256] = jnp.where(key - row <= ahead, 0.0, HIDDEN).astype(BF)

    scores, tops = (b["score0"], b["score1"]), (b["top0"], b["top1"])

    def overlapped(n, u, weigh_n, weigh=True):
        one, g, block, _, _, from_core = tile_at(n, u)
        queries = qa[one, g]
        top = jnp.full((8, 512), HIDDEN, F32)
        if weigh:
            w_one, w_g, w_block, _, _, w_core = tile_at(weigh_n, 1 - u)
            old = m[w_one, w_g]
            peak = jnp.max(tops[1 - u][...], axis=0, keepdims=True)
            new = jnp.maximum(old, jnp.broadcast_to(peak, (8, 512)))
            total = (acc[w_one, w_g].reshape(18, 8, 512) * jnp.exp2((old - new) * SCALE)[None]).reshape(144, 512)
        for j in range(3):
            keys = slice(j * 256, (j + 1) * 256)
            fresh = dot(b["kx"][block, from_core, keys, :], queries)
            scores[u][keys, :] = fresh
            top = jnp.maximum(top, jnp.max(fresh.reshape(32, 8, 512), axis=0))
            if weigh:
                held = scores[1 - u][keys, :].reshape(32, 8, 512)
                weights = jnp.exp2((held - new[None]) * SCALE).reshape(256, 512).astype(BF)
                total = total + dot(b["vt"][w_block, w_core, :, keys], weights)
        tops[u][...] = top
        if weigh:
            m[w_one, w_g] = new
            acc[w_one, w_g] = total

    def attention(hooks):
        build(0, 0)
        overlapped(0, 0, 0, weigh=False)

        def step(n, carry):
            for at_step, hook in hooks.items():
                pl.when(n == at_step)(hook)
            build(n, 1)
            overlapped(n, 1, n)
            after = (n + 1) % 24
            build(after, 0)
            overlapped(after, 0, n)
            return carry

        lax.fori_loop(0, 24, step, 0)

    def part_of(one, g):
        total = acc[one, g, 128:136, :]
        mean = (acc[one, g, 0:128, :].reshape(16, 8, 512) * (1.0 / total)[None]).reshape(128, 512)
        return mean, m[one, g] * SCALE + jnp.log(total) * LOG2E

    def partner_part():
        for g in (1, 0):
            mean, logs = part_of(0, g)
            b["o_out"][g] = mean.astype(BF)
            b["l_out"][g] = logs
            give_o[1 - g].start()
            give_l[1 - g].start()

    def keep_context(one, plane, both, ctx):
        both = both.T.astype(BF)
        count, first = tokens[one], 64 * (one // 2)
        for h in range(heads[one]):
            held = both[h * count : (h + 1) * count, :]
            ctx[plane * 4 + x, c, first : first + count, h * 128 : (h + 1) * 128] = held

    def s_context(g):
        give_o[g].wait_recv()
        give_l[g].wait_recv()
        mine, log_mine = part_of(0, g)
        share = 1.0 / (1.0 + jnp.exp2(log_mine - b["l_in"][g]))
        other = b["o_in"][g].astype(F32)
        both = mine + ((other - mine).reshape(16, 8, 512) * share[None]).reshape(128, 512)
        keep_context(0, (yh + g) % 2, both, b["sctx"])
        g_s.root(g)

    def t_context(half):
        keep_context(1 + half, yh, part_of(1 + half, 0)[0], b["tctx"])
        g_t[half].root(0)

    class Reduce:
        def __init__(self, ctx, w, name, half):
            self.ctx, self.w, self.half = ctx, w, half

            def of(key):
                return b[name + key] if half is None else b[name + key].at[half]

            self.y_out, self.y_in, self.part, self.hid = of("y_out"), of("y_in"), of("part"), of("hid")
            self.r_out, self.r_in, self.z_out, self.z_in = of("r_out"), of("r_in"), of("z_out"), of("z_in")
            self.rows = self.part.shape[2] // 2
            near = (tp_dev(0, 3), tp_dev(0, 1))
            self.relay = [
                wire.copy(self.r_out.at[:, pl.ds(i * self.rows, self.rows)], self.r_in.at[i], near[i]) for i in range(2)
            ]
            self.along = [wire.copy(self.z_out.at[i], self.z_in.at[i], near[i]) for i in range(2)]
            self.beside = wire.copy(self.y_out, self.y_in, tp_dev(1, 0))

        def multiply(self, first, last, waits):
            def pair(j, carry):
                for at, wait in waits.items():
                    pl.when(j == at)(wait)
                zd = ((yh + j // 2) % 2) * 2 + (x // 2 + j % 2) % 2

                both = pl.ds(zd * 2, 2)
                if self.half is None:
                    held = self.ctx[both]
                else:
                    held = self.ctx[both, :, self.half * 64 : self.half * 64 + 64]
                done = dot(held.reshape(-1, held.shape[3]), self.w[...])
                self.part[zd] = done.reshape(2, -1, done.shape[1])

                @pl.when(zd == (z + 2) % 4)
                def _():
                    self.r_out[...] = self.part[zd].astype(BF)
                    self.relay[0].start()
                    self.relay[1].start()

                return carry

            lax.fori_loop(first, last, pair, 0)

        def send_on(self):
            for i, zd in enumerate(((z + 3) % 4, (z + 1) % 4)):
                mid = slice(i * self.rows, (i + 1) * self.rows)
                rest = slice((1 - i) * self.rows, (2 - i) * self.rows)
                self.z_out[i, :, rest, :] = self.part[zd, :, rest, :].astype(BF)
                self.relay[i].wait_recv()
                self.z_out[i, :, mid, :] = (self.part[zd, :, mid, :] + self.r_in[i].astype(F32)).astype(BF)
                self.along[i].start()

        def settle(self):
            self.along[0].wait_recv()
            self.along[1].wait_recv()

            def block(u):
                return self.part[z, u] + self.z_in[0, u].astype(F32) + self.z_in[1, u].astype(F32)

            self.y_out[...] = block(1 - yl).astype(BF)
            self.beside.start()
            self.hid[...] = block(yl)

        def finish(self, resid):
            if self.half is None:
                own = resid[...]
            else:
                first = self.half * 64
                own = jnp.concatenate([resid[first : first + 64, :], resid[first + 128 : first + 192, :]], axis=0)
            total = self.hid[...] + own.astype(F32)
            self.beside.wait_recv()
            self.hid[...] = total + self.y_in[...].astype(F32)

    def send_squares(hid, sq, copies):
        value = hid[...]
        ones = jnp.ones((8, value.shape[1]), F32)
        sq[s] = dot(ones, value * value, ((1,), (1,)), lax.Precision.HIGHEST)
        for made in copies:
            made.start()

    def inverse_scale(sq, copies, width):
        for made in copies:
            made.wait_recv()
        total = sq[0]
        for i in range(1, 16):
            total = total + sq[i]
        first = jnp.where(lax.broadcasted_iota(jnp.int32, (8, 128), 0) == 0, 1.0, 0.0)
        column = dot(total, first, ((0,), (0,)), lax.Precision.HIGHEST)
        return 1.0 / jnp.sqrt(column * (1.0 / width) + 1e-05)

    r_s = Reduce(b["sctx"], b["sw"], "s", None)
    r_t = [Reduce(b["tctx"], b["tw"], "t", half) for half in range(2)]

    def ready(gather, plane):
        gather.have_own(plane)
        gather.have_near(plane)
        gather.have_far(plane)

    fill_queries(0, sq, 0)
    prepare(0, 4, (0,))
    loads[0].wait()
    loads[1].wait()
    pl.semaphore_wait(barrier, 22)
    g_skv.root(0)
    give_sq.start()
    g_tkv.cross.start()

    def s_partner():
        g_skv.have_own(0)
        give_sq.wait_recv()
        fill_queries(0, b["sq_in"], 1)

    def s_near():
        prepare(4, 12, (1, 2))
        fill_queries(1, tq, 0)
        fill_queries(2, tq, 0)
        g_skv.mid(0)
        g_tkv.root(0, False)

    def t_start():
        partner_part()
        g_tkv.have_own(0)
        g_tkv.mid(0)
        g_tkv.root(1)

    def s_sums():
        for load in loads[2:]:
            load.wait()
        r_s.multiply(0, 4, {0: lambda: ready(g_s, 0), 2: lambda: ready(g_s, 1)})

    def s_squares():
        r_s.finish(sres)
        send_squares(b["shid"], b["ssq"], s_sq)

    def s_normed():
        inverse = inverse_scale(b["ssq"], s_sq, D_S)
        inverse = jnp.concatenate([inverse, inverse], axis=1)
        normed = (b["shid"][...] * inverse * sg[...]).astype(BF)
        for at, first in enumerate((0, 128, 64, 192)):
            b["nb"][s, at * 64 : (at + 1) * 64, :] = normed[first : first + 64, :]
        g_n.root(0)

    def t1_sums():
        r_t[0].multiply(0, 4, {0: lambda: ready(g_t[0], 0), 2: lambda: ready(g_t[0], 1)})

    def both(*hooks):
        def run():
            for hook in hooks:
                hook()

        return run

    attention(
        {
            0: s_partner,
            1: s_near,
            2: lambda: g_skv.have_left(0),
            4: lambda: g_skv.have_right(0),
            5: lambda: g_skv.far(0),
            6: lambda: g_skv.have_far(0),
            8: t_start,
            9: lambda: g_tkv.have_left(0),
            10: both(lambda: g_tkv.have_right(0), lambda: g_tkv.far(0)),
            11: lambda: g_tkv.have_far(0),
            12: lambda: s_context(0),
            16: both(lambda: g_tkv.have_own(1), lambda: s_context(1)),
            17: lambda: g_tkv.mid(1),
            18: both(lambda: g_tkv.have_left(1), lambda: g_s.mid(0)),
            20: both(lambda: g_tkv.have_right(1), lambda: g_s.mid(1), lambda: g_s.far(0)),
            21: lambda: g_tkv.far(1),
            22: both(lambda: g_tkv.have_far(1), lambda: g_s.far(1)),
            23: lambda: t_context(0),
        }
    )
    for load in map_loads:
        load.start()
    t_context(1)
    s_sums()
    r_s.send_on()
    g_t[0].mid(0)
    g_t[0].root(1)
    g_t[1].mid(0)
    g_t[1].root(1)
    wire.close(0, keys_sent)
    g_t[0].far(0)
    g_t[0].mid(1)
    r_s.settle()
    g_t[0].far(1)
    t1_sums()
    g_t[1].far(0)
    g_t[1].mid(1)
    s_squares()
    g_t[1].far(1)
    r_t[0].send_on()
    r_t[1].multiply(0, 4, {0: lambda: ready(g_t[1], 0), 2: lambda: ready(g_t[1], 1)})
    s_normed()
    r_t[1].send_on()
    r_t[0].settle()
    g_n.mid(0)
    g_n.root(1)
    r_t[0].finish(tres)
    send_squares(b["thid"].at[0], b["tsq"].at[0], t_sq[0])
    g_n.far(0)
    g_n.mid(1)
    r_t[1].settle()
    g_n.far(1)
    for made in n_tp:
        made.start()
    r_t[1].finish(tres)
    send_squares(b["thid"].at[1], b["tsq"].at[1], t_sq[1])
    wire.close(keys_sent, contexts_sent)
    ready(g_n, 0)
    ready(g_n, 1)
    b["diff"][...] = jnp.zeros((2, 128, 512), F32)
    for load in map_loads:
        load.wait()

    def match(k, carry):
        lhs = jnp.concatenate([b["nb"][2 * k], b["nb"][2 * k + 1]], axis=1)
        for u in range(2):
            b["diff"][:, :, u * 256 : (u + 1) * 256] += dot(lhs, b["kx"][k, u, 0:512, :]).reshape(2, 128, 256)
        return carry

    lax.fori_loop(0, 8, match, 0)

    def delta(half):
        inverse = inverse_scale(b["tsq"].at[half], t_sq[half], D_T)
        inverse = jnp.concatenate([inverse, inverse, inverse, inverse], axis=1)
        target = b["thid"][half] * inverse * tg[...]
        b["dl"][half, p] = ((b["diff"][half] - target) * (1.0 / math.sqrt(SLAB))).astype(BF)
        g_d[half].root(0)

    def gradient(half, plane, offs):
        def one(i, carry):
            q = ((z + offs[0] + i * offs[1]) % 4) * 2 + (yl + plane) % 2
            for at in range(2):
                rows = slice(at * 256, (at + 1) * 256)
                lhs = b["ng"][q, at, half * 128 : (half + 1) * 128, :]
                out[rows, :] += dot(lhs, b["dl"][half, q], ((0,), (0,)))
            return carry

        lax.fori_loop(0, offs[2], one, 0)

    own, near, far = (0, 1, 1), (1, 2, 2), (2, 1, 1)
    delta(0)
    delta(1)
    b["ng"][p, 0] = b["nb"][2 * p]
    b["ng"][p, 1] = b["nb"][2 * p + 1]
    out[...] = jnp.zeros((512, 512), F32)
    g_d[0].mid(0)
    g_d[0].root(1)
    for made, onward in zip(n_tp, n_core):
        made.wait_recv()
        onward.start()
    g_d[0].far(0)
    g_d[0].mid(1)
    for made in n_core:
        made.wait_recv()
    gradient(0, 0, own)
    gradient(0, 0, near)
    gradient(0, 0, far)
    gradient(0, 1, own)
    g_d[1].mid(0)
    g_d[1].root(1)
    gradient(0, 1, near)
    g_d[0].far(1)
    gradient(0, 1, far)
    gradient(1, 0, own)
    gradient(1, 0, near)
    gradient(1, 1, own)
    g_d[1].far(0)
    g_d[1].mid(1)
    gradient(1, 0, far)
    gradient(1, 1, near)
    g_d[1].far(1)
    gradient(1, 1, far)
    wire.close()


def per_device(tq, tkv, sq, skv, doc, tres, tw, tg, sres, sw, sg, mp):
    V = pl.BlockSpec(memory_space=pltpu.VMEM)
    A = pl.BlockSpec(memory_space=pl.ANY)
    S = pl.BlockSpec(memory_space=pltpu.SMEM)
    return pl.pallas_call(
        kernel,
        out_shape=jax.ShapeDtypeStruct((512, 512), F32),
        in_specs=[S, V, A, V, A, V, A, V, V, A, V, A],
        out_specs=V,
        scratch_shapes=list(scratch_plan().values()),
        compiler_params=pltpu.CompilerParams(
            collective_id=0, has_side_effects=True, vmem_limit_bytes=63 * 1024 * 1024
        ),
    )(
        doc, tq, tkv, sq, skv, tres, tw, tg.reshape(1, -1), sres, sw, sg.reshape(1, -1), mp.reshape(8, 512, 512)
    )


def solution(mesh):
    in_specs = (
        P("seq", "tp"),
        P(None, "seq", "tp"),
        P("seq", "tp"),
        P(None, "seq", "tp"),
        P(),
        P("tp", "seq"),
        P("tp", "seq"),
        P("seq"),
        P("tp", "seq"),
        P("tp", "seq"),
        P("seq"),
        P(None, "seq"),
    )
    out_specs = P("tp", "seq")
    return jax.shard_map(per_device, mesh=mesh, in_specs=in_specs, out_specs=out_specs, check_vma=False)
```

```python
import math

import jax
import jax.numpy as jnp
from jax import lax
from jax.experimental import pallas as pl
from jax.experimental.pallas import tpu as pltpu
from jax.sharding import PartitionSpec as P

D_T = 8192
D_S = 4096
HEAD = 128
SLAB = 2048
CACHE = 10240
KEYS_CHIP = 1536
HIDDEN = -1e30
LOG2E = math.log2(math.e)
SCALE = LOG2E / math.sqrt(HEAD)
MESH = pl.DeviceIdType.MESH
BF = jnp.bfloat16
F32 = jnp.float32


class Wire:
    def __init__(self, send, recv):
        self.send, self.recv, self.made, self.left = send, recv, [], set()

    def copy(self, src, dst, dev):
        i = len(self.made)
        made = pltpu.make_async_remote_copy(
            src_ref=src, dst_ref=dst, send_sem=self.send.at[i], recv_sem=self.recv.at[i],
            device_id=dev, device_id_type=MESH,
        )
        self.made.append(made)
        return made

    def close(self, first=0, last=None):
        for i in range(first, len(self.made) if last is None else last):
            if i not in self.left:
                self.left.add(i)
                self.made[i].wait_send()


class Gather:
    def __init__(self, wire, block, right, left, across=None, core=None, planes=None):
        self.planes = planes or (1 if across is None else 2)
        self.core = core is not None
        self.cross = wire.copy(block(0, 0, None), block(0, 0, None), across) if across is not None else None
        self.right, self.left, self.on_right, self.on_left, self.pass_on = [], [], [], [], []
        for plane in range(self.planes):
            own = block(plane, 0, None)
            self.right.append(wire.copy(own, own, right))
            self.left.append(wire.copy(own, own, left))
            first, second = block(plane, 3, 0), block(plane, 1, 1)
            self.on_right.append(wire.copy(first, first, right))
            self.on_left.append(wire.copy(second, second, left))
            if self.core:
                refs = [own, block(plane, 3, None), block(plane, 1, None), block(plane, 2, None)]
                self.pass_on.append([wire.copy(ref, ref, core) for ref in refs])

    def root(self, plane, start_cross=True):
        if plane == 1 and self.cross is not None:
            self.cross.wait_recv()
        self.right[plane].start()
        self.left[plane].start()
        if plane == 0 and self.cross is not None and start_cross:
            self.cross.start()
        if self.core:
            self.pass_on[plane][0].start()

    def mid(self, plane):
        self.right[plane].wait_recv()
        self.on_right[plane].start()
        if self.core:
            self.pass_on[plane][1].start()
        self.left[plane].wait_recv()
        self.on_left[plane].start()
        if self.core:
            self.pass_on[plane][2].start()

    def far(self, plane):
        self.on_right[plane].wait_recv()
        self.on_left[plane].wait_recv()
        if self.core:
            self.pass_on[plane][3].start()

    def have_own(self, plane):
        self.pass_on[plane][0].wait_recv()

    def have_left(self, plane):
        self.pass_on[plane][1].wait_recv()

    def have_right(self, plane):
        self.pass_on[plane][2].wait_recv()

    def have_near(self, plane):
        self.have_left(plane)
        self.have_right(plane)

    def have_far(self, plane):
        self.pass_on[plane][3].wait_recv()


def dot(a, b, dims=((1,), (0,)), precision=None):
    return lax.dot_general(a, b, (dims, ((), ())), precision=precision, preferred_element_type=F32)


def scratch_plan():
    V = pltpu.VMEM
    D = pltpu.SemaphoreType.DMA
    return dict(
        kv=V((12, 2, 2, 768, 128), BF),
        kx=V((12, 2, 768, 256), BF),
        vt=V((12, 2, 144, 768), BF),
        score0=V((768, 512), F32),
        score1=V((768, 512), F32),
        top0=V((8, 512), F32),
        top1=V((8, 512), F32),
        qa=V((3, 2, 256, 512), BF),
        sq_in=V((128, 512), BF),
        tq_in=V((128, 1024), BF),
        to_out=V((2, 128, 512), BF),
        to_in=V((2, 128, 512), BF),
        tl_out=V((2, 8, 512), F32),
        tl_in=V((2, 8, 512), F32),
        m=V((3, 2, 8, 512), F32),
        acc=V((3, 2, 144, 512), F32),
        o_out=V((2, 128, 512), BF),
        o_in=V((2, 128, 512), BF),
        l_out=V((2, 8, 512), F32),
        l_in=V((2, 8, 512), F32),
        tctx=V((8, 2, 128, 1024), BF),
        sctx=V((8, 2, 128, 512), BF),
        tw=V((1024, 512), BF),
        sw=V((512, 256), BF),
        ty_out=V((2, 128, 512), BF),
        ty_in=V((2, 128, 512), BF),
        sy_out=V((256, 256), BF),
        sy_in=V((256, 256), BF),
        tpart=V((2, 4, 2, 128, 512), F32),
        spart=V((4, 2, 256, 256), F32),
        tr_out=V((2, 2, 128, 512), BF),
        tr_in=V((2, 2, 2, 64, 512), BF),
        sr_out=V((2, 256, 256), BF),
        sr_in=V((2, 2, 128, 256), BF),
        tz_out=V((2, 2, 2, 128, 512), BF),
        tz_in=V((2, 2, 2, 128, 512), BF),
        sz_out=V((2, 2, 256, 256), BF),
        sz_in=V((2, 2, 256, 256), BF),
        thid=V((2, 128, 512), F32),
        shid=V((256, 256), F32),
        tsq=V((2, 8, 8, 128), F32),
        ssq=V((8, 8, 256), F32),
        tsq_chip=V((2, 2, 8, 128), F32),
        ssq_chip=V((2, 8, 256), F32),
        nb=V((16, 256, 256), BF),
        ng=V((8, 2, 256, 256), BF),
        dl=V((2, 8, 128, 512), BF),
        diff=V((2, 128, 512), F32),
        wsend=D((200,)),
        wrecv=D((200,)),
        loc=D((8,)),
    )


def kernel(doc, tq, tkv_h, sq, skv_h, tres, tw_h, tg, sres, sw_h, sg, mp_h, out, *scratch):
    b = dict(zip(scratch_plan(), scratch))
    s = lax.axis_index("seq")
    p = lax.axis_index("tp")
    yh, x, c = s // 8, (s // 2) % 4, s % 2
    z, yl = p // 2, p % 2
    k_own = yh * 4 + x

    def seq_dev(plane, off, other):
        return ((((yh + plane) % 2) * 4 + (x + off) % 4) * 2 + (c + other) % 2, p)

    def tp_dev(plane, off):
        return (s, ((z + off) % 4) * 2 + (yl + plane) % 2)

    right, left, across, core = seq_dev(0, 1, 0), seq_dev(0, 3, 0), seq_dev(1, 0, 0), seq_dev(0, 0, 1)

    loads = [
        pltpu.make_async_copy(skv_h, b["kv"].at[x, c], b["loc"].at[0]),
        pltpu.make_async_copy(tkv_h, b["kv"].at[4 + k_own, c], b["loc"].at[1]),
        pltpu.make_async_copy(sw_h, b["sw"], b["loc"].at[2]),
        pltpu.make_async_copy(tw_h, b["tw"], b["loc"].at[3]),
    ]
    for load in loads:
        load.start()
    map_loads = [
        pltpu.make_async_copy(
            mp_h.at[:, :, pl.ds(u * 256, 256)], b["kx"].at[pl.ds(0, 8), u, pl.ds(0, 512)], b["loc"].at[4 + u]
        )
        for u in range(2)
    ]

    barrier = pltpu.get_barrier_semaphore()
    for off in range(1, 16):
        pl.semaphore_signal(barrier, inc=1, device_id=((s + off) % 16, p), device_id_type=MESH)
    for off in range(1, 8):
        pl.semaphore_signal(barrier, inc=1, device_id=(s, (p + off) % 8), device_id_type=MESH)

    wire = Wire(b["wsend"], b["wrecv"])
    give_sq = wire.copy(sq, b["sq_in"], across)
    give_tq = wire.copy(tq, b["tq_in"], core)

    def kv_block(model):
        def block(plane, off, part):
            at = (x + off) % 4 + model * (4 + ((yh + plane) % 2) * 4)
            if part is None:
                return b["kv"].at[at, c]
            return b["kv"].at[at, c, part]

        return block

    def s_block(plane, off, part):
        at = ((yh + plane) % 2) * 4 + (x + off) % 4
        if part is None:
            return b["sctx"].at[at, c]
        return b["sctx"].at[at, c, pl.ds(part * 64, 64)]

    def t_block(half):
        def block(plane, off, part):
            at = ((yh + plane) % 2) * 4 + (x + off) % 4
            if part is None:
                return b["tctx"].at[at, c, pl.ds(half * 64, 64)]
            return b["tctx"].at[at, c, pl.ds(half * 64 + part * 32, 32)]

        return block

    def nb_block(plane, off, part):
        at = (((yh + plane) % 2) * 4 + (x + off) % 4) * 2 + c
        if part is None:
            return b["nb"].at[at]
        return b["nb"].at[at, pl.ds(part * 128, 128)]

    def dl_block(half):
        def block(plane, off, part):
            at = ((z + off) % 4) * 2 + (yl + plane) % 2
            if part is None:
                return b["dl"].at[half, at]
            return b["dl"].at[half, at, pl.ds(part * 64, 64)]

        return block

    g_skv = Gather(wire, kv_block(0), right, left, None, core)
    g_tkv = Gather(wire, kv_block(1), right, left, across)
    keys_sent = len(wire.made)
    g_s = Gather(wire, s_block, right, left, None, core, 2)
    g_t = [Gather(wire, t_block(half), right, left, across, core) for half in range(2)]
    contexts_sent = len(wire.made)
    g_n = Gather(wire, nb_block, right, left, across, core)
    g_d = [Gather(wire, dl_block(half), tp_dev(0, 1), tp_dev(0, 3), tp_dev(1, 0), None) for half in range(2)]
    give_to = [wire.copy(b["to_out"].at[i], b["to_in"].at[i], core) for i in range(2)]
    give_tl = [wire.copy(b["tl_out"].at[i], b["tl_in"].at[i], core) for i in range(2)]
    give_o = [wire.copy(b["o_out"].at[1 - g], b["o_in"].at[g], across) for g in range(2)]
    give_l = [wire.copy(b["l_out"].at[1 - g], b["l_in"].at[g], across) for g in range(2)]
    def square_copies(chip, sq):
        between = wire.copy(chip.at[c], chip.at[c], core)
        offs = range(1, 8)
        spread = [wire.copy(sq.at[k_own], sq.at[k_own], (((k_own + off) % 8) * 2 + c, p)) for off in offs]
        return chip, sq, between, spread

    s_sq = square_copies(b["ssq_chip"], b["ssq"])
    t_sq = [square_copies(b["tsq_chip"].at[half], b["tsq"].at[half]) for half in range(2)]
    n_tp = [
        wire.copy(b["nb"].at[((p + off) % 8) * 2 + c], b["ng"].at[p, c], (s, (p + off) % 8)) for off in range(1, 8)
    ]
    n_core = wire.copy(b["ng"].at[:, c], b["ng"].at[:, c], core)

    qa, m, acc = b["qa"], b["m"], b["acc"]
    heads, tokens = (4, 8, 8), (128, 64, 64)

    def fill_queries(one, src, group):
        first = 64 * (one // 2)
        for i in range(4):
            if one == 0:
                held = src[:, i * 128 : (i + 1) * 128]
            else:
                pair = [src[first : first + 64, h * 128 : (h + 1) * 128] for h in (2 * i, 2 * i + 1)]
                held = jnp.concatenate(pair, axis=0)
            qa[one, group, 0:128, i * 128 : (i + 1) * 128] = held.T

    def prepare(first, last, passes):
        rows = lax.broadcasted_iota(jnp.int32, (128, 128), 0)
        lanes = lax.broadcasted_iota(jnp.int32, (128, 128), 1)
        for one in passes:
            eye = jnp.where(lanes % tokens[one] + 64 * (one // 2) == rows, 1.0, 0.0).astype(BF)
            for g in range(2):
                for i in range(4):
                    qa[one, g, 128:256, i * 128 : (i + 1) * 128] = eye
            m[one] = jnp.full((2, 8, 512), HIDDEN, F32)
            acc[one] = jnp.zeros((2, 144, 512), F32)

        def extra(i, carry):
            b["kx"][i, :, :, 128:256] = jnp.zeros((2, 768, 128), BF)
            b["vt"][i, :, 128:144, :] = jnp.ones((2, 16, 768), BF)
            return carry

        lax.fori_loop(first, last, extra, 0)

    first_key = doc[0]

    def tile_at(n):
        third = n // 8
        t = (third + 1) // 2
        other = third // 2
        one = t * (1 + (1 - other) * ((n % 8) // 4) + other * (n % 2))
        i = (1 - t + other) * ((n % 8) // 2) + (t - other) * (n % 4)
        plane = (yh + other) % 2
        at = (x + 3 * i + 3 * (i // 2) + 2 * (i // 3)) % 4
        return one, t, t * (4 + plane * 4) + at, plane, at, (c + (1 - t) * (n % 2)) % 2

    def build(n, g):
        one, t, block, plane, at, from_core = tile_at(n)
        base = (plane * 4 + at) * KEYS_CHIP + from_core * 768

        if g == 0:

            @pl.when(one <= 1)
            def _():
                b["vt"][block, from_core, 0:128, :] = b["kv"][block, from_core, 1].T
                b["kx"][block, from_core, :, 0:128] = b["kv"][block, from_core, 0]

                @pl.when(plane == 0)
                def _():
                    key = lax.broadcasted_iota(jnp.int32, (768, 128), 0)
                    b["kx"][block, from_core, :, 128:256] = jnp.where(key >= first_key - base, 0.0, HIDDEN).astype(BF)

        @pl.when((plane == 1) & (at >= 2))
        def _():
            ahead = CACHE + ((((yh + (1 - t) * g) % 2) * 4 + x) * 2 + (c + t * g) % 2) * 128 - base
            key = lax.broadcasted_iota(jnp.int32, (768, 128), 0)
            row = lax.broadcasted_iota(jnp.int32, (768, 128), 1)
            b["kx"][block, from_core, :, 128:256] = jnp.where(key - row <= ahead, 0.0, HIDDEN).astype(BF)

    scores, tops = (b["score0"], b["score1"]), (b["top0"], b["top1"])

    def overlapped(n, u, weigh_n, weigh=True):
        one, _, block, _, _, from_core = tile_at(n)
        queries = qa[one, u]
        top = jnp.full((8, 512), HIDDEN, F32)
        if weigh:
            w_one, _, w_block, _, _, w_core = tile_at(weigh_n)
            w_g = 1 - u
            old = m[w_one, w_g]
            peak = jnp.max(tops[1 - u][...], axis=0, keepdims=True)
            new = jnp.maximum(old, jnp.broadcast_to(peak, (8, 512)))
            total = (acc[w_one, w_g].reshape(18, 8, 512) * jnp.exp2((old - new) * SCALE)[None]).reshape(144, 512)
        for j in range(3):
            keys = slice(j * 256, (j + 1) * 256)
            fresh = dot(b["kx"][block, from_core, keys, :], queries)
            scores[u][keys, :] = fresh
            top = jnp.maximum(top, jnp.max(fresh.reshape(32, 8, 512), axis=0))
            if weigh:
                held = scores[1 - u][keys, :].reshape(32, 8, 512)
                weights = jnp.exp2((held - new[None]) * SCALE).reshape(256, 512).astype(BF)
                total = total + dot(b["vt"][w_block, w_core, :, keys], weights)
        tops[u][...] = top
        if weigh:
            m[w_one, w_g] = new
            acc[w_one, w_g] = total

    def attention(hooks):
        build(0, 0)
        overlapped(0, 0, 0, weigh=False)

        def step(n, carry):
            for at_step, hook in hooks.items():
                pl.when(n == at_step)(hook)
            build(n, 1)
            overlapped(n, 1, n)
            after = (n + 1) % 24
            build(after, 0)
            overlapped(after, 0, n)
            return carry

        lax.fori_loop(0, 24, step, 0)

    def part_of(one, g):
        total = acc[one, g, 128:136, :]
        mean = (acc[one, g, 0:128, :].reshape(16, 8, 512) * (1.0 / total)[None]).reshape(128, 512)
        return mean, m[one, g] * SCALE + jnp.log(total) * LOG2E

    def partner_part():
        for g in (1, 0):
            mean, logs = part_of(0, g)
            b["o_out"][g] = mean.astype(BF)
            b["l_out"][g] = logs
            give_o[1 - g].start()
            give_l[1 - g].start()

    def keep_context(one, plane, both, ctx):
        both = both.T.astype(BF)
        count, first = tokens[one], 64 * (one // 2)
        for h in range(heads[one]):
            held = both[h * count : (h + 1) * count, :]
            ctx[plane * 4 + x, c, first : first + count, h * 128 : (h + 1) * 128] = held

    def joined(one, g, o_in, l_in):
        mine, log_mine = part_of(one, g)
        share = 1.0 / (1.0 + jnp.exp2(log_mine - l_in[...]))
        other = o_in[...].astype(F32)
        return mine + ((other - mine).reshape(16, 8, 512) * share[None]).reshape(128, 512)

    def s_context(g):
        give_o[g].wait_recv()
        give_l[g].wait_recv()
        keep_context(0, (yh + g) % 2, joined(0, g, b["o_in"].at[g], b["l_in"].at[g]), b["sctx"])
        g_s.root(g)

    def t_part(half):
        mean, logs = part_of(1 + half, 1)
        b["to_out"][half] = mean.astype(BF)
        b["tl_out"][half] = logs
        give_to[half].start()
        give_tl[half].start()

    def t_context(half):
        give_to[half].wait_recv()
        give_tl[half].wait_recv()
        keep_context(1 + half, yh, joined(1 + half, 0, b["to_in"].at[half], b["tl_in"].at[half]), b["tctx"])
        g_t[half].root(0)

    class Reduce:
        def __init__(self, ctx, w, name, half):
            self.ctx, self.w, self.half = ctx, w, half

            def of(key):
                return b[name + key] if half is None else b[name + key].at[half]

            self.y_out, self.y_in, self.part, self.hid = of("y_out"), of("y_in"), of("part"), of("hid")
            self.r_out, self.r_in, self.z_out, self.z_in = of("r_out"), of("r_in"), of("z_out"), of("z_in")
            self.rows = self.part.shape[2] // 2
            near = (tp_dev(0, 3), tp_dev(0, 1))
            self.relay = [
                wire.copy(self.r_out.at[:, pl.ds(i * self.rows, self.rows)], self.r_in.at[i], near[i]) for i in range(2)
            ]
            self.along = [wire.copy(self.z_out.at[i], self.z_in.at[i], near[i]) for i in range(2)]
            self.beside = wire.copy(self.y_out, self.y_in, tp_dev(1, 0))

        def multiply(self, first, last, waits):
            def pair(j, carry):
                for at, wait in waits.items():
                    pl.when(j == at)(wait)
                zd = ((yh + j // 2) % 2) * 2 + (x // 2 + j % 2) % 2

                both = pl.ds(zd * 2, 2)
                if self.half is None:
                    held = self.ctx[both]
                else:
                    held = self.ctx[both, :, self.half * 64 : self.half * 64 + 64]
                done = dot(held.reshape(-1, held.shape[3]), self.w[...])
                self.part[zd] = done.reshape(2, -1, done.shape[1])

                @pl.when(zd == (z + 2) % 4)
                def _():
                    self.r_out[...] = self.part[zd].astype(BF)
                    self.relay[0].start()
                    self.relay[1].start()

                return carry

            lax.fori_loop(first, last, pair, 0)

        def send_on(self):
            for i, zd in enumerate(((z + 3) % 4, (z + 1) % 4)):
                mid = slice(i * self.rows, (i + 1) * self.rows)
                rest = slice((1 - i) * self.rows, (2 - i) * self.rows)
                self.z_out[i, :, rest, :] = self.part[zd, :, rest, :].astype(BF)
                self.relay[i].wait_recv()
                self.z_out[i, :, mid, :] = (self.part[zd, :, mid, :] + self.r_in[i].astype(F32)).astype(BF)
                self.along[i].start()

        def settle(self):
            self.along[0].wait_recv()
            self.along[1].wait_recv()

            def block(u):
                return self.part[z, u] + self.z_in[0, u].astype(F32) + self.z_in[1, u].astype(F32)

            self.y_out[...] = block(1 - yl).astype(BF)
            self.beside.start()
            self.hid[...] = block(yl)

        def finish(self, resid):
            if self.half is None:
                own = resid[...]
            else:
                first = self.half * 64
                own = jnp.concatenate([resid[first : first + 64, :], resid[first + 128 : first + 192, :]], axis=0)
            total = self.hid[...] + own.astype(F32)
            self.beside.wait_recv()
            self.hid[...] = total + self.y_in[...].astype(F32)

    def send_squares(hid, squares):
        chip, sq, between, spread = squares
        value = hid[...]
        ones = jnp.ones((8, value.shape[1]), F32)
        chip[c] = dot(ones, value * value, ((1,), (1,)), lax.Precision.HIGHEST)
        between.start()
        between.wait_recv()
        sq[k_own] = chip[0] + chip[1]
        for made in spread:
            made.start()

    def inverse_scale(squares, width):
        _, sq, _, spread = squares
        for made in spread:
            made.wait_recv()
        total = sq[0]
        for i in range(1, 8):
            total = total + sq[i]
        first = jnp.where(lax.broadcasted_iota(jnp.int32, (8, 128), 0) == 0, 1.0, 0.0)
        column = dot(total, first, ((0,), (0,)), lax.Precision.HIGHEST)
        return 1.0 / jnp.sqrt(column * (1.0 / width) + 1e-05)

    r_s = Reduce(b["sctx"], b["sw"], "s", None)
    r_t = [Reduce(b["tctx"], b["tw"], "t", half) for half in range(2)]

    def ready(gather, plane):
        gather.have_own(plane)
        gather.have_near(plane)
        gather.have_far(plane)

    fill_queries(0, sq, 0)
    prepare(0, 4, (0,))
    loads[0].wait()
    loads[1].wait()
    pl.semaphore_wait(barrier, 22)
    g_skv.root(0)
    give_sq.start()
    give_tq.start()
    g_tkv.cross.start()

    def s_partner():
        g_skv.have_own(0)
        give_sq.wait_recv()
        fill_queries(0, b["sq_in"], 1)

    def s_near():
        prepare(4, 12, (1, 2))
        fill_queries(1, tq, 0)
        fill_queries(2, tq, 0)
        give_tq.wait_recv()
        fill_queries(1, b["tq_in"], 1)
        fill_queries(2, b["tq_in"], 1)
        g_skv.mid(0)
        g_tkv.root(0, False)

    def t_start():
        partner_part()
        g_tkv.mid(0)
        g_tkv.root(1)

    def s_sums():
        for load in loads[2:]:
            load.wait()
        r_s.multiply(0, 4, {0: lambda: ready(g_s, 0), 2: lambda: ready(g_s, 1)})

    def s_squares():
        r_s.finish(sres)
        send_squares(b["shid"], s_sq)

    def s_normed():
        inverse = inverse_scale(s_sq, D_S)
        inverse = jnp.concatenate([inverse, inverse], axis=1)
        normed = (b["shid"][...] * inverse * sg[...]).astype(BF)
        for at, first in enumerate((0, 128, 64, 192)):
            b["nb"][s, at * 64 : (at + 1) * 64, :] = normed[first : first + 64, :]
        g_n.root(0)

    def t1_sums():
        r_t[0].multiply(0, 4, {0: lambda: ready(g_t[0], 0), 2: lambda: ready(g_t[0], 1)})

    def both(*hooks):
        def run():
            for hook in hooks:
                hook()

        return run

    attention(
        {
            0: s_partner,
            1: s_near,
            2: lambda: g_skv.have_left(0),
            4: lambda: g_skv.have_right(0),
            5: lambda: g_skv.far(0),
            6: lambda: g_skv.have_far(0),
            8: t_start,
            10: lambda: g_tkv.far(0),
            12: lambda: s_context(0),
            16: lambda: s_context(1),
            17: lambda: g_tkv.mid(1),
            18: lambda: g_s.mid(0),
            20: both(lambda: g_s.mid(1), lambda: g_s.far(0)),
            21: lambda: g_tkv.far(1),
            22: lambda: g_s.far(1),
            23: lambda: t_part(0),
        }
    )
    for load in map_loads:
        load.start()
    t_part(1)
    t_context(0)
    t_context(1)
    s_sums()
    r_s.send_on()
    g_t[0].mid(0)
    g_t[0].root(1)
    g_t[1].mid(0)
    g_t[1].root(1)
    wire.close(0, keys_sent)
    g_t[0].far(0)
    g_t[0].mid(1)
    r_s.settle()
    g_t[0].far(1)
    t1_sums()
    g_t[1].far(0)
    g_t[1].mid(1)
    s_squares()
    g_t[1].far(1)
    r_t[0].send_on()
    r_t[1].multiply(0, 4, {0: lambda: ready(g_t[1], 0), 2: lambda: ready(g_t[1], 1)})
    s_normed()
    r_t[1].send_on()
    r_t[0].settle()
    g_n.mid(0)
    g_n.root(1)
    r_t[0].finish(tres)
    send_squares(b["thid"].at[0], t_sq[0])
    g_n.far(0)
    g_n.mid(1)
    r_t[1].settle()
    g_n.far(1)
    for made in n_tp:
        made.start()
    r_t[1].finish(tres)
    send_squares(b["thid"].at[1], t_sq[1])
    wire.close(keys_sent, contexts_sent)
    ready(g_n, 0)
    ready(g_n, 1)
    b["diff"][...] = jnp.zeros((2, 128, 512), F32)
    for load in map_loads:
        load.wait()

    def match(k, carry):
        lhs = jnp.concatenate([b["nb"][2 * k], b["nb"][2 * k + 1]], axis=1)
        for u in range(2):
            b["diff"][:, :, u * 256 : (u + 1) * 256] += dot(lhs, b["kx"][k, u, 0:512, :]).reshape(2, 128, 256)
        return carry

    lax.fori_loop(0, 8, match, 0)

    def delta(half):
        inverse = inverse_scale(t_sq[half], D_T)
        inverse = jnp.concatenate([inverse, inverse, inverse, inverse], axis=1)
        target = b["thid"][half] * inverse * tg[...]
        b["dl"][half, p] = ((b["diff"][half] - target) * (1.0 / math.sqrt(SLAB))).astype(BF)
        g_d[half].root(0)

    def gradient(half, plane, offs):
        def one(i, carry):
            q = ((z + offs[0] + i * offs[1]) % 4) * 2 + (yl + plane) % 2
            for at in range(2):
                rows = slice(at * 256, (at + 1) * 256)
                lhs = b["ng"][q, at, half * 128 : (half + 1) * 128, :]
                out[rows, :] += dot(lhs, b["dl"][half, q], ((0,), (0,)))
            return carry

        lax.fori_loop(0, offs[2], one, 0)

    own, near, far = (0, 1, 1), (1, 2, 2), (2, 1, 1)
    delta(0)
    delta(1)
    b["ng"][p, c] = b["nb"][2 * p + c]
    out[...] = jnp.zeros((512, 512), F32)
    g_d[0].mid(0)
    g_d[0].root(1)
    for made in n_tp:
        made.wait_recv()
    n_core.start()
    g_d[0].far(0)
    g_d[0].mid(1)
    n_core.wait_recv()
    gradient(0, 0, own)
    gradient(0, 0, near)
    gradient(0, 0, far)
    gradient(0, 1, own)
    g_d[1].mid(0)
    g_d[1].root(1)
    gradient(0, 1, near)
    g_d[0].far(1)
    gradient(0, 1, far)
    gradient(1, 0, own)
    gradient(1, 0, near)
    gradient(1, 1, own)
    g_d[1].far(0)
    g_d[1].mid(1)
    gradient(1, 0, far)
    gradient(1, 1, near)
    g_d[1].far(1)
    gradient(1, 1, far)
    wire.close()


def per_device(tq, tkv, sq, skv, doc, tres, tw, tg, sres, sw, sg, mp):
    V = pl.BlockSpec(memory_space=pltpu.VMEM)
    A = pl.BlockSpec(memory_space=pl.ANY)
    S = pl.BlockSpec(memory_space=pltpu.SMEM)
    return pl.pallas_call(
        kernel,
        out_shape=jax.ShapeDtypeStruct((512, 512), F32),
        in_specs=[S, V, A, V, A, V, A, V, V, A, V, A],
        out_specs=V,
        scratch_shapes=list(scratch_plan().values()),
        compiler_params=pltpu.CompilerParams(
            collective_id=0, has_side_effects=True, vmem_limit_bytes=63 * 1024 * 1024
        ),
    )(
        doc, tq, tkv, sq, skv, tres, tw, tg.reshape(1, -1), sres, sw, sg.reshape(1, -1), mp.reshape(8, 512, 512)
    )


def solution(mesh):
    in_specs = (
        P("seq", "tp"),
        P(None, "seq", "tp"),
        P("seq", "tp"),
        P(None, "seq", "tp"),
        P(),
        P("tp", "seq"),
        P("tp", "seq"),
        P("seq"),
        P("tp", "seq"),
        P("tp", "seq"),
        P("seq"),
        P(None, "seq"),
    )
    out_specs = P("tp", "seq")
    return jax.shard_map(per_device, mesh=mesh, in_specs=in_specs, out_specs=out_specs, check_vma=False)
```

```python
import math

import jax
import jax.numpy as jnp
from jax import lax
from jax.experimental import pallas as pl
from jax.experimental.pallas import tpu as pltpu
from jax.sharding import PartitionSpec as P

D_T = 8192
D_S = 4096
HEAD = 128
SLAB = 2048
CACHE = 10240
KEYS_CHIP = 1536
HIDDEN = -1e30
LOG2E = math.log2(math.e)
SCALE = LOG2E / math.sqrt(HEAD)
MESH = pl.DeviceIdType.MESH
BF = jnp.bfloat16
F32 = jnp.float32


class Wire:
    def __init__(self, send, recv):
        self.send, self.recv, self.made, self.left = send, recv, [], set()

    def copy(self, src, dst, dev):
        i = len(self.made)
        made = pltpu.make_async_remote_copy(
            src_ref=src, dst_ref=dst, send_sem=self.send.at[i], recv_sem=self.recv.at[i],
            device_id=dev, device_id_type=MESH,
        )
        self.made.append(made)
        return made

    def close(self, first=0, last=None):
        for i in range(first, len(self.made) if last is None else last):
            if i not in self.left:
                self.left.add(i)
                self.made[i].wait_send()


class Gather:
    def __init__(self, wire, block, right, left, across=None, core=None, planes=None):
        self.planes = planes or (1 if across is None else 2)
        self.core = core is not None
        self.cross = wire.copy(block(0, 0, None), block(0, 0, None), across) if across is not None else None
        self.right, self.left, self.on_right, self.on_left, self.pass_on = [], [], [], [], []
        for plane in range(self.planes):
            own = block(plane, 0, None)
            self.right.append(wire.copy(own, own, right))
            self.left.append(wire.copy(own, own, left))
            first, second = block(plane, 3, 0), block(plane, 1, 1)
            self.on_right.append(wire.copy(first, first, right))
            self.on_left.append(wire.copy(second, second, left))
            if self.core:
                refs = [own, block(plane, 3, None), block(plane, 1, None), block(plane, 2, None)]
                self.pass_on.append([wire.copy(ref, ref, core) for ref in refs])

    def root(self, plane, start_cross=True):
        if plane == 1 and self.cross is not None:
            self.cross.wait_recv()
        self.right[plane].start()
        self.left[plane].start()
        if plane == 0 and self.cross is not None and start_cross:
            self.cross.start()
        if self.core:
            self.pass_on[plane][0].start()

    def mid(self, plane):
        self.right[plane].wait_recv()
        self.on_right[plane].start()
        if self.core:
            self.pass_on[plane][1].start()
        self.left[plane].wait_recv()
        self.on_left[plane].start()
        if self.core:
            self.pass_on[plane][2].start()

    def far(self, plane):
        self.on_right[plane].wait_recv()
        self.on_left[plane].wait_recv()
        if self.core:
            self.pass_on[plane][3].start()

    def have_own(self, plane):
        self.pass_on[plane][0].wait_recv()

    def have_left(self, plane):
        self.pass_on[plane][1].wait_recv()

    def have_right(self, plane):
        self.pass_on[plane][2].wait_recv()

    def have_near(self, plane):
        self.have_left(plane)
        self.have_right(plane)

    def have_far(self, plane):
        self.pass_on[plane][3].wait_recv()


def dot(a, b, dims=((1,), (0,)), precision=None):
    return lax.dot_general(a, b, (dims, ((), ())), precision=precision, preferred_element_type=F32)


def scratch_plan():
    V = pltpu.VMEM
    D = pltpu.SemaphoreType.DMA
    return dict(
        kv=V((12, 2, 2, 768, 128), BF),
        kx=V((12, 2, 768, 256), BF),
        vt=V((12, 2, 144, 768), BF),
        score0=V((768, 512), F32),
        score1=V((768, 512), F32),
        top0=V((8, 512), F32),
        top1=V((8, 512), F32),
        qa=V((3, 2, 256, 512), BF),
        sq_in=V((128, 512), BF),
        tq_in=V((128, 1024), BF),
        to_out=V((2, 128, 512), BF),
        to_in=V((2, 128, 512), BF),
        tl_out=V((2, 8, 512), F32),
        tl_in=V((2, 8, 512), F32),
        m=V((3, 2, 8, 512), F32),
        acc=V((3, 2, 144, 512), F32),
        o_out=V((2, 128, 512), BF),
        o_in=V((2, 128, 512), BF),
        l_out=V((2, 8, 512), F32),
        l_in=V((2, 8, 512), F32),
        tctx=V((8, 2, 128, 1024), BF),
        sctx=V((8, 2, 128, 512), BF),
        tw=V((1024, 512), BF),
        sw=V((512, 256), BF),
        ty_out=V((2, 128, 512), BF),
        ty_in=V((2, 128, 512), BF),
        sy_out=V((256, 256), BF),
        sy_in=V((256, 256), BF),
        tpart=V((2, 4, 2, 128, 512), F32),
        spart=V((4, 2, 256, 256), F32),
        tr_out=V((2, 2, 128, 512), BF),
        tr_in=V((2, 2, 2, 64, 512), BF),
        sr_out=V((2, 256, 256), BF),
        sr_in=V((2, 2, 128, 256), BF),
        tz_out=V((2, 2, 2, 128, 512), BF),
        tz_in=V((2, 2, 2, 128, 512), BF),
        sz_out=V((2, 2, 256, 256), BF),
        sz_in=V((2, 2, 256, 256), BF),
        thid=V((2, 128, 512), F32),
        shid=V((256, 256), F32),
        tsq=V((2, 8, 8, 128), F32),
        ssq=V((8, 8, 256), F32),
        tsq_chip=V((2, 2, 8, 128), F32),
        ssq_chip=V((2, 8, 256), F32),
        nb=V((16, 256, 256), BF),
        ng=V((8, 2, 256, 256), BF),
        dl=V((2, 8, 128, 512), BF),
        diff=V((2, 128, 512), F32),
        wsend=D((200,)),
        wrecv=D((200,)),
        loc=D((8,)),
    )


def kernel(doc, tq, tkv_h, sq, skv_h, tres, tw_h, tg, sres, sw_h, sg, mp_h, out, *scratch):
    b = dict(zip(scratch_plan(), scratch))
    s = lax.axis_index("seq")
    p = lax.axis_index("tp")
    yh, x, c = s // 8, (s // 2) % 4, s % 2
    z, yl = p // 2, p % 2
    k_own = yh * 4 + x

    def seq_dev(plane, off, other):
        return ((((yh + plane) % 2) * 4 + (x + off) % 4) * 2 + (c + other) % 2, p)

    def tp_dev(plane, off):
        return (s, ((z + off) % 4) * 2 + (yl + plane) % 2)

    right, left, across, core = seq_dev(0, 1, 0), seq_dev(0, 3, 0), seq_dev(1, 0, 0), seq_dev(0, 0, 1)

    loads = [
        pltpu.make_async_copy(skv_h, b["kv"].at[x, c], b["loc"].at[0]),
        pltpu.make_async_copy(tkv_h, b["kv"].at[4 + k_own, c], b["loc"].at[1]),
        pltpu.make_async_copy(sw_h, b["sw"], b["loc"].at[2]),
        pltpu.make_async_copy(tw_h, b["tw"], b["loc"].at[3]),
    ]
    for load in loads:
        load.start()
    map_loads = [
        pltpu.make_async_copy(
            mp_h.at[:, :, pl.ds(u * 256, 256)], b["kx"].at[pl.ds(0, 8), u, pl.ds(0, 512)], b["loc"].at[4 + u]
        )
        for u in range(2)
    ]

    barrier = pltpu.get_barrier_semaphore()
    for off in range(1, 16):
        pl.semaphore_signal(barrier, inc=1, device_id=((s + off) % 16, p), device_id_type=MESH)
    for off in range(1, 8):
        pl.semaphore_signal(barrier, inc=1, device_id=(s, (p + off) % 8), device_id_type=MESH)

    wire = Wire(b["wsend"], b["wrecv"])
    give_sq = wire.copy(sq, b["sq_in"], across)
    give_tq = wire.copy(tq, b["tq_in"], core)

    def kv_block(model):
        def block(plane, off, part):
            at = (x + off) % 4 + model * (4 + ((yh + plane) % 2) * 4)
            if part is None:
                return b["kv"].at[at, c]
            return b["kv"].at[at, c, part]

        return block

    def s_block(plane, off, part):
        at = ((yh + plane) % 2) * 4 + (x + off) % 4
        if part is None:
            return b["sctx"].at[at, c]
        return b["sctx"].at[at, c, pl.ds(part * 64, 64)]

    def t_block(half):
        def block(plane, off, part):
            at = ((yh + plane) % 2) * 4 + (x + off) % 4
            if part is None:
                return b["tctx"].at[at, c, pl.ds(half * 64, 64)]
            return b["tctx"].at[at, c, pl.ds(half * 64 + part * 32, 32)]

        return block

    def nb_block(plane, off, part):
        at = (((yh + plane) % 2) * 4 + (x + off) % 4) * 2 + c
        if part is None:
            return b["nb"].at[at]
        return b["nb"].at[at, pl.ds(part * 128, 128)]

    def dl_block(half):
        def block(plane, off, part):
            at = ((z + off) % 4) * 2 + (yl + plane) % 2
            if part is None:
                return b["dl"].at[half, at]
            return b["dl"].at[half, at, pl.ds(part * 64, 64)]

        return block

    g_skv = Gather(wire, kv_block(0), right, left, None, core)
    g_tkv = Gather(wire, kv_block(1), right, left, across)
    keys_sent = len(wire.made)
    g_s = Gather(wire, s_block, right, left, None, core, 2)
    g_t = [Gather(wire, t_block(half), right, left, across, core) for half in range(2)]
    contexts_sent = len(wire.made)
    g_n = Gather(wire, nb_block, right, left, across, core)
    g_d = [Gather(wire, dl_block(half), tp_dev(0, 1), tp_dev(0, 3), tp_dev(1, 0), None) for half in range(2)]
    give_to = [wire.copy(b["to_out"].at[i], b["to_in"].at[i], core) for i in range(2)]
    give_tl = [wire.copy(b["tl_out"].at[i], b["tl_in"].at[i], core) for i in range(2)]
    give_o = [wire.copy(b["o_out"].at[1 - g], b["o_in"].at[g], across) for g in range(2)]
    give_l = [wire.copy(b["l_out"].at[1 - g], b["l_in"].at[g], across) for g in range(2)]
    def square_copies(chip, sq):
        between = wire.copy(chip.at[c], chip.at[c], core)
        offs = range(1, 8)
        spread = [wire.copy(sq.at[k_own], sq.at[k_own], (((k_own + off) % 8) * 2 + c, p)) for off in offs]
        return chip, sq, between, spread

    s_sq = square_copies(b["ssq_chip"], b["ssq"])
    t_sq = [square_copies(b["tsq_chip"].at[half], b["tsq"].at[half]) for half in range(2)]
    n_tp = [
        wire.copy(b["nb"].at[((p + off) % 8) * 2 + c], b["ng"].at[p, c], (s, (p + off) % 8)) for off in range(1, 8)
    ]
    n_core = wire.copy(b["ng"].at[:, c], b["ng"].at[:, c], core)

    qa, m, acc = b["qa"], b["m"], b["acc"]
    heads, tokens = (4, 8, 8), (128, 64, 64)

    def fill_queries(one, src, group):
        first = 64 * (one // 2)
        for i in range(4):
            if one == 0:
                held = src[:, i * 128 : (i + 1) * 128]
            else:
                pair = [src[first : first + 64, h * 128 : (h + 1) * 128] for h in (2 * i, 2 * i + 1)]
                held = jnp.concatenate(pair, axis=0)
            qa[one, group, 0:128, i * 128 : (i + 1) * 128] = held.T

    def prepare(first, last, passes):
        rows = lax.broadcasted_iota(jnp.int32, (128, 128), 0)
        lanes = lax.broadcasted_iota(jnp.int32, (128, 128), 1)
        for one in passes:
            eye = jnp.where(lanes % tokens[one] + 64 * (one // 2) == rows, 1.0, 0.0).astype(BF)
            for g in range(2):
                for i in range(4):
                    qa[one, g, 128:256, i * 128 : (i + 1) * 128] = eye
            m[one] = jnp.full((2, 8, 512), HIDDEN, F32)
            acc[one] = jnp.zeros((2, 144, 512), F32)

        def extra(i, carry):
            b["kx"][i, :, :, 128:256] = jnp.zeros((2, 768, 128), BF)
            b["vt"][i, :, 128:144, :] = jnp.ones((2, 16, 768), BF)
            return carry

        lax.fori_loop(first, last, extra, 0)

    first_key = doc[0]

    def tile_at(n):
        third = n // 8
        t = (third + 1) // 2
        other = third // 2
        one = t * (1 + (1 - other) * ((n % 8) // 4) + other * (n % 2))
        i = (1 - t + other) * ((n % 8) // 2) + (t - other) * (n % 4)
        plane = (yh + other) % 2
        at = (x + 3 * i + 3 * (i // 2) + 2 * (i // 3)) % 4
        return one, t, t * (4 + plane * 4) + at, plane, at, (c + (1 - t) * (n % 2)) % 2

    def build(n, g):
        one, t, block, plane, at, from_core = tile_at(n)
        base = (plane * 4 + at) * KEYS_CHIP + from_core * 768

        if g == 0:

            @pl.when(one <= 1)
            def _():
                b["vt"][block, from_core, 0:128, :] = b["kv"][block, from_core, 1].T
                b["kx"][block, from_core, :, 0:128] = b["kv"][block, from_core, 0]

                @pl.when(plane == 0)
                def _():
                    key = lax.broadcasted_iota(jnp.int32, (768, 128), 0)
                    b["kx"][block, from_core, :, 128:256] = jnp.where(key >= first_key - base, 0.0, HIDDEN).astype(BF)

        @pl.when((plane == 1) & (at >= 2))
        def _():
            ahead = CACHE + ((((yh + (1 - t) * g) % 2) * 4 + x) * 2 + (c + t * g) % 2) * 128 - base
            key = lax.broadcasted_iota(jnp.int32, (768, 128), 0)
            row = lax.broadcasted_iota(jnp.int32, (768, 128), 1)
            b["kx"][block, from_core, :, 128:256] = jnp.where(key - row <= ahead, 0.0, HIDDEN).astype(BF)

    scores, tops = (b["score0"], b["score1"]), (b["top0"], b["top1"])

    def overlapped(n, u, weigh_n, weigh=True):
        one, _, block, _, _, from_core = tile_at(n)
        queries = qa[one, u]
        top = jnp.full((8, 512), HIDDEN, F32)
        if weigh:
            w_one, _, w_block, _, _, w_core = tile_at(weigh_n)
            w_g = 1 - u
            old = m[w_one, w_g]
            peak = jnp.max(tops[1 - u][...], axis=0, keepdims=True)
            new = jnp.maximum(old, jnp.broadcast_to(peak, (8, 512)))
            total = (acc[w_one, w_g].reshape(18, 8, 512) * jnp.exp2((old - new) * SCALE)[None]).reshape(144, 512)
        for j in range(3):
            keys = slice(j * 256, (j + 1) * 256)
            fresh = dot(b["kx"][block, from_core, keys, :], queries)
            scores[u][keys, :] = fresh
            top = jnp.maximum(top, jnp.max(fresh.reshape(32, 8, 512), axis=0))
            if weigh:
                held = scores[1 - u][keys, :].reshape(32, 8, 512)
                weights = jnp.exp2((held - new[None]) * SCALE).reshape(256, 512).astype(BF)
                total = total + dot(b["vt"][w_block, w_core, :, keys], weights)
        tops[u][...] = top
        if weigh:
            m[w_one, w_g] = new
            acc[w_one, w_g] = total

    def attention(hooks):
        build(0, 0)
        overlapped(0, 0, 0, weigh=False)

        def step(n, carry):
            for at_step, hook in hooks.items():
                pl.when(n == at_step)(hook)
            build(n, 1)
            overlapped(n, 1, n)
            after = (n + 1) % 24
            build(after, 0)
            overlapped(after, 0, n)
            return carry

        lax.fori_loop(0, 24, step, 0)

    def part_of(one, g):
        total = acc[one, g, 128:136, :]
        mean = (acc[one, g, 0:128, :].reshape(16, 8, 512) * (1.0 / total)[None]).reshape(128, 512)
        return mean, m[one, g] * SCALE + jnp.log(total) * LOG2E

    def partner_part():
        for g in (1, 0):
            mean, logs = part_of(0, g)
            b["o_out"][g] = mean.astype(BF)
            b["l_out"][g] = logs
            give_o[1 - g].start()
            give_l[1 - g].start()

    def keep_context(one, plane, both, ctx):
        both = both.T.astype(BF)
        count, first = tokens[one], 64 * (one // 2)
        for h in range(heads[one]):
            held = both[h * count : (h + 1) * count, :]
            ctx[plane * 4 + x, c, first : first + count, h * 128 : (h + 1) * 128] = held

    def joined(one, g, o_in, l_in):
        mine, log_mine = part_of(one, g)
        share = 1.0 / (1.0 + jnp.exp2(log_mine - l_in[...]))
        other = o_in[...].astype(F32)
        return mine + ((other - mine).reshape(16, 8, 512) * share[None]).reshape(128, 512)

    def s_context(g):
        give_o[g].wait_recv()
        give_l[g].wait_recv()
        keep_context(0, (yh + g) % 2, joined(0, g, b["o_in"].at[g], b["l_in"].at[g]), b["sctx"])
        g_s.root(g)

    def t_part(half):
        mean, logs = part_of(1 + half, 1)
        b["to_out"][half] = mean.astype(BF)
        b["tl_out"][half] = logs
        give_to[half].start()
        give_tl[half].start()

    def t_context(half):
        give_to[half].wait_recv()
        give_tl[half].wait_recv()
        keep_context(1 + half, yh, joined(1 + half, 0, b["to_in"].at[half], b["tl_in"].at[half]), b["tctx"])
        g_t[half].root(0)

    class Reduce:
        def __init__(self, ctx, w, name, half):
            self.ctx, self.w, self.half = ctx, w, half

            def of(key):
                return b[name + key] if half is None else b[name + key].at[half]

            self.y_out, self.y_in, self.part, self.hid = of("y_out"), of("y_in"), of("part"), of("hid")
            self.r_out, self.r_in, self.z_out, self.z_in = of("r_out"), of("r_in"), of("z_out"), of("z_in")
            self.rows = self.part.shape[2] // 2
            near = (tp_dev(0, 3), tp_dev(0, 1))
            self.relay = [
                wire.copy(self.r_out.at[:, pl.ds(i * self.rows, self.rows)], self.r_in.at[i], near[i]) for i in range(2)
            ]
            self.along = [wire.copy(self.z_out.at[i], self.z_in.at[i], near[i]) for i in range(2)]
            self.beside = wire.copy(self.y_out, self.y_in, tp_dev(1, 0))

        def multiply(self, first, last, waits):
            def pair(j, carry):
                for at, wait in waits.items():
                    pl.when(j == at)(wait)
                zd = ((yh + j // 2) % 2) * 2 + (x // 2 + j % 2) % 2

                both = pl.ds(zd * 2, 2)
                if self.half is None:
                    held = self.ctx[both]
                else:
                    held = self.ctx[both, :, self.half * 64 : self.half * 64 + 64]
                done = dot(held.reshape(-1, held.shape[3]), self.w[...])
                self.part[zd] = done.reshape(2, -1, done.shape[1])

                @pl.when(zd == (z + 2) % 4)
                def _():
                    self.r_out[...] = self.part[zd].astype(BF)
                    self.relay[0].start()
                    self.relay[1].start()

                return carry

            lax.fori_loop(first, last, pair, 0)

        def send_on(self):
            for i, zd in enumerate(((z + 3) % 4, (z + 1) % 4)):
                mid = slice(i * self.rows, (i + 1) * self.rows)
                rest = slice((1 - i) * self.rows, (2 - i) * self.rows)
                self.z_out[i, :, rest, :] = self.part[zd, :, rest, :].astype(BF)
                self.relay[i].wait_recv()
                self.z_out[i, :, mid, :] = (self.part[zd, :, mid, :] + self.r_in[i].astype(F32)).astype(BF)
                self.along[i].start()

        def settle(self):
            self.along[0].wait_recv()
            self.along[1].wait_recv()

            def block(u):
                return self.part[z, u] + self.z_in[0, u].astype(F32) + self.z_in[1, u].astype(F32)

            self.y_out[...] = block(1 - yl).astype(BF)
            self.beside.start()
            self.hid[...] = block(yl)

        def finish(self, resid):
            if self.half is None:
                own = resid[...]
            else:
                first = self.half * 64
                own = jnp.concatenate([resid[first : first + 64, :], resid[first + 128 : first + 192, :]], axis=0)
            total = self.hid[...] + own.astype(F32)
            self.beside.wait_recv()
            self.hid[...] = total + self.y_in[...].astype(F32)

    def send_squares(hid, squares):
        chip, sq, between, spread = squares
        value = hid[...]
        ones = jnp.ones((8, value.shape[1]), F32)
        chip[c] = dot(ones, value * value, ((1,), (1,)), lax.Precision.HIGHEST)
        between.start()
        between.wait_recv()
        sq[k_own] = chip[0] + chip[1]
        for made in spread:
            made.start()

    def inverse_scale(squares, width):
        _, sq, _, spread = squares
        for made in spread:
            made.wait_recv()
        total = sq[0]
        for i in range(1, 8):
            total = total + sq[i]
        first = jnp.where(lax.broadcasted_iota(jnp.int32, (8, 128), 0) == 0, 1.0, 0.0)
        column = dot(total, first, ((0,), (0,)), lax.Precision.HIGHEST)
        return 1.0 / jnp.sqrt(column * (1.0 / width) + 1e-05)

    r_s = Reduce(b["sctx"], b["sw"], "s", None)
    r_t = [Reduce(b["tctx"], b["tw"], "t", half) for half in range(2)]

    def ready(gather, plane):
        gather.have_own(plane)
        gather.have_near(plane)
        gather.have_far(plane)

    fill_queries(0, sq, 0)
    prepare(0, 4, (0,))
    loads[0].wait()
    loads[1].wait()
    pl.semaphore_wait(barrier, 22)
    g_skv.root(0)
    give_sq.start()
    give_tq.start()
    g_tkv.cross.start()

    def s_partner():
        g_skv.have_own(0)
        give_sq.wait_recv()
        fill_queries(0, b["sq_in"], 1)

    def s_near():
        prepare(4, 12, (1, 2))
        fill_queries(1, tq, 0)
        fill_queries(2, tq, 0)
        give_tq.wait_recv()
        fill_queries(1, b["tq_in"], 1)
        fill_queries(2, b["tq_in"], 1)
        g_skv.mid(0)
        g_tkv.root(0, False)

    def t_start():
        partner_part()
        g_tkv.mid(0)
        g_tkv.root(1)

    def s_sums():
        for load in loads[2:]:
            load.wait()
        r_s.multiply(0, 4, {0: lambda: ready(g_s, 0), 2: lambda: ready(g_s, 1)})

    def s_squares():
        r_s.finish(sres)
        send_squares(b["shid"], s_sq)

    def s_normed():
        inverse = inverse_scale(s_sq, D_S)
        inverse = jnp.concatenate([inverse, inverse], axis=1)
        normed = (b["shid"][...] * inverse * sg[...]).astype(BF)
        for at, first in enumerate((0, 128, 64, 192)):
            b["nb"][s, at * 64 : (at + 1) * 64, :] = normed[first : first + 64, :]
        g_n.root(0)

    def t1_sums():
        r_t[0].multiply(0, 4, {0: lambda: ready(g_t[0], 0), 2: lambda: ready(g_t[0], 1)})

    def both(*hooks):
        def run():
            for hook in hooks:
                hook()

        return run

    attention(
        {
            0: s_partner,
            1: s_near,
            2: lambda: g_skv.have_left(0),
            4: lambda: g_skv.have_right(0),
            5: lambda: g_skv.far(0),
            6: lambda: g_skv.have_far(0),
            8: t_start,
            10: lambda: g_tkv.far(0),
            12: lambda: s_context(0),
            16: lambda: s_context(1),
            17: lambda: g_tkv.mid(1),
            18: lambda: g_s.mid(0),
            20: both(lambda: g_s.mid(1), lambda: g_s.far(0)),
            21: lambda: g_tkv.far(1),
            22: lambda: g_s.far(1),
            23: lambda: t_part(0),
        }
    )
    for load in map_loads:
        load.start()
    t_part(1)
    t_context(0)
    t_context(1)
    s_sums()
    r_s.send_on()
    g_t[0].mid(0)
    g_t[0].root(1)
    g_t[1].mid(0)
    g_t[1].root(1)
    wire.close(0, keys_sent)
    g_t[0].far(0)
    g_t[0].mid(1)
    r_s.settle()
    g_t[0].far(1)
    t1_sums()
    g_t[1].far(0)
    g_t[1].mid(1)
    s_squares()
    g_t[1].far(1)
    r_t[0].send_on()
    r_t[1].multiply(0, 4, {0: lambda: ready(g_t[1], 0), 2: lambda: ready(g_t[1], 1)})
    s_normed()
    r_t[1].send_on()
    r_t[0].settle()
    g_n.mid(0)
    g_n.root(1)
    r_t[0].finish(tres)
    send_squares(b["thid"].at[0], t_sq[0])
    g_n.far(0)
    g_n.mid(1)
    b["diff"][...] = jnp.zeros((2, 128, 512), F32)
    for load in map_loads:
        load.wait()

    def match(plane):
        def one(i, carry):
            k = ((yh + plane) % 2) * 4 + i
            lhs = jnp.concatenate([b["nb"][2 * k], b["nb"][2 * k + 1]], axis=1)
            for u in range(2):
                b["diff"][:, :, u * 256 : (u + 1) * 256] += dot(lhs, b["kx"][k, u, 0:512, :]).reshape(2, 128, 256)
            return carry

        lax.fori_loop(0, 4, one, 0)

    def delta(half):
        inverse = inverse_scale(t_sq[half], D_T)
        inverse = jnp.concatenate([inverse, inverse, inverse, inverse], axis=1)
        target = b["thid"][half] * inverse * tg[...]
        b["dl"][half, p] = ((b["diff"][half] - target) * (1.0 / math.sqrt(SLAB))).astype(BF)
        g_d[half].root(0)

    def gradient(plane, offs):
        def one(i, carry):
            q = ((z + offs[0] + i * offs[1]) % 4) * 2 + (yl + plane) % 2
            deltas = b["dl"][:, q].reshape(256, 512)
            for at in range(2):
                out[at * 256 : (at + 1) * 256, :] += dot(b["ng"][q, at], deltas, ((0,), (0,)))
            return carry

        lax.fori_loop(0, offs[2], one, 0)

    own, near, far = (0, 1, 1), (1, 2, 2), (2, 1, 1)
    ready(g_n, 0)
    match(0)
    r_t[1].settle()
    g_n.far(1)
    for made in n_tp:
        made.start()
    ready(g_n, 1)
    match(1)
    delta(0)
    r_t[1].finish(tres)
    send_squares(b["thid"].at[1], t_sq[1])
    b["ng"][p, c] = b["nb"][2 * p + c]
    out[...] = jnp.zeros((512, 512), F32)
    delta(1)
    for half in range(2):
        g_d[half].mid(0)
        g_d[half].root(1)
    for made in n_tp:
        made.wait_recv()
    n_core.start()
    for half in range(2):
        g_d[half].far(0)
        g_d[half].mid(1)
    wire.close(keys_sent, contexts_sent)
    n_core.wait_recv()
    gradient(0, own)
    gradient(0, near)
    gradient(0, far)
    gradient(1, own)
    gradient(1, near)
    for half in range(2):
        g_d[half].far(1)
    gradient(1, far)
    wire.close()


def per_device(tq, tkv, sq, skv, doc, tres, tw, tg, sres, sw, sg, mp):
    V = pl.BlockSpec(memory_space=pltpu.VMEM)
    A = pl.BlockSpec(memory_space=pl.ANY)
    S = pl.BlockSpec(memory_space=pltpu.SMEM)
    return pl.pallas_call(
        kernel,
        out_shape=jax.ShapeDtypeStruct((512, 512), F32),
        in_specs=[S, V, A, V, A, V, A, V, V, A, V, A],
        out_specs=V,
        scratch_shapes=list(scratch_plan().values()),
        compiler_params=pltpu.CompilerParams(
            collective_id=0, has_side_effects=True, vmem_limit_bytes=63 * 1024 * 1024
        ),
    )(
        doc, tq, tkv, sq, skv, tres, tw, tg.reshape(1, -1), sres, sw, sg.reshape(1, -1), mp.reshape(8, 512, 512)
    )


def solution(mesh):
    in_specs = (
        P("seq", "tp"),
        P(None, "seq", "tp"),
        P("seq", "tp"),
        P(None, "seq", "tp"),
        P(),
        P("tp", "seq"),
        P("tp", "seq"),
        P("seq"),
        P("tp", "seq"),
        P("tp", "seq"),
        P("seq"),
        P(None, "seq"),
    )
    out_specs = P("tp", "seq")
    return jax.shard_map(per_device, mesh=mesh, in_specs=in_specs, out_specs=out_specs, check_vma=False)
```

```python
import math

import jax
import jax.numpy as jnp
from jax import lax
from jax.experimental import pallas as pl
from jax.experimental.pallas import tpu as pltpu
from jax.sharding import PartitionSpec as P

D_T = 8192
D_S = 4096
HEAD = 128
SLAB = 2048
CACHE = 10240
KEYS_CHIP = 1536
HIDDEN = -1e30
LOG2E = math.log2(math.e)
SCALE = LOG2E / math.sqrt(HEAD)
MESH = pl.DeviceIdType.MESH
BF = jnp.bfloat16
F32 = jnp.float32


class Wire:
    def __init__(self, send, recv):
        self.send, self.recv, self.made, self.left = send, recv, [], set()

    def copy(self, src, dst, dev):
        i = len(self.made)
        made = pltpu.make_async_remote_copy(
            src_ref=src, dst_ref=dst, send_sem=self.send.at[i], recv_sem=self.recv.at[i],
            device_id=dev, device_id_type=MESH,
        )
        self.made.append(made)
        return made

    def close(self, first=0, last=None):
        for i in range(first, len(self.made) if last is None else last):
            if i not in self.left:
                self.left.add(i)
                self.made[i].wait_send()


class Gather:
    def __init__(self, wire, block, right, left, across=None, core=None, planes=None):
        self.planes = planes or (1 if across is None else 2)
        self.core = core is not None
        self.cross = wire.copy(block(0, 0, None), block(0, 0, None), across) if across is not None else None
        self.right, self.left, self.on_right, self.on_left, self.pass_on = [], [], [], [], []
        for plane in range(self.planes):
            own = block(plane, 0, None)
            self.right.append(wire.copy(own, own, right))
            self.left.append(wire.copy(own, own, left))
            first, second = block(plane, 3, 0), block(plane, 1, 1)
            self.on_right.append(wire.copy(first, first, right))
            self.on_left.append(wire.copy(second, second, left))
            if self.core:
                refs = [own, block(plane, 3, None), block(plane, 1, None), block(plane, 2, None)]
                self.pass_on.append([wire.copy(ref, ref, core) for ref in refs])

    def root(self, plane, start_cross=True):
        if plane == 1 and self.cross is not None:
            self.cross.wait_recv()
        self.right[plane].start()
        self.left[plane].start()
        if plane == 0 and self.cross is not None and start_cross:
            self.cross.start()
        if self.core:
            self.pass_on[plane][0].start()

    def mid(self, plane):
        self.right[plane].wait_recv()
        self.on_right[plane].start()
        if self.core:
            self.pass_on[plane][1].start()
        self.left[plane].wait_recv()
        self.on_left[plane].start()
        if self.core:
            self.pass_on[plane][2].start()

    def far(self, plane):
        self.on_right[plane].wait_recv()
        self.on_left[plane].wait_recv()
        if self.core:
            self.pass_on[plane][3].start()

    def have_own(self, plane):
        self.pass_on[plane][0].wait_recv()

    def have_left(self, plane):
        self.pass_on[plane][1].wait_recv()

    def have_right(self, plane):
        self.pass_on[plane][2].wait_recv()

    def have_near(self, plane):
        self.have_left(plane)
        self.have_right(plane)

    def have_far(self, plane):
        self.pass_on[plane][3].wait_recv()


def dot(a, b, dims=((1,), (0,)), precision=None):
    return lax.dot_general(a, b, (dims, ((), ())), precision=precision, preferred_element_type=F32)


def scratch_plan():
    V = pltpu.VMEM
    D = pltpu.SemaphoreType.DMA
    return dict(
        kv=V((12, 2, 2, 768, 128), BF),
        kx=V((12, 2, 768, 256), BF),
        vt=V((12, 2, 144, 768), BF),
        score0=V((768, 512), F32),
        score1=V((768, 512), F32),
        top0=V((8, 512), F32),
        top1=V((8, 512), F32),
        qa=V((3, 2, 256, 512), BF),
        sq_in=V((128, 512), BF),
        tq_in=V((128, 1024), BF),
        to_out=V((2, 128, 512), BF),
        to_in=V((2, 128, 512), BF),
        tl_out=V((2, 8, 512), F32),
        tl_in=V((2, 8, 512), F32),
        m=V((3, 2, 8, 512), F32),
        acc=V((3, 2, 144, 512), F32),
        o_out=V((2, 128, 512), BF),
        o_in=V((2, 128, 512), BF),
        l_out=V((2, 8, 512), F32),
        l_in=V((2, 8, 512), F32),
        tctx=V((8, 2, 128, 1024), BF),
        sctx=V((8, 2, 128, 512), BF),
        tw=V((1024, 512), BF),
        sw=V((512, 256), BF),
        ty_out=V((2, 128, 512), BF),
        ty_in=V((2, 128, 512), BF),
        sy_out=V((256, 256), BF),
        sy_in=V((256, 256), BF),
        tpart=V((2, 4, 2, 128, 512), F32),
        spart=V((4, 2, 256, 256), F32),
        tr_out=V((2, 2, 128, 512), BF),
        tr_in=V((2, 2, 2, 64, 512), BF),
        sr_out=V((2, 256, 256), BF),
        sr_in=V((2, 2, 128, 256), BF),
        tz_out=V((2, 2, 2, 128, 512), BF),
        tz_in=V((2, 2, 2, 128, 512), BF),
        sz_out=V((2, 2, 256, 256), BF),
        sz_in=V((2, 2, 256, 256), BF),
        thid=V((2, 128, 512), F32),
        shid=V((256, 256), F32),
        tsq=V((2, 8, 8, 128), F32),
        ssq=V((8, 8, 256), F32),
        tsq_chip=V((2, 2, 8, 128), F32),
        ssq_chip=V((2, 8, 256), F32),
        nb=V((16, 256, 256), BF),
        ng=V((8, 2, 256, 256), BF),
        dl=V((2, 8, 128, 512), BF),
        diff=V((2, 128, 512), F32),
        nts=D((8,)),
        ntr=D((8,)),
        wsend=D((200,)),
        wrecv=D((200,)),
        loc=D((8,)),
    )


def kernel(doc, tq, tkv_h, sq, skv_h, tres, tw_h, tg, sres, sw_h, sg, mp_h, out, *scratch):
    b = dict(zip(scratch_plan(), scratch))
    s = lax.axis_index("seq")
    p = lax.axis_index("tp")
    yh, x, c = s // 8, (s // 2) % 4, s % 2
    z, yl = p // 2, p % 2
    k_own = yh * 4 + x

    def seq_dev(plane, off, other):
        return ((((yh + plane) % 2) * 4 + (x + off) % 4) * 2 + (c + other) % 2, p)

    def tp_dev(plane, off):
        return (s, ((z + off) % 4) * 2 + (yl + plane) % 2)

    right, left, across, core = seq_dev(0, 1, 0), seq_dev(0, 3, 0), seq_dev(1, 0, 0), seq_dev(0, 0, 1)

    loads = [
        pltpu.make_async_copy(skv_h, b["kv"].at[x, c], b["loc"].at[0]),
        pltpu.make_async_copy(tkv_h, b["kv"].at[4 + k_own, c], b["loc"].at[1]),
        pltpu.make_async_copy(sw_h, b["sw"], b["loc"].at[2]),
        pltpu.make_async_copy(tw_h, b["tw"], b["loc"].at[3]),
    ]
    for load in loads:
        load.start()
    map_loads = [
        pltpu.make_async_copy(
            mp_h.at[:, :, pl.ds(u * 256, 256)], b["kx"].at[pl.ds(0, 8), u, pl.ds(0, 512)], b["loc"].at[4 + u]
        )
        for u in range(2)
    ]

    barrier = pltpu.get_barrier_semaphore()
    for off in range(1, 16):
        pl.semaphore_signal(barrier, inc=1, device_id=((s + off) % 16, p), device_id_type=MESH)
    for off in range(1, 8):
        pl.semaphore_signal(barrier, inc=1, device_id=(s, (p + off) % 8), device_id_type=MESH)

    wire = Wire(b["wsend"], b["wrecv"])
    give_sq = wire.copy(sq, b["sq_in"], across)
    give_tq = wire.copy(tq, b["tq_in"], core)

    def kv_block(model):
        def block(plane, off, part):
            at = (x + off) % 4 + model * (4 + ((yh + plane) % 2) * 4)
            if part is None:
                return b["kv"].at[at, c]
            return b["kv"].at[at, c, part]

        return block

    def s_block(plane, off, part):
        at = ((yh + plane) % 2) * 4 + (x + off) % 4
        if part is None:
            return b["sctx"].at[at, c]
        return b["sctx"].at[at, c, pl.ds(part * 64, 64)]

    def t_block(half):
        def block(plane, off, part):
            at = ((yh + plane) % 2) * 4 + (x + off) % 4
            if part is None:
                return b["tctx"].at[at, c, pl.ds(half * 64, 64)]
            return b["tctx"].at[at, c, pl.ds(half * 64 + part * 32, 32)]

        return block

    def nb_block(plane, off, part):
        at = (((yh + plane) % 2) * 4 + (x + off) % 4) * 2 + c
        if part is None:
            return b["nb"].at[at]
        return b["nb"].at[at, pl.ds(part * 128, 128)]

    def dl_block(half):
        def block(plane, off, part):
            at = ((z + off) % 4) * 2 + (yl + plane) % 2
            if part is None:
                return b["dl"].at[half, at]
            return b["dl"].at[half, at, pl.ds(part * 64, 64)]

        return block

    g_skv = Gather(wire, kv_block(0), right, left, None, core)
    g_tkv = Gather(wire, kv_block(1), right, left, across)
    keys_sent = len(wire.made)
    g_s = Gather(wire, s_block, right, left, None, core, 2)
    g_t = [Gather(wire, t_block(half), right, left, across, core) for half in range(2)]
    contexts_sent = len(wire.made)
    g_n = Gather(wire, nb_block, right, left, across, core)
    g_d = [Gather(wire, dl_block(half), tp_dev(0, 1), tp_dev(0, 3), tp_dev(1, 0), None) for half in range(2)]
    give_to = [wire.copy(b["to_out"].at[i], b["to_in"].at[i], core) for i in range(2)]
    give_tl = [wire.copy(b["tl_out"].at[i], b["tl_in"].at[i], core) for i in range(2)]
    give_o = [wire.copy(b["o_out"].at[1 - g], b["o_in"].at[g], across) for g in range(2)]
    give_l = [wire.copy(b["l_out"].at[1 - g], b["l_in"].at[g], across) for g in range(2)]
    def square_copies(chip, sq):
        between = wire.copy(chip.at[c], chip.at[c], core)
        offs = range(1, 8)
        spread = [wire.copy(sq.at[k_own], sq.at[k_own], (((k_own + off) % 8) * 2 + c, p)) for off in offs]
        return chip, sq, between, spread

    s_sq = square_copies(b["ssq_chip"], b["ssq"])
    t_sq = [square_copies(b["tsq_chip"].at[half], b["tsq"].at[half]) for half in range(2)]
    def give_normed(q):
        return pltpu.make_async_remote_copy(
            src_ref=b["nb"].at[q * 2 + c], dst_ref=b["ng"].at[p, c], send_sem=b["nts"].at[q], recv_sem=b["ntr"].at[p],
            device_id=(s, q), device_id_type=MESH,
        )

    def start_normed(plane):
        for i in range(4):
            q = ((yh + plane) % 2) * 4 + i
            pl.when(q != p)(lambda q=q: give_normed(q).start())

    def have_normed():
        for off in range(1, 8):
            q = (p + off) % 8
            pltpu.make_async_remote_copy(
                src_ref=b["ng"].at[q, c], dst_ref=b["ng"].at[q, c], send_sem=b["nts"].at[q],
                recv_sem=b["ntr"].at[q], device_id=(s, q), device_id_type=MESH,
            ).wait_recv()

    def close_normed():
        for off in range(1, 8):
            give_normed((p + off) % 8).wait_send()

    n_core = wire.copy(b["ng"].at[:, c], b["ng"].at[:, c], core)

    qa, m, acc = b["qa"], b["m"], b["acc"]
    heads, tokens = (4, 8, 8), (128, 64, 64)

    def fill_queries(one, src, group):
        first = 64 * (one // 2)
        for i in range(4):
            if one == 0:
                held = src[:, i * 128 : (i + 1) * 128]
            else:
                pair = [src[first : first + 64, h * 128 : (h + 1) * 128] for h in (2 * i, 2 * i + 1)]
                held = jnp.concatenate(pair, axis=0)
            qa[one, group, 0:128, i * 128 : (i + 1) * 128] = held.T

    def prepare(first, last, passes):
        rows = lax.broadcasted_iota(jnp.int32, (128, 128), 0)
        lanes = lax.broadcasted_iota(jnp.int32, (128, 128), 1)
        for one in passes:
            eye = jnp.where(lanes % tokens[one] + 64 * (one // 2) == rows, 1.0, 0.0).astype(BF)
            for g in range(2):
                for i in range(4):
                    qa[one, g, 128:256, i * 128 : (i + 1) * 128] = eye
            m[one] = jnp.full((2, 8, 512), HIDDEN, F32)
            acc[one] = jnp.zeros((2, 144, 512), F32)

        def extra(i, carry):
            b["kx"][i, :, :, 128:256] = jnp.zeros((2, 768, 128), BF)
            b["vt"][i, :, 128:144, :] = jnp.ones((2, 16, 768), BF)
            return carry

        lax.fori_loop(first, last, extra, 0)

    first_key = doc[0]

    def tile_at(n):
        third = n // 8
        t = (third + 1) // 2
        other = third // 2
        one = t * (1 + (1 - other) * ((n % 8) // 4) + other * (n % 2))
        i = (1 - t + other) * ((n % 8) // 2) + (t - other) * (n % 4)
        plane = (yh + other) % 2
        at = (x + 3 * i + 3 * (i // 2) + 2 * (i // 3)) % 4
        return one, t, t * (4 + plane * 4) + at, plane, at, (c + (1 - t) * (n % 2)) % 2

    def build(n, g):
        one, t, block, plane, at, from_core = tile_at(n)
        base = (plane * 4 + at) * KEYS_CHIP + from_core * 768

        if g == 0:

            @pl.when(one <= 1)
            def _():
                b["vt"][block, from_core, 0:128, :] = b["kv"][block, from_core, 1].T
                b["kx"][block, from_core, :, 0:128] = b["kv"][block, from_core, 0]

                @pl.when(plane == 0)
                def _():
                    key = lax.broadcasted_iota(jnp.int32, (768, 128), 0)
                    b["kx"][block, from_core, :, 128:256] = jnp.where(key >= first_key - base, 0.0, HIDDEN).astype(BF)

        @pl.when((plane == 1) & (at >= 2))
        def _():
            ahead = CACHE + ((((yh + (1 - t) * g) % 2) * 4 + x) * 2 + (c + t * g) % 2) * 128 - base
            key = lax.broadcasted_iota(jnp.int32, (768, 128), 0)
            row = lax.broadcasted_iota(jnp.int32, (768, 128), 1)
            b["kx"][block, from_core, :, 128:256] = jnp.where(key - row <= ahead, 0.0, HIDDEN).astype(BF)

    scores, tops = (b["score0"], b["score1"]), (b["top0"], b["top1"])

    def overlapped(n, u, weigh_n, weigh=True):
        one, _, block, _, _, from_core = tile_at(n)
        queries = qa[one, u]
        top = jnp.full((8, 512), HIDDEN, F32)
        if weigh:
            w_one, _, w_block, _, _, w_core = tile_at(weigh_n)
            w_g = 1 - u
            old = m[w_one, w_g]
            peak = jnp.max(tops[1 - u][...], axis=0, keepdims=True)
            new = jnp.maximum(old, jnp.broadcast_to(peak, (8, 512)))
            total = (acc[w_one, w_g].reshape(18, 8, 512) * jnp.exp2((old - new) * SCALE)[None]).reshape(144, 512)
        for j in range(3):
            keys = slice(j * 256, (j + 1) * 256)
            fresh = dot(b["kx"][block, from_core, keys, :], queries)
            scores[u][keys, :] = fresh
            top = jnp.maximum(top, jnp.max(fresh.reshape(32, 8, 512), axis=0))
            if weigh:
                held = scores[1 - u][keys, :].reshape(32, 8, 512)
                weights = jnp.exp2((held - new[None]) * SCALE).reshape(256, 512).astype(BF)
                total = total + dot(b["vt"][w_block, w_core, :, keys], weights)
        tops[u][...] = top
        if weigh:
            m[w_one, w_g] = new
            acc[w_one, w_g] = total

    def attention(hooks):
        build(0, 0)
        overlapped(0, 0, 0, weigh=False)

        def step(n, carry):
            for at_step, hook in hooks.items():
                pl.when(n == at_step)(hook)
            build(n, 1)
            overlapped(n, 1, n)
            after = (n + 1) % 24
            build(after, 0)
            overlapped(after, 0, n)
            return carry

        lax.fori_loop(0, 24, step, 0)

    def part_of(one, g):
        total = acc[one, g, 128:136, :]
        mean = (acc[one, g, 0:128, :].reshape(16, 8, 512) * (1.0 / total)[None]).reshape(128, 512)
        return mean, m[one, g] * SCALE + jnp.log(total) * LOG2E

    def partner_part():
        for g in (1, 0):
            mean, logs = part_of(0, g)
            b["o_out"][g] = mean.astype(BF)
            b["l_out"][g] = logs
            give_o[1 - g].start()
            give_l[1 - g].start()

    def keep_context(one, plane, both, ctx):
        both = both.T.astype(BF)
        count, first = tokens[one], 64 * (one // 2)
        for h in range(heads[one]):
            held = both[h * count : (h + 1) * count, :]
            ctx[plane * 4 + x, c, first : first + count, h * 128 : (h + 1) * 128] = held

    def joined(one, g, o_in, l_in):
        mine, log_mine = part_of(one, g)
        share = 1.0 / (1.0 + jnp.exp2(log_mine - l_in[...]))
        other = o_in[...].astype(F32)
        return mine + ((other - mine).reshape(16, 8, 512) * share[None]).reshape(128, 512)

    def s_context(g):
        give_o[g].wait_recv()
        give_l[g].wait_recv()
        keep_context(0, (yh + g) % 2, joined(0, g, b["o_in"].at[g], b["l_in"].at[g]), b["sctx"])
        g_s.root(g)

    def t_part(half):
        mean, logs = part_of(1 + half, 1)
        b["to_out"][half] = mean.astype(BF)
        b["tl_out"][half] = logs
        give_to[half].start()
        give_tl[half].start()

    def t_context(half):
        give_to[half].wait_recv()
        give_tl[half].wait_recv()
        keep_context(1 + half, yh, joined(1 + half, 0, b["to_in"].at[half], b["tl_in"].at[half]), b["tctx"])
        g_t[half].root(0)

    class Reduce:
        def __init__(self, ctx, w, name, half):
            self.ctx, self.w, self.half = ctx, w, half

            def of(key):
                return b[name + key] if half is None else b[name + key].at[half]

            self.y_out, self.y_in, self.part, self.hid = of("y_out"), of("y_in"), of("part"), of("hid")
            self.r_out, self.r_in, self.z_out, self.z_in = of("r_out"), of("r_in"), of("z_out"), of("z_in")
            self.rows = self.part.shape[2] // 2
            near = (tp_dev(0, 3), tp_dev(0, 1))
            self.relay = [
                wire.copy(self.r_out.at[:, pl.ds(i * self.rows, self.rows)], self.r_in.at[i], near[i]) for i in range(2)
            ]
            self.along = [wire.copy(self.z_out.at[i], self.z_in.at[i], near[i]) for i in range(2)]
            self.beside = wire.copy(self.y_out, self.y_in, tp_dev(1, 0))

        def multiply(self, first, last, waits):
            def pair(j, carry):
                for at, wait in waits.items():
                    pl.when(j == at)(wait)
                zd = ((yh + j // 2) % 2) * 2 + (x // 2 + j % 2) % 2

                both = pl.ds(zd * 2, 2)
                if self.half is None:
                    held = self.ctx[both]
                else:
                    held = self.ctx[both, :, self.half * 64 : self.half * 64 + 64]
                done = dot(held.reshape(-1, held.shape[3]), self.w[...])
                self.part[zd] = done.reshape(2, -1, done.shape[1])

                @pl.when(zd == (z + 2) % 4)
                def _():
                    self.r_out[...] = self.part[zd].astype(BF)
                    self.relay[0].start()
                    self.relay[1].start()

                return carry

            lax.fori_loop(first, last, pair, 0)

        def send_on(self):
            for i, zd in enumerate(((z + 3) % 4, (z + 1) % 4)):
                mid = slice(i * self.rows, (i + 1) * self.rows)
                rest = slice((1 - i) * self.rows, (2 - i) * self.rows)
                self.z_out[i, :, rest, :] = self.part[zd, :, rest, :].astype(BF)
                self.relay[i].wait_recv()
                self.z_out[i, :, mid, :] = (self.part[zd, :, mid, :] + self.r_in[i].astype(F32)).astype(BF)
                self.along[i].start()

        def settle(self):
            self.along[0].wait_recv()
            self.along[1].wait_recv()

            def block(u):
                return self.part[z, u] + self.z_in[0, u].astype(F32) + self.z_in[1, u].astype(F32)

            self.y_out[...] = block(1 - yl).astype(BF)
            self.beside.start()
            self.hid[...] = block(yl)

        def finish(self, resid):
            if self.half is None:
                own = resid[...]
            else:
                first = self.half * 64
                own = jnp.concatenate([resid[first : first + 64, :], resid[first + 128 : first + 192, :]], axis=0)
            total = self.hid[...] + own.astype(F32)
            self.beside.wait_recv()
            self.hid[...] = total + self.y_in[...].astype(F32)

    def send_squares(hid, squares):
        chip, sq, between, spread = squares
        value = hid[...]
        ones = jnp.ones((8, value.shape[1]), F32)
        chip[c] = dot(ones, value * value, ((1,), (1,)), lax.Precision.HIGHEST)
        between.start()
        between.wait_recv()
        sq[k_own] = chip[0] + chip[1]
        for made in spread:
            made.start()

    def inverse_scale(squares, width):
        _, sq, _, spread = squares
        for made in spread:
            made.wait_recv()
        total = sq[0]
        for i in range(1, 8):
            total = total + sq[i]
        first = jnp.where(lax.broadcasted_iota(jnp.int32, (8, 128), 0) == 0, 1.0, 0.0)
        column = dot(total, first, ((0,), (0,)), lax.Precision.HIGHEST)
        return 1.0 / jnp.sqrt(column * (1.0 / width) + 1e-05)

    r_s = Reduce(b["sctx"], b["sw"], "s", None)
    r_t = [Reduce(b["tctx"], b["tw"], "t", half) for half in range(2)]

    def ready(gather, plane):
        gather.have_own(plane)
        gather.have_near(plane)
        gather.have_far(plane)

    fill_queries(0, sq, 0)
    prepare(0, 4, (0,))
    loads[0].wait()
    loads[1].wait()
    pl.semaphore_wait(barrier, 22)
    g_skv.root(0)
    give_sq.start()
    give_tq.start()
    g_tkv.cross.start()

    def s_partner():
        g_skv.have_own(0)
        give_sq.wait_recv()
        fill_queries(0, b["sq_in"], 1)

    def s_near():
        prepare(4, 12, (1, 2))
        fill_queries(1, tq, 0)
        fill_queries(2, tq, 0)
        give_tq.wait_recv()
        fill_queries(1, b["tq_in"], 1)
        fill_queries(2, b["tq_in"], 1)
        g_skv.mid(0)
        g_tkv.root(0, False)

    def t_start():
        partner_part()
        g_tkv.mid(0)
        g_tkv.root(1)

    def s_sums():
        for load in loads[2:]:
            load.wait()
        r_s.multiply(0, 4, {0: lambda: ready(g_s, 0), 2: lambda: ready(g_s, 1)})

    def s_squares():
        r_s.finish(sres)
        send_squares(b["shid"], s_sq)

    def s_normed():
        inverse = inverse_scale(s_sq, D_S)
        inverse = jnp.concatenate([inverse, inverse], axis=1)
        normed = (b["shid"][...] * inverse * sg[...]).astype(BF)
        for at, first in enumerate((0, 128, 64, 192)):
            b["nb"][s, at * 64 : (at + 1) * 64, :] = normed[first : first + 64, :]
        g_n.root(0)

    def t1_sums():
        r_t[0].multiply(0, 4, {0: lambda: ready(g_t[0], 0), 2: lambda: ready(g_t[0], 1)})

    def both(*hooks):
        def run():
            for hook in hooks:
                hook()

        return run

    attention(
        {
            0: s_partner,
            1: s_near,
            2: lambda: g_skv.have_left(0),
            4: lambda: g_skv.have_right(0),
            5: lambda: g_skv.far(0),
            6: lambda: g_skv.have_far(0),
            8: t_start,
            10: lambda: g_tkv.far(0),
            12: lambda: s_context(0),
            16: lambda: s_context(1),
            17: lambda: g_tkv.mid(1),
            18: lambda: g_s.mid(0),
            20: both(lambda: g_s.mid(1), lambda: g_s.far(0)),
            21: lambda: g_tkv.far(1),
            22: lambda: g_s.far(1),
            23: lambda: t_part(0),
        }
    )
    for load in map_loads:
        load.start()
    t_part(1)
    t_context(0)
    t_context(1)
    s_sums()
    r_s.send_on()
    g_t[0].mid(0)
    g_t[0].root(1)
    g_t[1].mid(0)
    g_t[1].root(1)
    wire.close(0, keys_sent)
    g_t[0].far(0)
    g_t[0].mid(1)
    r_s.settle()
    g_t[0].far(1)
    t1_sums()
    g_t[1].far(0)
    g_t[1].mid(1)
    s_squares()
    g_t[1].far(1)
    r_t[0].send_on()
    r_t[1].multiply(0, 4, {0: lambda: ready(g_t[1], 0), 2: lambda: ready(g_t[1], 1)})
    s_normed()
    r_t[1].send_on()
    r_t[0].settle()
    g_n.mid(0)
    g_n.root(1)
    r_t[0].finish(tres)
    send_squares(b["thid"].at[0], t_sq[0])
    g_n.far(0)
    g_n.mid(1)
    start_normed(0)
    b["diff"][...] = jnp.zeros((2, 128, 512), F32)
    for load in map_loads:
        load.wait()

    def match(plane):
        def one(i, carry):
            k = ((yh + plane) % 2) * 4 + i
            lhs = jnp.concatenate([b["nb"][2 * k], b["nb"][2 * k + 1]], axis=1)
            for u in range(2):
                b["diff"][:, :, u * 256 : (u + 1) * 256] += dot(lhs, b["kx"][k, u, 0:512, :]).reshape(2, 128, 256)
            return carry

        lax.fori_loop(0, 4, one, 0)

    def delta(half):
        inverse = inverse_scale(t_sq[half], D_T)
        inverse = jnp.concatenate([inverse, inverse, inverse, inverse], axis=1)
        target = b["thid"][half] * inverse * tg[...]
        b["dl"][half, p] = ((b["diff"][half] - target) * (1.0 / math.sqrt(SLAB))).astype(BF)
        g_d[half].root(0)

    def gradient(plane, offs):
        def one(i, carry):
            q = ((z + offs[0] + i * offs[1]) % 4) * 2 + (yl + plane) % 2
            deltas = b["dl"][:, q].reshape(256, 512)
            for at in range(2):
                out[at * 256 : (at + 1) * 256, :] += dot(b["ng"][q, at], deltas, ((0,), (0,)))
            return carry

        lax.fori_loop(0, offs[2], one, 0)

    own, near, far = (0, 1, 1), (1, 2, 2), (2, 1, 1)
    ready(g_n, 0)
    match(0)
    r_t[1].settle()
    g_n.far(1)
    start_normed(1)
    ready(g_n, 1)
    match(1)
    delta(0)
    r_t[1].finish(tres)
    send_squares(b["thid"].at[1], t_sq[1])
    b["ng"][p, c] = b["nb"][2 * p + c]
    out[...] = jnp.zeros((512, 512), F32)
    delta(1)
    for half in range(2):
        g_d[half].mid(0)
        g_d[half].root(1)
    have_normed()
    n_core.start()
    for half in range(2):
        g_d[half].far(0)
        g_d[half].mid(1)
    wire.close(keys_sent, contexts_sent)
    n_core.wait_recv()
    gradient(0, own)
    gradient(0, near)
    gradient(0, far)
    gradient(1, own)
    gradient(1, near)
    for half in range(2):
        g_d[half].far(1)
    gradient(1, far)
    close_normed()
    wire.close()


def per_device(tq, tkv, sq, skv, doc, tres, tw, tg, sres, sw, sg, mp):
    V = pl.BlockSpec(memory_space=pltpu.VMEM)
    A = pl.BlockSpec(memory_space=pl.ANY)
    S = pl.BlockSpec(memory_space=pltpu.SMEM)
    return pl.pallas_call(
        kernel,
        out_shape=jax.ShapeDtypeStruct((512, 512), F32),
        in_specs=[S, V, A, V, A, V, A, V, V, A, V, A],
        out_specs=V,
        scratch_shapes=list(scratch_plan().values()),
        compiler_params=pltpu.CompilerParams(
            collective_id=0, has_side_effects=True, vmem_limit_bytes=63 * 1024 * 1024
        ),
    )(
        doc, tq, tkv, sq, skv, tres, tw, tg.reshape(1, -1), sres, sw, sg.reshape(1, -1), mp.reshape(8, 512, 512)
    )


def solution(mesh):
    in_specs = (
        P("seq", "tp"),
        P(None, "seq", "tp"),
        P("seq", "tp"),
        P(None, "seq", "tp"),
        P(),
        P("tp", "seq"),
        P("tp", "seq"),
        P("seq"),
        P("tp", "seq"),
        P("tp", "seq"),
        P("seq"),
        P(None, "seq"),
    )
    out_specs = P("tp", "seq")
    return jax.shard_map(per_device, mesh=mesh, in_specs=in_specs, out_specs=out_specs, check_vma=False)
```

```python
import math

import jax
import jax.numpy as jnp
from jax import lax
from jax.experimental import pallas as pl
from jax.experimental.pallas import tpu as pltpu
from jax.sharding import PartitionSpec as P

D_T = 8192
D_S = 4096
HEAD = 128
SLAB = 2048
CACHE = 10240
KEYS_CHIP = 1536
HIDDEN = -1e30
LOG2E = math.log2(math.e)
SCALE = LOG2E / math.sqrt(HEAD)
MESH = pl.DeviceIdType.MESH
BF = jnp.bfloat16
F32 = jnp.float32


class Wire:
    def __init__(self, send, recv):
        self.send, self.recv, self.made, self.left = send, recv, [], set()

    def copy(self, src, dst, dev):
        i = len(self.made)
        made = pltpu.make_async_remote_copy(
            src_ref=src, dst_ref=dst, send_sem=self.send.at[i], recv_sem=self.recv.at[i],
            device_id=dev, device_id_type=MESH,
        )
        self.made.append(made)
        return made

    def close(self, first=0, last=None):
        for i in range(first, len(self.made) if last is None else last):
            if i not in self.left:
                self.left.add(i)
                self.made[i].wait_send()


class Gather:
    def __init__(self, wire, block, right, left, across=None, core=None, planes=None):
        self.planes = planes or (1 if across is None else 2)
        self.core = core is not None
        self.cross = wire.copy(block(0, 0, None), block(0, 0, None), across) if across is not None else None
        self.right, self.left, self.on_right, self.on_left, self.pass_on = [], [], [], [], []
        for plane in range(self.planes):
            own = block(plane, 0, None)
            self.right.append(wire.copy(own, own, right))
            self.left.append(wire.copy(own, own, left))
            first, second = block(plane, 3, 0), block(plane, 1, 1)
            self.on_right.append(wire.copy(first, first, right))
            self.on_left.append(wire.copy(second, second, left))
            if self.core:
                refs = [own, block(plane, 3, None), block(plane, 1, None), block(plane, 2, None)]
                self.pass_on.append([wire.copy(ref, ref, core) for ref in refs])

    def root(self, plane, start_cross=True):
        if plane == 1 and self.cross is not None:
            self.cross.wait_recv()
        self.right[plane].start()
        self.left[plane].start()
        if plane == 0 and self.cross is not None and start_cross:
            self.cross.start()
        if self.core:
            self.pass_on[plane][0].start()

    def mid(self, plane):
        self.right[plane].wait_recv()
        self.on_right[plane].start()
        if self.core:
            self.pass_on[plane][1].start()
        self.left[plane].wait_recv()
        self.on_left[plane].start()
        if self.core:
            self.pass_on[plane][2].start()

    def far(self, plane):
        self.on_right[plane].wait_recv()
        self.on_left[plane].wait_recv()
        if self.core:
            self.pass_on[plane][3].start()

    def have_own(self, plane):
        self.pass_on[plane][0].wait_recv()

    def have_left(self, plane):
        self.pass_on[plane][1].wait_recv()

    def have_right(self, plane):
        self.pass_on[plane][2].wait_recv()

    def have_near(self, plane):
        self.have_left(plane)
        self.have_right(plane)

    def have_far(self, plane):
        self.pass_on[plane][3].wait_recv()


def dot(a, b, dims=((1,), (0,)), precision=None):
    return lax.dot_general(a, b, (dims, ((), ())), precision=precision, preferred_element_type=F32)


def scratch_plan():
    V = pltpu.VMEM
    D = pltpu.SemaphoreType.DMA
    return dict(
        kv=V((12, 2, 2, 768, 128), BF),
        kx=V((12, 2, 768, 256), BF),
        vt=V((12, 2, 144, 768), BF),
        score0=V((768, 512), F32),
        score1=V((768, 512), F32),
        top0=V((8, 512), F32),
        top1=V((8, 512), F32),
        qa=V((3, 2, 256, 512), BF),
        sq_in=V((128, 512), BF),
        tq_in=V((128, 1024), BF),
        to_out=V((2, 128, 512), BF),
        to_in=V((2, 128, 512), BF),
        tl_out=V((2, 8, 512), F32),
        tl_in=V((2, 8, 512), F32),
        m=V((3, 2, 8, 512), F32),
        acc=V((3, 2, 144, 512), F32),
        o_out=V((2, 128, 512), BF),
        o_in=V((2, 128, 512), BF),
        l_out=V((2, 8, 512), F32),
        l_in=V((2, 8, 512), F32),
        tctx=V((8, 2, 128, 1024), BF),
        sctx=V((8, 2, 128, 512), BF),
        tw=V((1024, 512), BF),
        sw=V((512, 256), BF),
        ty_out=V((2, 128, 512), BF),
        ty_in=V((2, 128, 512), BF),
        sy_out=V((256, 256), BF),
        sy_in=V((256, 256), BF),
        tpart=V((2, 4, 2, 128, 512), F32),
        spart=V((4, 2, 256, 256), F32),
        tr_out=V((2, 2, 128, 512), BF),
        tr_in=V((2, 2, 2, 64, 512), BF),
        sr_out=V((2, 256, 256), BF),
        sr_in=V((2, 2, 128, 256), BF),
        tz_out=V((2, 2, 2, 128, 512), BF),
        tz_in=V((2, 2, 2, 128, 512), BF),
        sz_out=V((2, 2, 256, 256), BF),
        sz_in=V((2, 2, 256, 256), BF),
        thid=V((2, 128, 512), F32),
        shid=V((256, 256), F32),
        tsq=V((2, 8, 8, 128), F32),
        ssq=V((8, 8, 256), F32),
        tsq_chip=V((2, 2, 8, 128), F32),
        ssq_chip=V((2, 8, 256), F32),
        nb=V((16, 256, 256), BF),
        ng=V((8, 2, 256, 256), BF),
        dl=V((2, 8, 128, 512), BF),
        diff=V((2, 128, 512), F32),
        wsend=D((200,)),
        wrecv=D((200,)),
        loc=D((8,)),
    )


def kernel(doc, tq, tkv_h, sq, skv_h, tres, tw_h, tg, sres, sw_h, sg, mp_h, out, *scratch):
    b = dict(zip(scratch_plan(), scratch))
    s = lax.axis_index("seq")
    p = lax.axis_index("tp")
    yh, x, c = s // 8, (s // 2) % 4, s % 2
    z, yl = p // 2, p % 2
    k_own = yh * 4 + x

    def seq_dev(plane, off, other):
        return ((((yh + plane) % 2) * 4 + (x + off) % 4) * 2 + (c + other) % 2, p)

    def tp_dev(plane, off):
        return (s, ((z + off) % 4) * 2 + (yl + plane) % 2)

    right, left, across, core = seq_dev(0, 1, 0), seq_dev(0, 3, 0), seq_dev(1, 0, 0), seq_dev(0, 0, 1)

    loads = [
        pltpu.make_async_copy(skv_h, b["kv"].at[x, c], b["loc"].at[0]),
        pltpu.make_async_copy(tkv_h, b["kv"].at[4 + k_own, c], b["loc"].at[1]),
        pltpu.make_async_copy(sw_h, b["sw"], b["loc"].at[2]),
        pltpu.make_async_copy(tw_h, b["tw"], b["loc"].at[3]),
    ]
    for load in loads:
        load.start()
    map_loads = [
        pltpu.make_async_copy(
            mp_h.at[:, :, pl.ds(u * 256, 256)], b["kx"].at[pl.ds(0, 8), u, pl.ds(0, 512)], b["loc"].at[4 + u]
        )
        for u in range(2)
    ]

    barrier = pltpu.get_barrier_semaphore()
    for off in range(1, 16):
        pl.semaphore_signal(barrier, inc=1, device_id=((s + off) % 16, p), device_id_type=MESH)
    for off in range(1, 8):
        pl.semaphore_signal(barrier, inc=1, device_id=(s, (p + off) % 8), device_id_type=MESH)

    wire = Wire(b["wsend"], b["wrecv"])
    give_sq = wire.copy(sq, b["sq_in"], across)
    give_tq = wire.copy(tq, b["tq_in"], core)

    def kv_block(model):
        def block(plane, off, part):
            at = (x + off) % 4 + model * (4 + ((yh + plane) % 2) * 4)
            if part is None:
                return b["kv"].at[at, c]
            return b["kv"].at[at, c, part]

        return block

    def s_block(plane, off, part):
        at = ((yh + plane) % 2) * 4 + (x + off) % 4
        if part is None:
            return b["sctx"].at[at, c]
        return b["sctx"].at[at, c, pl.ds(part * 64, 64)]

    def t_block(half):
        def block(plane, off, part):
            at = ((yh + plane) % 2) * 4 + (x + off) % 4
            if part is None:
                return b["tctx"].at[at, c, pl.ds(half * 64, 64)]
            return b["tctx"].at[at, c, pl.ds(half * 64 + part * 32, 32)]

        return block

    def nb_block(plane, off, part):
        at = (((yh + plane) % 2) * 4 + (x + off) % 4) * 2 + c
        if part is None:
            return b["nb"].at[at]
        return b["nb"].at[at, pl.ds(part * 128, 128)]

    def dl_block(half):
        def block(plane, off, part):
            at = ((z + off) % 4) * 2 + (yl + plane) % 2
            if part is None:
                return b["dl"].at[half, at]
            return b["dl"].at[half, at, pl.ds(part * 64, 64)]

        return block

    g_skv = Gather(wire, kv_block(0), right, left, None, core)
    g_tkv = Gather(wire, kv_block(1), right, left, across)
    keys_sent = len(wire.made)
    g_s = Gather(wire, s_block, right, left, None, core, 2)
    g_t = [Gather(wire, t_block(half), right, left, across, core) for half in range(2)]
    contexts_sent = len(wire.made)
    g_n = Gather(wire, nb_block, right, left, across, core)
    g_d = [Gather(wire, dl_block(half), tp_dev(0, 1), tp_dev(0, 3), tp_dev(1, 0), None) for half in range(2)]
    give_to = [wire.copy(b["to_out"].at[i], b["to_in"].at[i], core) for i in range(2)]
    give_tl = [wire.copy(b["tl_out"].at[i], b["tl_in"].at[i], core) for i in range(2)]
    give_o = [wire.copy(b["o_out"].at[1 - g], b["o_in"].at[g], across) for g in range(2)]
    give_l = [wire.copy(b["l_out"].at[1 - g], b["l_in"].at[g], across) for g in range(2)]
    def square_copies(chip, sq):
        between = wire.copy(chip.at[c], chip.at[c], core)
        offs = range(1, 8)
        spread = [wire.copy(sq.at[k_own], sq.at[k_own], (((k_own + off) % 8) * 2 + c, p)) for off in offs]
        return chip, sq, between, spread

    s_sq = square_copies(b["ssq_chip"], b["ssq"])
    t_sq = [square_copies(b["tsq_chip"].at[half], b["tsq"].at[half]) for half in range(2)]
    n_tp = [
        wire.copy(b["nb"].at[((p + off) % 8) * 2 + c], b["ng"].at[p, c], (s, (p + off) % 8)) for off in range(1, 8)
    ]
    n_core = wire.copy(b["ng"].at[:, c], b["ng"].at[:, c], core)

    qa, m, acc = b["qa"], b["m"], b["acc"]
    heads, tokens = (4, 8, 8), (128, 64, 64)

    def fill_queries(one, src, group):
        first = 64 * (one // 2)
        for i in range(4):
            if one == 0:
                held = src[:, i * 128 : (i + 1) * 128]
            else:
                pair = [src[first : first + 64, h * 128 : (h + 1) * 128] for h in (2 * i, 2 * i + 1)]
                held = jnp.concatenate(pair, axis=0)
            qa[one, group, 0:128, i * 128 : (i + 1) * 128] = held.T

    def prepare(first, last, passes):
        rows = lax.broadcasted_iota(jnp.int32, (128, 128), 0)
        lanes = lax.broadcasted_iota(jnp.int32, (128, 128), 1)
        for one in passes:
            eye = jnp.where(lanes % tokens[one] + 64 * (one // 2) == rows, 1.0, 0.0).astype(BF)
            for g in range(2):
                for i in range(4):
                    qa[one, g, 128:256, i * 128 : (i + 1) * 128] = eye
            m[one] = jnp.full((2, 8, 512), HIDDEN, F32)
            acc[one] = jnp.zeros((2, 144, 512), F32)

        def extra(i, carry):
            b["kx"][i, :, :, 128:256] = jnp.zeros((2, 768, 128), BF)
            b["vt"][i, :, 128:144, :] = jnp.ones((2, 16, 768), BF)
            return carry

        lax.fori_loop(first, last, extra, 0)

    first_key = doc[0]

    def tile_at(n):
        third = n // 8
        t = (third + 1) // 2
        other = third // 2
        one = t * (1 + (1 - other) * ((n % 8) // 4) + other * (n % 2))
        i = (1 - t + other) * ((n % 8) // 2) + (t - other) * (n % 4)
        plane = (yh + other) % 2
        at = (x + 3 * i + 3 * (i // 2) + 2 * (i // 3)) % 4
        return one, t, t * (4 + plane * 4) + at, plane, at, (c + (1 - t) * (n % 2)) % 2

    def build(n, g):
        one, t, block, plane, at, from_core = tile_at(n)
        base = (plane * 4 + at) * KEYS_CHIP + from_core * 768

        if g == 0:

            @pl.when(one <= 1)
            def _():
                b["vt"][block, from_core, 0:128, :] = b["kv"][block, from_core, 1].T
                b["kx"][block, from_core, :, 0:128] = b["kv"][block, from_core, 0]

                @pl.when(plane == 0)
                def _():
                    key = lax.broadcasted_iota(jnp.int32, (768, 128), 0)
                    b["kx"][block, from_core, :, 128:256] = jnp.where(key >= first_key - base, 0.0, HIDDEN).astype(BF)

        @pl.when((plane == 1) & (at >= 2))
        def _():
            ahead = CACHE + ((((yh + (1 - t) * g) % 2) * 4 + x) * 2 + (c + t * g) % 2) * 128 - base
            key = lax.broadcasted_iota(jnp.int32, (768, 128), 0)
            row = lax.broadcasted_iota(jnp.int32, (768, 128), 1)
            b["kx"][block, from_core, :, 128:256] = jnp.where(key - row <= ahead, 0.0, HIDDEN).astype(BF)

    scores, tops = (b["score0"], b["score1"]), (b["top0"], b["top1"])

    def overlapped(n, u, weigh_n, weigh=True):
        one, _, block, _, _, from_core = tile_at(n)
        queries = qa[one, u]
        top = jnp.full((8, 512), HIDDEN, F32)
        if weigh:
            w_one, _, w_block, _, _, w_core = tile_at(weigh_n)
            w_g = 1 - u
            old = m[w_one, w_g]
            peak = jnp.max(tops[1 - u][...], axis=0, keepdims=True)
            new = jnp.maximum(old, jnp.broadcast_to(peak, (8, 512)))
            total = (acc[w_one, w_g].reshape(18, 8, 512) * jnp.exp2((old - new) * SCALE)[None]).reshape(144, 512)
        for first, count in ((0, 512), (512, 256)):
            keys = slice(first, first + count)
            fresh = dot(b["kx"][block, from_core, keys, :], queries)
            scores[u][keys, :] = fresh
            top = jnp.maximum(top, jnp.max(fresh.reshape(count // 8, 8, 512), axis=0))
            if weigh:
                held = scores[1 - u][keys, :].reshape(count // 8, 8, 512)
                weights = jnp.exp2((held - new[None]) * SCALE).reshape(count, 512).astype(BF)
                total = total + dot(b["vt"][w_block, w_core, :, keys], weights)
        tops[u][...] = top
        if weigh:
            m[w_one, w_g] = new
            acc[w_one, w_g] = total

    def attention(hooks):
        build(0, 0)
        overlapped(0, 0, 0, weigh=False)

        def step(n, carry):
            for at_step, hook in hooks.items():
                pl.when(n == at_step)(hook)
            build(n, 1)
            overlapped(n, 1, n)
            after = (n + 1) % 24
            build(after, 0)
            overlapped(after, 0, n)
            return carry

        lax.fori_loop(0, 24, step, 0)

    def part_of(one, g):
        total = acc[one, g, 128:136, :]
        mean = (acc[one, g, 0:128, :].reshape(16, 8, 512) * (1.0 / total)[None]).reshape(128, 512)
        return mean, m[one, g] * SCALE + jnp.log(total) * LOG2E

    def partner_part():
        for g in (1, 0):
            mean, logs = part_of(0, g)
            b["o_out"][g] = mean.astype(BF)
            b["l_out"][g] = logs
            give_o[1 - g].start()
            give_l[1 - g].start()

    def keep_context(one, plane, both, ctx):
        both = both.T.astype(BF)
        count, first = tokens[one], 64 * (one // 2)
        for h in range(heads[one]):
            held = both[h * count : (h + 1) * count, :]
            ctx[plane * 4 + x, c, first : first + count, h * 128 : (h + 1) * 128] = held

    def joined(one, g, o_in, l_in):
        mine, log_mine = part_of(one, g)
        share = 1.0 / (1.0 + jnp.exp2(log_mine - l_in[...]))
        other = o_in[...].astype(F32)
        return mine + ((other - mine).reshape(16, 8, 512) * share[None]).reshape(128, 512)

    def s_context(g):
        give_o[g].wait_recv()
        give_l[g].wait_recv()
        keep_context(0, (yh + g) % 2, joined(0, g, b["o_in"].at[g], b["l_in"].at[g]), b["sctx"])
        g_s.root(g)

    def t_part(half):
        mean, logs = part_of(1 + half, 1)
        b["to_out"][half] = mean.astype(BF)
        b["tl_out"][half] = logs
        give_to[half].start()
        give_tl[half].start()

    def t_context(half):
        give_to[half].wait_recv()
        give_tl[half].wait_recv()
        keep_context(1 + half, yh, joined(1 + half, 0, b["to_in"].at[half], b["tl_in"].at[half]), b["tctx"])
        g_t[half].root(0)

    class Reduce:
        def __init__(self, ctx, w, name, half):
            self.ctx, self.w, self.half = ctx, w, half

            def of(key):
                return b[name + key] if half is None else b[name + key].at[half]

            self.y_out, self.y_in, self.part, self.hid = of("y_out"), of("y_in"), of("part"), of("hid")
            self.r_out, self.r_in, self.z_out, self.z_in = of("r_out"), of("r_in"), of("z_out"), of("z_in")
            self.rows = self.part.shape[2] // 2
            near = (tp_dev(0, 3), tp_dev(0, 1))
            self.relay = [
                wire.copy(self.r_out.at[:, pl.ds(i * self.rows, self.rows)], self.r_in.at[i], near[i]) for i in range(2)
            ]
            self.along = [wire.copy(self.z_out.at[i], self.z_in.at[i], near[i]) for i in range(2)]
            self.beside = wire.copy(self.y_out, self.y_in, tp_dev(1, 0))

        def multiply(self, first, last, waits):
            def pair(j, carry):
                for at, wait in waits.items():
                    pl.when(j == at)(wait)
                zd = ((yh + j // 2) % 2) * 2 + (x // 2 + j % 2) % 2

                both = pl.ds(zd * 2, 2)
                if self.half is None:
                    held = self.ctx[both]
                else:
                    held = self.ctx[both, :, self.half * 64 : self.half * 64 + 64]
                done = dot(held.reshape(-1, held.shape[3]), self.w[...])
                self.part[zd] = done.reshape(2, -1, done.shape[1])

                @pl.when(zd == (z + 2) % 4)
                def _():
                    self.r_out[...] = self.part[zd].astype(BF)
                    self.relay[0].start()
                    self.relay[1].start()

                return carry

            lax.fori_loop(first, last, pair, 0)

        def send_on(self):
            for i, zd in enumerate(((z + 3) % 4, (z + 1) % 4)):
                mid = slice(i * self.rows, (i + 1) * self.rows)
                rest = slice((1 - i) * self.rows, (2 - i) * self.rows)
                self.z_out[i, :, rest, :] = self.part[zd, :, rest, :].astype(BF)
                self.relay[i].wait_recv()
                self.z_out[i, :, mid, :] = (self.part[zd, :, mid, :] + self.r_in[i].astype(F32)).astype(BF)
                self.along[i].start()

        def settle(self):
            self.along[0].wait_recv()
            self.along[1].wait_recv()

            def block(u):
                return self.part[z, u] + self.z_in[0, u].astype(F32) + self.z_in[1, u].astype(F32)

            self.y_out[...] = block(1 - yl).astype(BF)
            self.beside.start()
            self.hid[...] = block(yl)

        def finish(self, resid):
            if self.half is None:
                own = resid[...]
            else:
                first = self.half * 64
                own = jnp.concatenate([resid[first : first + 64, :], resid[first + 128 : first + 192, :]], axis=0)
            total = self.hid[...] + own.astype(F32)
            self.beside.wait_recv()
            self.hid[...] = total + self.y_in[...].astype(F32)

    def send_squares(hid, squares):
        chip, sq, between, spread = squares
        value = hid[...]
        ones = jnp.ones((8, value.shape[1]), F32)
        chip[c] = dot(ones, value * value, ((1,), (1,)), lax.Precision.HIGHEST)
        between.start()
        between.wait_recv()
        sq[k_own] = chip[0] + chip[1]
        for made in spread:
            made.start()

    def inverse_scale(squares, width):
        _, sq, _, spread = squares
        for made in spread:
            made.wait_recv()
        total = sq[0]
        for i in range(1, 8):
            total = total + sq[i]
        first = jnp.where(lax.broadcasted_iota(jnp.int32, (8, 128), 0) == 0, 1.0, 0.0)
        column = dot(total, first, ((0,), (0,)), lax.Precision.HIGHEST)
        return 1.0 / jnp.sqrt(column * (1.0 / width) + 1e-05)

    r_s = Reduce(b["sctx"], b["sw"], "s", None)
    r_t = [Reduce(b["tctx"], b["tw"], "t", half) for half in range(2)]

    def ready(gather, plane):
        gather.have_own(plane)
        gather.have_near(plane)
        gather.have_far(plane)

    fill_queries(0, sq, 0)
    prepare(0, 4, (0,))
    loads[0].wait()
    loads[1].wait()
    pl.semaphore_wait(barrier, 22)
    g_skv.root(0)
    give_sq.start()
    give_tq.start()
    g_tkv.cross.start()

    def s_partner():
        g_skv.have_own(0)
        give_sq.wait_recv()
        fill_queries(0, b["sq_in"], 1)

    def s_near():
        prepare(4, 12, (1, 2))
        fill_queries(1, tq, 0)
        fill_queries(2, tq, 0)
        give_tq.wait_recv()
        fill_queries(1, b["tq_in"], 1)
        fill_queries(2, b["tq_in"], 1)
        g_skv.mid(0)
        g_tkv.root(0, False)

    def t_start():
        partner_part()
        g_tkv.mid(0)
        g_tkv.root(1)

    def s_sums():
        for load in loads[2:]:
            load.wait()
        r_s.multiply(0, 4, {0: lambda: ready(g_s, 0), 2: lambda: ready(g_s, 1)})

    def s_squares():
        r_s.finish(sres)
        send_squares(b["shid"], s_sq)

    def s_normed():
        inverse = inverse_scale(s_sq, D_S)
        inverse = jnp.concatenate([inverse, inverse], axis=1)
        normed = (b["shid"][...] * inverse * sg[...]).astype(BF)
        for at, first in enumerate((0, 128, 64, 192)):
            b["nb"][s, at * 64 : (at + 1) * 64, :] = normed[first : first + 64, :]
        g_n.root(0)

    def t1_sums():
        r_t[0].multiply(0, 4, {0: lambda: ready(g_t[0], 0), 2: lambda: ready(g_t[0], 1)})

    def both(*hooks):
        def run():
            for hook in hooks:
                hook()

        return run

    attention(
        {
            0: s_partner,
            1: s_near,
            2: lambda: g_skv.have_left(0),
            4: lambda: g_skv.have_right(0),
            5: lambda: g_skv.far(0),
            6: lambda: g_skv.have_far(0),
            8: t_start,
            10: lambda: g_tkv.far(0),
            12: lambda: s_context(0),
            16: lambda: s_context(1),
            17: lambda: g_tkv.mid(1),
            18: lambda: g_s.mid(0),
            20: both(lambda: g_s.mid(1), lambda: g_s.far(0)),
            21: lambda: g_tkv.far(1),
            22: lambda: g_s.far(1),
            23: lambda: t_part(0),
        }
    )
    for load in map_loads:
        load.start()
    t_part(1)
    t_context(0)
    t_context(1)
    s_sums()
    r_s.send_on()
    g_t[0].mid(0)
    g_t[0].root(1)
    g_t[1].mid(0)
    g_t[1].root(1)
    wire.close(0, keys_sent)
    g_t[0].far(0)
    g_t[0].mid(1)
    r_s.settle()
    g_t[0].far(1)
    t1_sums()
    g_t[1].far(0)
    g_t[1].mid(1)
    s_squares()
    g_t[1].far(1)
    r_t[0].send_on()
    r_t[1].multiply(0, 4, {0: lambda: ready(g_t[1], 0), 2: lambda: ready(g_t[1], 1)})
    s_normed()
    r_t[1].send_on()
    r_t[0].settle()
    g_n.mid(0)
    g_n.root(1)
    r_t[0].finish(tres)
    send_squares(b["thid"].at[0], t_sq[0])
    g_n.far(0)
    g_n.mid(1)
    r_t[1].settle()
    g_n.far(1)
    for made in n_tp:
        made.start()
    r_t[1].finish(tres)
    send_squares(b["thid"].at[1], t_sq[1])
    wire.close(keys_sent, contexts_sent)
    ready(g_n, 0)
    ready(g_n, 1)
    b["diff"][...] = jnp.zeros((2, 128, 512), F32)
    for load in map_loads:
        load.wait()

    def match(k, carry):
        lhs = jnp.concatenate([b["nb"][2 * k], b["nb"][2 * k + 1]], axis=1)
        for u in range(2):
            b["diff"][:, :, u * 256 : (u + 1) * 256] += dot(lhs, b["kx"][k, u, 0:512, :]).reshape(2, 128, 256)
        return carry

    lax.fori_loop(0, 8, match, 0)

    def delta(half):
        inverse = inverse_scale(t_sq[half], D_T)
        inverse = jnp.concatenate([inverse, inverse, inverse, inverse], axis=1)
        target = b["thid"][half] * inverse * tg[...]
        b["dl"][half, p] = ((b["diff"][half] - target) * (1.0 / math.sqrt(SLAB))).astype(BF)
        g_d[half].root(0)

    def gradient(half, plane, offs):
        def one(i, carry):
            q = ((z + offs[0] + i * offs[1]) % 4) * 2 + (yl + plane) % 2
            for at in range(2):
                rows = slice(at * 256, (at + 1) * 256)
                lhs = b["ng"][q, at, half * 128 : (half + 1) * 128, :]
                out[rows, :] += dot(lhs, b["dl"][half, q], ((0,), (0,)))
            return carry

        lax.fori_loop(0, offs[2], one, 0)

    own, near, far = (0, 1, 1), (1, 2, 2), (2, 1, 1)
    delta(0)
    delta(1)
    b["ng"][p, c] = b["nb"][2 * p + c]
    out[...] = jnp.zeros((512, 512), F32)
    g_d[0].mid(0)
    g_d[0].root(1)
    for made in n_tp:
        made.wait_recv()
    n_core.start()
    g_d[0].far(0)
    g_d[0].mid(1)
    n_core.wait_recv()
    gradient(0, 0, own)
    gradient(0, 0, near)
    gradient(0, 0, far)
    gradient(0, 1, own)
    g_d[1].mid(0)
    g_d[1].root(1)
    gradient(0, 1, near)
    g_d[0].far(1)
    gradient(0, 1, far)
    gradient(1, 0, own)
    gradient(1, 0, near)
    gradient(1, 1, own)
    g_d[1].far(0)
    g_d[1].mid(1)
    gradient(1, 0, far)
    gradient(1, 1, near)
    g_d[1].far(1)
    gradient(1, 1, far)
    wire.close()


def per_device(tq, tkv, sq, skv, doc, tres, tw, tg, sres, sw, sg, mp):
    V = pl.BlockSpec(memory_space=pltpu.VMEM)
    A = pl.BlockSpec(memory_space=pl.ANY)
    S = pl.BlockSpec(memory_space=pltpu.SMEM)
    return pl.pallas_call(
        kernel,
        out_shape=jax.ShapeDtypeStruct((512, 512), F32),
        in_specs=[S, V, A, V, A, V, A, V, V, A, V, A],
        out_specs=V,
        scratch_shapes=list(scratch_plan().values()),
        compiler_params=pltpu.CompilerParams(
            collective_id=0, has_side_effects=True, vmem_limit_bytes=63 * 1024 * 1024
        ),
    )(
        doc, tq, tkv, sq, skv, tres, tw, tg.reshape(1, -1), sres, sw, sg.reshape(1, -1), mp.reshape(8, 512, 512)
    )


def solution(mesh):
    in_specs = (
        P("seq", "tp"),
        P(None, "seq", "tp"),
        P("seq", "tp"),
        P(None, "seq", "tp"),
        P(),
        P("tp", "seq"),
        P("tp", "seq"),
        P("seq"),
        P("tp", "seq"),
        P("tp", "seq"),
        P("seq"),
        P(None, "seq"),
    )
    out_specs = P("tp", "seq")
    return jax.shard_map(per_device, mesh=mesh, in_specs=in_specs, out_specs=out_specs, check_vma=False)
```

```python
import math

import jax
import jax.numpy as jnp
from jax import lax
from jax.experimental import pallas as pl
from jax.experimental.pallas import tpu as pltpu
from jax.sharding import PartitionSpec as P

D_T = 8192
D_S = 4096
HEAD = 128
SLAB = 2048
CACHE = 10240
KEYS_CHIP = 1536
HIDDEN = -1e30
LOG2E = math.log2(math.e)
SCALE = LOG2E / math.sqrt(HEAD)
MESH = pl.DeviceIdType.MESH
BF = jnp.bfloat16
F32 = jnp.float32


class Wire:
    def __init__(self, send, recv):
        self.send, self.recv, self.made, self.left = send, recv, [], set()

    def copy(self, src, dst, dev):
        i = len(self.made)
        made = pltpu.make_async_remote_copy(
            src_ref=src, dst_ref=dst, send_sem=self.send.at[i], recv_sem=self.recv.at[i],
            device_id=dev, device_id_type=MESH,
        )
        self.made.append(made)
        return made

    def close(self, first=0, last=None):
        for i in range(first, len(self.made) if last is None else last):
            if i not in self.left:
                self.left.add(i)
                self.made[i].wait_send()


class Gather:
    def __init__(self, wire, block, right, left, across=None, core=None, planes=None):
        self.planes = planes or (1 if across is None else 2)
        self.core = core is not None
        self.cross = wire.copy(block(0, 0, None), block(0, 0, None), across) if across is not None else None
        self.right, self.left, self.on_right, self.on_left, self.pass_on = [], [], [], [], []
        for plane in range(self.planes):
            own = block(plane, 0, None)
            self.right.append(wire.copy(own, own, right))
            self.left.append(wire.copy(own, own, left))
            first, second = block(plane, 3, 0), block(plane, 1, 1)
            self.on_right.append(wire.copy(first, first, right))
            self.on_left.append(wire.copy(second, second, left))
            if self.core:
                refs = [own, block(plane, 3, None), block(plane, 1, None), block(plane, 2, None)]
                self.pass_on.append([wire.copy(ref, ref, core) for ref in refs])

    def root(self, plane, start_cross=True):
        if plane == 1 and self.cross is not None:
            self.cross.wait_recv()
        self.right[plane].start()
        self.left[plane].start()
        if plane == 0 and self.cross is not None and start_cross:
            self.cross.start()
        if self.core:
            self.pass_on[plane][0].start()

    def mid(self, plane):
        self.right[plane].wait_recv()
        self.on_right[plane].start()
        if self.core:
            self.pass_on[plane][1].start()
        self.left[plane].wait_recv()
        self.on_left[plane].start()
        if self.core:
            self.pass_on[plane][2].start()

    def far(self, plane):
        self.on_right[plane].wait_recv()
        self.on_left[plane].wait_recv()
        if self.core:
            self.pass_on[plane][3].start()

    def have_own(self, plane):
        self.pass_on[plane][0].wait_recv()

    def have_left(self, plane):
        self.pass_on[plane][1].wait_recv()

    def have_right(self, plane):
        self.pass_on[plane][2].wait_recv()

    def have_near(self, plane):
        self.have_left(plane)
        self.have_right(plane)

    def have_far(self, plane):
        self.pass_on[plane][3].wait_recv()


def dot(a, b, dims=((1,), (0,)), precision=None):
    return lax.dot_general(a, b, (dims, ((), ())), precision=precision, preferred_element_type=F32)


def scratch_plan():
    V = pltpu.VMEM
    D = pltpu.SemaphoreType.DMA
    return dict(
        kv=V((12, 2, 2, 768, 128), BF),
        kx=V((12, 2, 768, 256), BF),
        vt=V((12, 2, 144, 768), BF),
        score0=V((768, 512), F32),
        score1=V((768, 512), F32),
        top0=V((8, 512), F32),
        top1=V((8, 512), F32),
        qa=V((3, 2, 256, 512), BF),
        sq_in=V((128, 512), BF),
        tq_in=V((128, 1024), BF),
        to_out=V((2, 128, 512), BF),
        to_in=V((2, 128, 512), BF),
        tl_out=V((2, 8, 512), F32),
        tl_in=V((2, 8, 512), F32),
        m=V((3, 2, 8, 512), F32),
        acc=V((3, 2, 144, 512), F32),
        o_out=V((2, 128, 512), BF),
        o_in=V((2, 128, 512), BF),
        l_out=V((2, 8, 512), F32),
        l_in=V((2, 8, 512), F32),
        tctx=V((8, 2, 128, 1024), BF),
        sctx=V((8, 2, 128, 512), BF),
        tw=V((1024, 512), BF),
        sw=V((512, 256), BF),
        ty_out=V((2, 128, 512), BF),
        ty_in=V((2, 128, 512), BF),
        sy_out=V((256, 256), BF),
        sy_in=V((256, 256), BF),
        tpart=V((2, 4, 2, 128, 512), F32),
        spart=V((4, 2, 256, 256), F32),
        tr_out=V((2, 2, 128, 512), BF),
        tr_in=V((2, 2, 2, 64, 512), BF),
        sr_out=V((2, 256, 256), BF),
        sr_in=V((2, 2, 128, 256), BF),
        tz_out=V((2, 2, 2, 128, 512), BF),
        tz_in=V((2, 2, 2, 128, 512), BF),
        sz_out=V((2, 2, 256, 256), BF),
        sz_in=V((2, 2, 256, 256), BF),
        thid=V((2, 128, 512), F32),
        shid=V((256, 256), F32),
        tsq=V((2, 8, 8, 128), F32),
        ssq=V((8, 8, 256), F32),
        tsq_chip=V((2, 2, 8, 128), F32),
        ssq_chip=V((2, 8, 256), F32),
        nb=V((16, 256, 256), BF),
        ng=V((8, 2, 256, 256), BF),
        dl=V((2, 8, 128, 512), BF),
        diff=V((2, 128, 512), F32),
        wsend=D((200,)),
        wrecv=D((200,)),
        loc=D((8,)),
    )


def kernel(doc, tq, tkv_h, sq, skv_h, tres, tw_h, tg, sres, sw_h, sg, mp_h, out, *scratch):
    b = dict(zip(scratch_plan(), scratch))
    s = lax.axis_index("seq")
    p = lax.axis_index("tp")
    yh, x, c = s // 8, (s // 2) % 4, s % 2
    z, yl = p // 2, p % 2
    k_own = yh * 4 + x

    def seq_dev(plane, off, other):
        return ((((yh + plane) % 2) * 4 + (x + off) % 4) * 2 + (c + other) % 2, p)

    def tp_dev(plane, off):
        return (s, ((z + off) % 4) * 2 + (yl + plane) % 2)

    right, left, across, core = seq_dev(0, 1, 0), seq_dev(0, 3, 0), seq_dev(1, 0, 0), seq_dev(0, 0, 1)

    loads = [
        pltpu.make_async_copy(skv_h, b["kv"].at[x, c], b["loc"].at[0]),
        pltpu.make_async_copy(tkv_h, b["kv"].at[4 + k_own, c], b["loc"].at[1]),
        pltpu.make_async_copy(sw_h, b["sw"], b["loc"].at[2]),
        pltpu.make_async_copy(tw_h, b["tw"], b["loc"].at[3]),
    ]
    for load in loads:
        load.start()
    map_loads = [
        pltpu.make_async_copy(
            mp_h.at[:, :, pl.ds(u * 256, 256)], b["kx"].at[pl.ds(0, 8), u, pl.ds(0, 512)], b["loc"].at[4 + u]
        )
        for u in range(2)
    ]

    barrier = pltpu.get_barrier_semaphore()
    for off in range(1, 16):
        pl.semaphore_signal(barrier, inc=1, device_id=((s + off) % 16, p), device_id_type=MESH)
    for off in range(1, 8):
        pl.semaphore_signal(barrier, inc=1, device_id=(s, (p + off) % 8), device_id_type=MESH)

    wire = Wire(b["wsend"], b["wrecv"])
    give_sq = wire.copy(sq, b["sq_in"], across)
    give_tq = wire.copy(tq, b["tq_in"], core)

    def kv_block(model):
        def block(plane, off, part):
            at = (x + off) % 4 + model * (4 + ((yh + plane) % 2) * 4)
            if part is None:
                return b["kv"].at[at, c]
            return b["kv"].at[at, c, part]

        return block

    def s_block(plane, off, part):
        at = ((yh + plane) % 2) * 4 + (x + off) % 4
        if part is None:
            return b["sctx"].at[at, c]
        return b["sctx"].at[at, c, pl.ds(part * 64, 64)]

    def t_block(half):
        def block(plane, off, part):
            at = ((yh + plane) % 2) * 4 + (x + off) % 4
            if part is None:
                return b["tctx"].at[at, c, pl.ds(half * 64, 64)]
            return b["tctx"].at[at, c, pl.ds(half * 64 + part * 32, 32)]

        return block

    def nb_block(plane, off, part):
        at = (((yh + plane) % 2) * 4 + (x + off) % 4) * 2 + c
        if part is None:
            return b["nb"].at[at]
        return b["nb"].at[at, pl.ds(part * 128, 128)]

    def dl_block(half):
        def block(plane, off, part):
            at = ((z + off) % 4) * 2 + (yl + plane) % 2
            if part is None:
                return b["dl"].at[half, at]
            return b["dl"].at[half, at, pl.ds(part * 64, 64)]

        return block

    g_skv = Gather(wire, kv_block(0), right, left, None, core)
    g_tkv = Gather(wire, kv_block(1), right, left, across)
    keys_sent = len(wire.made)
    g_s = Gather(wire, s_block, right, left, None, core, 2)
    g_t = [Gather(wire, t_block(half), right, left, across, core) for half in range(2)]
    contexts_sent = len(wire.made)
    g_n = Gather(wire, nb_block, right, left, across, core)
    g_d = [Gather(wire, dl_block(half), tp_dev(0, 1), tp_dev(0, 3), tp_dev(1, 0), None) for half in range(2)]
    give_to = [wire.copy(b["to_out"].at[i], b["to_in"].at[i], core) for i in range(2)]
    give_tl = [wire.copy(b["tl_out"].at[i], b["tl_in"].at[i], core) for i in range(2)]
    give_o = [wire.copy(b["o_out"].at[1 - g], b["o_in"].at[g], across) for g in range(2)]
    give_l = [wire.copy(b["l_out"].at[1 - g], b["l_in"].at[g], across) for g in range(2)]
    def square_copies(chip, sq):
        between = wire.copy(chip.at[c], chip.at[c], core)
        offs = range(1, 8)
        spread = [wire.copy(sq.at[k_own], sq.at[k_own], (((k_own + off) % 8) * 2 + c, p)) for off in offs]
        return chip, sq, between, spread

    s_sq = square_copies(b["ssq_chip"], b["ssq"])
    t_sq = [square_copies(b["tsq_chip"].at[half], b["tsq"].at[half]) for half in range(2)]
    n_tp = [
        wire.copy(b["nb"].at[((p + off) % 8) * 2 + c], b["ng"].at[p, c], (s, (p + off) % 8)) for off in range(1, 8)
    ]
    n_core = wire.copy(b["ng"].at[:, c], b["ng"].at[:, c], core)

    qa, m, acc = b["qa"], b["m"], b["acc"]
    heads, tokens = (4, 8, 8), (128, 64, 64)

    def fill_queries(one, src, group):
        first = 64 * (one // 2)
        for i in range(4):
            if one == 0:
                held = src[:, i * 128 : (i + 1) * 128]
            else:
                pair = [src[first : first + 64, h * 128 : (h + 1) * 128] for h in (2 * i, 2 * i + 1)]
                held = jnp.concatenate(pair, axis=0)
            qa[one, group, 0:128, i * 128 : (i + 1) * 128] = held.T

    def prepare(first, last, passes):
        rows = lax.broadcasted_iota(jnp.int32, (128, 128), 0)
        lanes = lax.broadcasted_iota(jnp.int32, (128, 128), 1)
        for one in passes:
            eye = jnp.where(lanes % tokens[one] + 64 * (one // 2) == rows, 1.0, 0.0).astype(BF)
            for g in range(2):
                for i in range(4):
                    qa[one, g, 128:256, i * 128 : (i + 1) * 128] = eye
            m[one] = jnp.full((2, 8, 512), HIDDEN, F32)
            acc[one] = jnp.zeros((2, 144, 512), F32)

        def extra(i, carry):
            b["kx"][i, :, :, 128:256] = jnp.zeros((2, 768, 128), BF)
            b["vt"][i, :, 128:144, :] = jnp.ones((2, 16, 768), BF)
            return carry

        lax.fori_loop(first, last, extra, 0)

    first_key = doc[0]

    def tile_at(n):
        third = n // 8
        t = (third + 1) // 2
        other = third // 2
        one = t * (1 + (1 - other) * ((n % 8) // 4) + other * (n % 2))
        i = (1 - t + other) * ((n % 8) // 2) + (t - other) * (n % 4)
        plane = (yh + other) % 2
        at = (x + 3 * i + 3 * (i // 2) + 2 * (i // 3)) % 4
        return one, t, t * (4 + plane * 4) + at, plane, at, (c + (1 - t) * (n % 2)) % 2

    def build(n, g):
        one, t, block, plane, at, from_core = tile_at(n)
        base = (plane * 4 + at) * KEYS_CHIP + from_core * 768

        if g == 0:

            @pl.when(one <= 1)
            def _():
                b["vt"][block, from_core, 0:128, :] = b["kv"][block, from_core, 1].T
                b["kx"][block, from_core, :, 0:128] = b["kv"][block, from_core, 0]

                @pl.when(plane == 0)
                def _():
                    key = lax.broadcasted_iota(jnp.int32, (768, 128), 0)
                    b["kx"][block, from_core, :, 128:256] = jnp.where(key >= first_key - base, 0.0, HIDDEN).astype(BF)

        @pl.when((plane == 1) & (at >= 2))
        def _():
            ahead = CACHE + ((((yh + (1 - t) * g) % 2) * 4 + x) * 2 + (c + t * g) % 2) * 128 - base
            key = lax.broadcasted_iota(jnp.int32, (768, 128), 0)
            row = lax.broadcasted_iota(jnp.int32, (768, 128), 1)
            b["kx"][block, from_core, :, 128:256] = jnp.where(key - row <= ahead, 0.0, HIDDEN).astype(BF)

    scores, tops = (b["score0"], b["score1"]), (b["top0"], b["top1"])

    def overlapped(n, u, weigh_n, weigh=True):
        one, _, block, _, _, from_core = tile_at(n)
        queries = qa[one, u]
        top = jnp.full((8, 512), HIDDEN, F32)
        if weigh:
            w_one, _, w_block, _, _, w_core = tile_at(weigh_n)
            w_g = 1 - u
            old = m[w_one, w_g]
            peak = jnp.max(tops[1 - u][...], axis=0, keepdims=True)
            new = jnp.maximum(old, jnp.broadcast_to(peak, (8, 512)))
            total = (acc[w_one, w_g].reshape(18, 8, 512) * jnp.exp2((old - new) * SCALE)[None]).reshape(144, 512)
        for j in range(3):
            keys = slice(j * 256, (j + 1) * 256)
            fresh = dot(b["kx"][block, from_core, keys, :], queries)
            scores[u][keys, :] = fresh
            top = jnp.maximum(top, jnp.max(fresh.reshape(32, 8, 512), axis=0))
            if weigh:
                held = scores[1 - u][keys, :].reshape(32, 8, 512)
                weights = jnp.exp2((held - new[None]) * SCALE).reshape(256, 512).astype(BF)
                total = total + dot(b["vt"][w_block, w_core, :, keys], weights)
        tops[u][...] = top
        if weigh:
            m[w_one, w_g] = new
            acc[w_one, w_g] = total

    def attention(hooks):
        build(0, 0)
        overlapped(0, 0, 0, weigh=False)

        def step(n, carry):
            for at_step, hook in hooks.items():
                pl.when(n == at_step)(hook)
            build(n, 1)
            overlapped(n, 1, n)
            after = (n + 1) % 24
            build(after, 0)
            overlapped(after, 0, n)
            return carry

        lax.fori_loop(0, 24, step, 0)

    def part_of(one, g):
        total = acc[one, g, 128:136, :]
        mean = (acc[one, g, 0:128, :].reshape(16, 8, 512) * (1.0 / total)[None]).reshape(128, 512)
        return mean, m[one, g] * SCALE + jnp.log(total) * LOG2E

    def partner_part():
        for g in (1, 0):
            mean, logs = part_of(0, g)
            b["o_out"][g] = mean.astype(BF)
            b["l_out"][g] = logs
            give_o[1 - g].start()
            give_l[1 - g].start()

    def keep_context(one, plane, both, ctx):
        both = both.T.astype(BF)
        count, first = tokens[one], 64 * (one // 2)
        for h in range(heads[one]):
            held = both[h * count : (h + 1) * count, :]
            ctx[plane * 4 + x, c, first : first + count, h * 128 : (h + 1) * 128] = held

    def joined(one, g, o_in, l_in):
        mine, log_mine = part_of(one, g)
        share = 1.0 / (1.0 + jnp.exp2(log_mine - l_in[...]))
        other = o_in[...].astype(F32)
        return mine + ((other - mine).reshape(16, 8, 512) * share[None]).reshape(128, 512)

    def s_context(g):
        give_o[g].wait_recv()
        give_l[g].wait_recv()
        keep_context(0, (yh + g) % 2, joined(0, g, b["o_in"].at[g], b["l_in"].at[g]), b["sctx"])
        g_s.root(g)

    def t_part(half):
        mean, logs = part_of(1 + half, 1)
        b["to_out"][half] = mean.astype(BF)
        b["tl_out"][half] = logs
        give_to[half].start()
        give_tl[half].start()

    def t_context(half):
        give_to[half].wait_recv()
        give_tl[half].wait_recv()
        keep_context(1 + half, yh, joined(1 + half, 0, b["to_in"].at[half], b["tl_in"].at[half]), b["tctx"])
        g_t[half].root(0)

    class Reduce:
        def __init__(self, ctx, w, name, half):
            self.ctx, self.w, self.half = ctx, w, half

            def of(key):
                return b[name + key] if half is None else b[name + key].at[half]

            self.y_out, self.y_in, self.part, self.hid = of("y_out"), of("y_in"), of("part"), of("hid")
            self.r_out, self.r_in, self.z_out, self.z_in = of("r_out"), of("r_in"), of("z_out"), of("z_in")
            self.rows = self.part.shape[2] // 2
            near = (tp_dev(0, 3), tp_dev(0, 1))
            self.relay = [
                wire.copy(self.r_out.at[:, pl.ds(i * self.rows, self.rows)], self.r_in.at[i], near[i]) for i in range(2)
            ]
            self.along = [wire.copy(self.z_out.at[i], self.z_in.at[i], near[i]) for i in range(2)]
            self.beside = wire.copy(self.y_out, self.y_in, tp_dev(1, 0))

        def multiply(self, first, last, waits):
            def pair(j, carry):
                for at, wait in waits.items():
                    pl.when(j == at)(wait)
                zd = ((yh + j // 2) % 2) * 2 + (x // 2 + j % 2) % 2

                both = pl.ds(zd * 2, 2)
                if self.half is None:
                    held = self.ctx[both]
                else:
                    held = self.ctx[both, :, self.half * 64 : self.half * 64 + 64]
                done = dot(held.reshape(-1, held.shape[3]), self.w[...])
                self.part[zd] = done.reshape(2, -1, done.shape[1])

                @pl.when(zd == (z + 2) % 4)
                def _():
                    self.r_out[...] = self.part[zd].astype(BF)
                    self.relay[0].start()
                    self.relay[1].start()

                return carry

            lax.fori_loop(first, last, pair, 0)

        def send_on(self):
            for i, zd in enumerate(((z + 3) % 4, (z + 1) % 4)):
                mid = slice(i * self.rows, (i + 1) * self.rows)
                rest = slice((1 - i) * self.rows, (2 - i) * self.rows)
                self.z_out[i, :, rest, :] = self.part[zd, :, rest, :].astype(BF)
                self.relay[i].wait_recv()
                self.z_out[i, :, mid, :] = (self.part[zd, :, mid, :] + self.r_in[i].astype(F32)).astype(BF)
                self.along[i].start()

        def settle(self):
            self.along[0].wait_recv()
            self.along[1].wait_recv()

            def block(u):
                return self.part[z, u] + self.z_in[0, u].astype(F32) + self.z_in[1, u].astype(F32)

            self.y_out[...] = block(1 - yl).astype(BF)
            self.beside.start()
            self.hid[...] = block(yl)

        def finish(self, resid):
            if self.half is None:
                own = resid[...]
            else:
                first = self.half * 64
                own = jnp.concatenate([resid[first : first + 64, :], resid[first + 128 : first + 192, :]], axis=0)
            total = self.hid[...] + own.astype(F32)
            self.beside.wait_recv()
            self.hid[...] = total + self.y_in[...].astype(F32)

    def send_squares(hid, squares):
        chip, sq, between, spread = squares
        value = hid[...]
        ones = jnp.ones((8, value.shape[1]), F32)
        chip[c] = dot(ones, value * value, ((1,), (1,)), lax.Precision.HIGHEST)
        between.start()
        between.wait_recv()
        sq[k_own] = chip[0] + chip[1]
        for made in spread:
            made.start()

    def inverse_scale(squares, width):
        _, sq, _, spread = squares
        for made in spread:
            made.wait_recv()
        total = sq[0]
        for i in range(1, 8):
            total = total + sq[i]
        first = jnp.where(lax.broadcasted_iota(jnp.int32, (8, 128), 0) == 0, 1.0, 0.0)
        column = dot(total, first, ((0,), (0,)), lax.Precision.HIGHEST)
        return 1.0 / jnp.sqrt(column * (1.0 / width) + 1e-05)

    r_s = Reduce(b["sctx"], b["sw"], "s", None)
    r_t = [Reduce(b["tctx"], b["tw"], "t", half) for half in range(2)]

    def ready(gather, plane):
        gather.have_own(plane)
        gather.have_near(plane)
        gather.have_far(plane)

    fill_queries(0, sq, 0)
    prepare(0, 4, (0,))
    loads[0].wait()
    loads[1].wait()
    pl.semaphore_wait(barrier, 22)
    g_skv.root(0)
    give_sq.start()
    give_tq.start()
    g_tkv.cross.start()

    def s_partner():
        g_skv.have_own(0)
        give_sq.wait_recv()
        fill_queries(0, b["sq_in"], 1)

    def s_near():
        prepare(4, 12, (1, 2))
        fill_queries(1, tq, 0)
        fill_queries(2, tq, 0)
        give_tq.wait_recv()
        fill_queries(1, b["tq_in"], 1)
        fill_queries(2, b["tq_in"], 1)
        g_skv.mid(0)
        g_tkv.root(0, False)

    def t_start():
        g_tkv.mid(0)
        g_tkv.root(1)
        partner_part()

    def s_sums():
        for load in loads[2:]:
            load.wait()
        r_s.multiply(0, 4, {0: lambda: ready(g_s, 0), 2: lambda: ready(g_s, 1)})

    def s_squares():
        r_s.finish(sres)
        send_squares(b["shid"], s_sq)

    def s_normed():
        inverse = inverse_scale(s_sq, D_S)
        inverse = jnp.concatenate([inverse, inverse], axis=1)
        normed = (b["shid"][...] * inverse * sg[...]).astype(BF)
        for at, first in enumerate((0, 128, 64, 192)):
            b["nb"][s, at * 64 : (at + 1) * 64, :] = normed[first : first + 64, :]
        g_n.root(0)

    def t1_sums():
        r_t[0].multiply(0, 4, {0: lambda: ready(g_t[0], 0), 2: lambda: ready(g_t[0], 1)})

    def both(*hooks):
        def run():
            for hook in hooks:
                hook()

        return run

    attention(
        {
            0: s_partner,
            1: s_near,
            2: lambda: g_skv.have_left(0),
            4: lambda: g_skv.have_right(0),
            5: lambda: g_skv.far(0),
            6: lambda: g_skv.have_far(0),
            8: t_start,
            10: lambda: g_tkv.far(0),
            12: lambda: s_context(0),
            16: lambda: g_tkv.mid(1),
            17: lambda: s_context(1),
            18: lambda: g_s.mid(0),
            20: both(lambda: g_s.mid(1), lambda: g_s.far(0)),
            21: lambda: g_tkv.far(1),
            22: lambda: g_s.far(1),
            23: lambda: t_part(0),
        }
    )
    for load in map_loads:
        load.start()
    t_part(1)
    t_context(0)
    t_context(1)
    s_sums()
    r_s.send_on()
    g_t[0].mid(0)
    g_t[0].root(1)
    g_t[1].mid(0)
    g_t[1].root(1)
    wire.close(0, keys_sent)
    g_t[0].far(0)
    g_t[0].mid(1)
    r_s.settle()
    g_t[0].far(1)
    t1_sums()
    g_t[1].far(0)
    g_t[1].mid(1)
    s_squares()
    g_t[1].far(1)
    r_t[0].send_on()
    r_t[1].multiply(0, 4, {0: lambda: ready(g_t[1], 0), 2: lambda: ready(g_t[1], 1)})
    s_normed()
    r_t[1].send_on()
    r_t[0].settle()
    g_n.mid(0)
    g_n.root(1)
    r_t[0].finish(tres)
    send_squares(b["thid"].at[0], t_sq[0])
    g_n.far(0)
    g_n.mid(1)
    r_t[1].settle()
    g_n.far(1)
    for made in n_tp:
        made.start()
    r_t[1].finish(tres)
    send_squares(b["thid"].at[1], t_sq[1])
    wire.close(keys_sent, contexts_sent)
    ready(g_n, 0)
    ready(g_n, 1)
    b["diff"][...] = jnp.zeros((2, 128, 512), F32)
    for load in map_loads:
        load.wait()

    def match(k, carry):
        lhs = jnp.concatenate([b["nb"][2 * k], b["nb"][2 * k + 1]], axis=1)
        for u in range(2):
            b["diff"][:, :, u * 256 : (u + 1) * 256] += dot(lhs, b["kx"][k, u, 0:512, :]).reshape(2, 128, 256)
        return carry

    lax.fori_loop(0, 8, match, 0)

    def delta(half):
        inverse = inverse_scale(t_sq[half], D_T)
        inverse = jnp.concatenate([inverse, inverse, inverse, inverse], axis=1)
        target = b["thid"][half] * inverse * tg[...]
        b["dl"][half, p] = ((b["diff"][half] - target) * (1.0 / math.sqrt(SLAB))).astype(BF)
        g_d[half].root(0)

    def gradient(half, plane, offs):
        def one(i, carry):
            q = ((z + offs[0] + i * offs[1]) % 4) * 2 + (yl + plane) % 2
            for at in range(2):
                rows = slice(at * 256, (at + 1) * 256)
                lhs = b["ng"][q, at, half * 128 : (half + 1) * 128, :]
                out[rows, :] += dot(lhs, b["dl"][half, q], ((0,), (0,)))
            return carry

        lax.fori_loop(0, offs[2], one, 0)

    own, near, far = (0, 1, 1), (1, 2, 2), (2, 1, 1)
    delta(0)
    delta(1)
    b["ng"][p, c] = b["nb"][2 * p + c]
    out[...] = jnp.zeros((512, 512), F32)
    g_d[0].mid(0)
    g_d[0].root(1)
    for made in n_tp:
        made.wait_recv()
    n_core.start()
    g_d[0].far(0)
    g_d[0].mid(1)
    n_core.wait_recv()
    gradient(0, 0, own)
    gradient(0, 0, near)
    gradient(0, 0, far)
    gradient(0, 1, own)
    g_d[1].mid(0)
    g_d[1].root(1)
    gradient(0, 1, near)
    g_d[0].far(1)
    gradient(0, 1, far)
    gradient(1, 0, own)
    gradient(1, 0, near)
    gradient(1, 1, own)
    g_d[1].far(0)
    g_d[1].mid(1)
    gradient(1, 0, far)
    gradient(1, 1, near)
    g_d[1].far(1)
    gradient(1, 1, far)
    wire.close()


def per_device(tq, tkv, sq, skv, doc, tres, tw, tg, sres, sw, sg, mp):
    V = pl.BlockSpec(memory_space=pltpu.VMEM)
    A = pl.BlockSpec(memory_space=pl.ANY)
    S = pl.BlockSpec(memory_space=pltpu.SMEM)
    return pl.pallas_call(
        kernel,
        out_shape=jax.ShapeDtypeStruct((512, 512), F32),
        in_specs=[S, V, A, V, A, V, A, V, V, A, V, A],
        out_specs=V,
        scratch_shapes=list(scratch_plan().values()),
        compiler_params=pltpu.CompilerParams(
            collective_id=0, has_side_effects=True, vmem_limit_bytes=63 * 1024 * 1024
        ),
    )(
        doc, tq, tkv, sq, skv, tres, tw, tg.reshape(1, -1), sres, sw, sg.reshape(1, -1), mp.reshape(8, 512, 512)
    )


def solution(mesh):
    in_specs = (
        P("seq", "tp"),
        P(None, "seq", "tp"),
        P("seq", "tp"),
        P(None, "seq", "tp"),
        P(),
        P("tp", "seq"),
        P("tp", "seq"),
        P("seq"),
        P("tp", "seq"),
        P("tp", "seq"),
        P("seq"),
        P(None, "seq"),
    )
    out_specs = P("tp", "seq")
    return jax.shard_map(per_device, mesh=mesh, in_specs=in_specs, out_specs=out_specs, check_vma=False)
```
